32 devices in a mesh: seq: 8 (over y, x, core), rows: 4 (over z).
Axes of the slice: x: 2, y: 2, z: 4, core: 2. Of those that a mesh axis runs over, the one named last changes fastest.
Arguments:
- tokens: bfloat16 [8, 2048, 2048], P('rows', 'seq'), may hold values from -6 to 6
- lengths: int32 [8], P('rows'), may hold values from 64 to 2048, as said below
- norm_gains: bfloat16 [2, 2048], P(None, ('seq', 'rows')), may hold values from 0.099609375 to 1.8984375
- qk_gains: bfloat16 [2, 64], replicated, may hold values from 0.099609375 to 1.8984375
- qkv_weight: bfloat16 [2048, 3072], P(('seq', 'rows')), may hold values from -0.125 to 0.125
- out_weight: bfloat16 [2048, 2048], P(('seq', 'rows')), may hold values from -0.5 to 0.5
- gate_up_weight: bfloat16 [2048, 16384], P(('seq', 'rows')), may hold values from -0.125 to 0.125
- down_weight: bfloat16 [2048, 8192], P(('seq', 'rows')), may hold values from -0.09375 to 0.09375
- cotangent: bfloat16 [8, 2048, 2048], P('rows', 'seq'), may hold values from -6 to 6
Outputs:
- output: bfloat16 [8, 2048, 2048], P('rows', 'seq')
- input_grad: bfloat16 [8, 2048, 2048], P('rows', 'seq')
- norm_gains_grad: float32 [2, 2048], P(None, ('seq', 'rows'))
- qk_gains_grad: float32 [2, 64], replicated
- qkv_grad: float32 [2048, 3072], P(('seq', 'rows'))
- out_grad: float32 [2048, 2048], P(('seq', 'rows'))
- gate_up_grad: float32 [2048, 16384], P(('seq', 'rows'))
- down_grad: float32 [2048, 8192], P(('seq', 'rows'))
The draws below stay inside these ranges and needn't reach their ends.
Inputs may be any that keep to these rules, and one draw needn't show every extreme that they name: `lengths`: in each aligned block of 2 rows (the rows of one device) one row has length 2048; some row has length 64.
All inputs are finite; a program needn't handle non-finite values.
Results may differ from the reference program's by a relative error of at most 0.025.
Values may be sent and summed in bfloat16 or wider, within the bound.
A program may use at most 768 MiB of HBM per device.

```python
import math
import jax
import jax.numpy as jnp
from jax import lax

D = 2048
QUERY_HEADS = 32
KEY_VALUE_HEADS = 8
HEAD_SIZE = 64
FF = 8192
SLOTS = 2048
MIN_LEN = 64
ROWS_DEV = 2
ROWS = 8
QKV = 3072


def draw_lengths(key, part):
    key = jax.random.fold_in(key, 11)
    keys = jax.random.split(key, 4)
    first = jax.random.randint(keys[0], (ROWS,), MIN_LEN, SLOTS + 1)
    second = jax.random.randint(keys[1], (ROWS,), MIN_LEN, SLOTS + 1)
    third = jax.random.randint(keys[2], (ROWS,), MIN_LEN, SLOTS + 1)
    ragged = jnp.minimum(jnp.minimum(first, second), third)
    picks = jax.random.randint(keys[3], (ROWS // ROWS_DEV,), 0, ROWS_DEV)
    row_places = jnp.arange(ROWS)
    owner = jnp.repeat(picks, ROWS_DEV)
    full_rows = row_places % ROWS_DEV == owner
    shortest = row_places == (picks[0] + 1) % ROWS_DEV
    return jnp.where(full_rows, SLOTS, jnp.where(shortest, MIN_LEN, ragged)).astype(jnp.int32)


def level_of(stream_key, extent, pieces, least, largest):
    loudness = 1.0
    for dim, parts in pieces:
        draws = jax.random.uniform(jax.random.fold_in(jax.random.fold_in(stream_key, 6), dim), (parts,), jnp.float32, least / len(pieces), largest / len(pieces))
        loudness = loudness * jnp.repeat(jnp.exp(draws), extent[dim] // parts).reshape((-1,) + (1,) * (len(extent) - 1 - dim))
    return loudness


def normal_values(rng, dims, scale, reach, pieces=(), dtype=jnp.bfloat16):
    values = jax.random.normal(rng, dims, jnp.float32) * scale
    if len(pieces) > 0:
        values = level_of(rng, dims, pieces, -0.22, 0.18) * values
    return jnp.clip(values, min=-reach, max=reach).astype(dtype)


def setup_inputs(seed: int = 0) -> dict:
    splits = jax.random.split(jax.random.key(seed), 10)
    return {
        "tokens": normal_values(splits[0], (ROWS, SLOTS, D), 1.0, 6.0, ((0, 4), (1, 8))),
        "lengths": draw_lengths(jax.random.fold_in(splits[9], 71), 0),
        "norm_gains": jnp.clip(1.0 + 0.18 * jax.random.normal(splits[2], (2, D), jnp.float32), 0.099609375, 1.8984375).astype(jnp.bfloat16),
        "qk_gains": jnp.clip(1.0 + 0.18 * jax.random.normal(splits[3], (2, HEAD_SIZE), jnp.float32), 0.099609375, 1.8984375).astype(jnp.bfloat16),
        "qkv_weight": normal_values(splits[4], (D, QKV), D ** -0.5, 0.125, ((0, 32),)),
        "out_weight": normal_values(splits[5], (D, QUERY_HEADS * HEAD_SIZE), (QUERY_HEADS * HEAD_SIZE // 16) ** -0.5, 0.5, ((0, 32),)),
        "gate_up_weight": normal_values(splits[6], (D, 2 * FF), D ** -0.5, 0.125, ((0, 32),)),
        "down_weight": normal_values(splits[7], (D, FF), (FF // 2) ** -0.5, 0.09375, ((0, 32),)),
        "cotangent": normal_values(splits[8], (ROWS, SLOTS, D), 1.0, 6.0, ((0, 4), (1, 8))),
    }


EPSILON = 1e-06
HIGHEST = lax.Precision.HIGHEST

@jax.custom_vjp
def low(v):
    return lax.optimization_barrier(v.astype(jnp.bfloat16)).astype(jnp.float32)

@jax.custom_vjp
def low_back(v):
    return v

def low_keep(v):
    return (low(v), None)

def low_pass(kept, grad):
    return (grad,)

def back_keep(v):
    return (v, None)

def back_low(kept, grad):
    return (low(grad),)
low.defvjp(low_keep, low_pass)
low_back.defvjp(back_keep, back_low)

def rms_norm(values, gain_vector):
    factor = lax.rsqrt(lax.optimization_barrier(jnp.mean(values * values, axis=-1, keepdims=True)) + EPSILON)
    return values * factor * gain_vector

def rotary(values, positions):
    half_width = values.shape[-1] // 2
    exponent = jnp.arange(half_width).astype(jnp.float32) * (2.0 / values.shape[-1])
    frequency = jnp.exp(-math.log(10000.0) * exponent)
    angles = positions.astype(jnp.float32)[:, None] * frequency[None, :]
    cosine = jnp.cos(angles)[:, None, :]
    sine_part = jnp.sin(angles)[:, None, :]
    first_half = values[..., :half_width]
    second_half = values[..., half_width:]
    return jnp.concatenate([first_half * cosine - second_half * sine_part, second_half * cosine + first_half * sine_part], axis=-1)

def swiglu(gate_up):
    half_width = gate_up.shape[-1] // 2
    return jax.nn.silu(gate_up[..., :half_width]) * gate_up[..., half_width:]

def attention(query_rows_all, key_row_block, value_row_block, length):
    count_of_slots = query_rows_all.shape[0]
    query_group_width = QUERY_HEADS // KEY_VALUE_HEADS
    block_rows = min(512, count_of_slots)
    grouped_queries = query_rows_all.reshape(count_of_slots, KEY_VALUE_HEADS, query_group_width, HEAD_SIZE)
    key_places = jnp.arange(count_of_slots).astype(jnp.int32)

    def one_block(block_start):
        query_block = lax.dynamic_slice_in_dim(grouped_queries, block_start, block_rows, 0)
        scores = jnp.einsum('qhgd,khd->hgqk', query_block, key_row_block, precision=HIGHEST) * HEAD_SIZE ** (-0.5)
        scores = low_back(scores)
        query_places = block_start + jnp.arange(block_rows).astype(jnp.int32)
        allowed = (key_places[None, :] <= query_places[:, None]) & (key_places[None, :] < length)
        scores = jnp.where(allowed, scores, -1e+30)
        highest = lax.optimization_barrier(jnp.max(scores, axis=-1, keepdims=True))
        weights = jnp.exp(scores - highest)
        probability = low(weights / lax.optimization_barrier(jnp.sum(weights, axis=-1, keepdims=True)))
        mixture = jnp.einsum('hgqk,khd->qhgd', probability, value_row_block, precision=HIGHEST)
        return mixture.reshape(block_rows, QUERY_HEADS * HEAD_SIZE)
    starts = (jnp.arange(count_of_slots // block_rows) * block_rows).astype(jnp.int32)
    blocks = lax.map(jax.checkpoint(one_block), starts)
    return blocks.reshape(count_of_slots, QUERY_HEADS * HEAD_SIZE)

def row_forward(row_input, row_length, norm_gains, qk_gains, qkv_weight, out_weight, gate_up_weight, down_weight):
    count_of_slots = row_input.shape[0]
    normed = low(rms_norm(row_input, norm_gains[0]))
    query_key_value_unnormed = low_back(jnp.dot(normed, qkv_weight, precision=HIGHEST))
    query_rows_all = query_key_value_unnormed[:, :QUERY_HEADS * HEAD_SIZE].reshape(count_of_slots, QUERY_HEADS, HEAD_SIZE)
    key_row_block = query_key_value_unnormed[:, QUERY_HEADS * HEAD_SIZE:(QUERY_HEADS + KEY_VALUE_HEADS) * HEAD_SIZE].reshape(count_of_slots, KEY_VALUE_HEADS, HEAD_SIZE)
    value_row_block = query_key_value_unnormed[:, (QUERY_HEADS + KEY_VALUE_HEADS) * HEAD_SIZE:].reshape(count_of_slots, KEY_VALUE_HEADS, HEAD_SIZE)
    positions = jnp.arange(count_of_slots).astype(jnp.int32)
    query_rows_all = low(rotary(rms_norm(query_rows_all, qk_gains[0]), positions))
    key_row_block = low(rotary(rms_norm(key_row_block, qk_gains[1]), positions))
    value_row_block = low(value_row_block)
    attended = low(low_back(attention(query_rows_all, key_row_block, value_row_block, row_length)))
    branch = low_back(jnp.dot(attended, out_weight.T, precision=HIGHEST))
    middle = row_input + branch
    hidden = low(rms_norm(middle, norm_gains[1]))
    gate_up = low_back(jnp.dot(hidden, gate_up_weight, precision=HIGHEST))
    activated = low(swiglu(gate_up))
    return middle + low_back(jnp.dot(activated, down_weight.T, precision=HIGHEST))

def reference(tokens, lengths, norm_gains, qk_gains, qkv_weight, out_weight, gate_up_weight, down_weight, cotangent):
    params_all = tuple((item.astype(jnp.float32) for item in (norm_gains, qk_gains, qkv_weight, out_weight, gate_up_weight, down_weight)))

    def one_row(totals, inputs):
        row_tokens, row_length, row_cotangent = inputs

        def forward(row_input, *params):
            return row_forward(row_input, row_length, *params)
        result, pullback = jax.vjp(forward, row_tokens.astype(jnp.float32), *params_all)
        row_grads = pullback(row_cotangent.astype(jnp.float32))
        totals = tuple((first + second for first, second in zip(totals, row_grads[1:])))
        return (totals, (result.astype(jnp.bfloat16), row_grads[0].astype(jnp.bfloat16)))
    initial = tuple((jnp.zeros(item.shape, jnp.float32) for item in params_all))
    totals, (output, input_grad) = lax.scan(one_row, initial, (tokens, lengths, cotangent))
    return (output, input_grad, totals[0], totals[1], totals[2], totals[3], totals[4], totals[5])
```

```python
from functools import partial
import math

import jax
import jax.numpy as jnp
from jax import lax
from jax.experimental import pallas as pl
from jax.experimental.pallas import tpu as pltpu
from jax.sharding import PartitionSpec as P

QUERY_HEADS = 32
KEY_VALUE_HEADS = 8
HEAD = 64
EPSILON = 1e-06
F32 = jnp.float32
BF16 = jnp.bfloat16
HIGHEST = lax.Precision.HIGHEST
SCALE = HEAD ** (-0.5)
SCALE2 = SCALE * math.log2(math.e)
VMEM = 56 * 1024 * 1024


def swap(block, mask):
    return lax.ppermute(block, "seq", [(i, i ^ mask) for i in range(lax.axis_size("seq"))])


def masks_between_chips():
    return [1 << bit for bit in range(1, lax.axis_size("seq").bit_length() - 1)]


def natural(place, me, seq):
    return me[0] ^ (2 * lax.rem(place, seq // 2) + lax.div(place, seq // 2))


def dot_nn(a, b):
    return jnp.dot(a, b, preferred_element_type=F32)


def dot_nt(a, b, precision=None):
    return lax.dot_general(
        a, b, (((1,), (1,)), ((), ())), preferred_element_type=F32, precision=precision
    )


def dot_tn(a, b):
    return lax.dot_general(a, b, (((0,), (0,)), ((), ())), preferred_element_type=F32)


def gather_plane(chunk):
    half = chunk.shape[0] // 2
    masks = masks_between_chips()
    own = [chunk]
    if len(masks) == 2:
        along_x = swap(chunk, 2)
        along_y = swap(chunk, 4)
        diagonal = jnp.concatenate([swap(along_y[:half], 2), swap(along_x[half:], 4)], axis=0)
        own = [chunk, along_x, along_y, diagonal]
    else:
        for mask in masks:
            own = own + [swap(part, mask) for part in own]
    return jnp.concatenate(own + [swap(part, 1) for part in own], axis=0)


def scatter_plane(odd, even):
    masks = masks_between_chips()
    size = even.shape[0] >> len(masks)
    half = size // 2
    both = even + swap(odd, 1).astype(F32)
    parts = [both[i * size : (i + 1) * size] for i in range(1 << len(masks))]
    if len(masks) == 2:
        mine, to_x, to_y, diagonal = parts
        diagonal = diagonal.astype(BF16)
        from_x = swap(diagonal[:half], 2).astype(F32)
        from_y = swap(diagonal[half:], 4).astype(F32)
        to_x = jnp.concatenate([to_x[:half], to_x[half:] + from_y], axis=0).astype(BF16)
        to_y = jnp.concatenate([to_y[:half] + from_x, to_y[half:]], axis=0).astype(BF16)
        return mine + swap(to_x, 2).astype(F32) + swap(to_y, 4).astype(F32)
    for mask in reversed(masks):
        kept = len(parts) // 2
        parts = [
            parts[i] + swap(parts[kept + i].astype(BF16), mask).astype(F32) for i in range(kept)
        ]
    return parts[0]


def lane_of(shape):
    return lax.broadcasted_iota(jnp.int32, shape, len(shape) - 1)


def swap_halves(v):
    first = lane_of(v.shape) % HEAD < HEAD // 2
    return jnp.where(first, pltpu.roll(v, 96, 1), pltpu.roll(v, 32, 1))


def head_mean(v):
    rows = lax.broadcasted_iota(jnp.int32, (128, 128), 0) // HEAD
    cols = lax.broadcasted_iota(jnp.int32, (128, 128), 1) // HEAD
    block = jnp.where(rows == cols, 1.0 / HEAD, 0.0).astype(F32)
    return jnp.dot(v, block, preferred_element_type=F32, precision=HIGHEST)


def qkv_kernel(me, x_ref, w_ref, cos_ref, sin_ref, gain_ref, raw_ref, q_ref, kv_ref):
    rows, slots = q_ref.shape[0], q_ref.shape[1]
    raw = dot_nn(x_ref[...], w_ref[...])
    cos, sin = cos_ref[...], sin_ref[...]
    keys = lane_of((slots, 128)) < HEAD
    for r in range(rows):
        part = raw[r * slots : (r + 1) * slots]
        raw_ref[r] = part
        last = part.shape[1] // 128 - 1
        for s in range(last + 1):
            v = part[:, s * 128 : (s + 1) * 128]
            factor = lax.rsqrt(head_mean(v * v) + EPSILON)
            n = v * factor * gain_ref[:, s * 128 : (s + 1) * 128]
            out = n * cos + swap_halves(n) * sin
            if s < last:
                q_ref[r, :, s * 128 : (s + 1) * 128] = out.astype(BF16)
            else:
                kv_ref[r] = jnp.where(keys, out, v).astype(BF16)


def qkv_call(me, x, w, cos, sin, gains, rows, slots):
    chunk = rows * slots
    width = w.shape[1]
    query_width = width - 128
    seq = x.shape[0] // chunk
    total = seq * slots
    return pl.pallas_call(
        qkv_kernel,
        grid_spec=pltpu.PrefetchScalarGridSpec(
            num_scalar_prefetch=1,
            grid=(seq,),
            in_specs=[
                pl.BlockSpec((chunk, x.shape[1]), lambda i, me: (i, 0)),
                pl.BlockSpec(w.shape, lambda i, me: (0, 0)),
                pl.BlockSpec((slots, 128), lambda i, me: (natural(i, me, seq), 0)),
                pl.BlockSpec((slots, 128), lambda i, me: (natural(i, me, seq), 0)),
                pl.BlockSpec((1, width), lambda i, me: (0, 0)),
            ],
            out_specs=[
                pl.BlockSpec((rows, slots, width), lambda i, me: (0, natural(i, me, seq), 0)),
                pl.BlockSpec((rows, slots, query_width), lambda i, me: (0, natural(i, me, seq), 0)),
                pl.BlockSpec((rows, slots, 128), lambda i, me: (0, natural(i, me, seq), 0)),
            ],
        ),
        out_shape=[
            jax.ShapeDtypeStruct((rows, total, width), F32),
            jax.ShapeDtypeStruct((rows, total, query_width), BF16),
            jax.ShapeDtypeStruct((rows, total, 128), BF16),
        ],
        compiler_params=pltpu.CompilerParams(vmem_limit_bytes=VMEM),
        name="qkv_prepare",
    )(me, x, w, cos, sin, gains)


def attend_kernel(lengths, q_ref, kv_ref, out_ref, low_ref, log_ref, k2, vo, acc):
    row, step = pl.program_id(0), pl.program_id(1)
    block = q_ref.shape[1]
    group = q_ref.shape[2] // HEAD
    length = lengths[row]

    @pl.when(step == 0)
    def _():
        kv = kv_ref[0].astype(F32)
        keys = lane_of(kv.shape) < HEAD
        k2[...] = jnp.where(keys, kv, pltpu.roll(kv, HEAD, 1)).astype(BF16)
        vo[...] = jnp.where(keys, 1.0, kv).astype(BF16)

    low_half = lane_of((block, 128)) < HEAD
    queries = []
    for h in range(group):
        part = q_ref[0, :, (h // 2) * 128 : (h // 2 + 1) * 128].astype(F32)
        kept = low_half if h % 2 == 0 else jnp.logical_not(low_half)
        queries.append(jnp.where(kept, part, 0.0).astype(BF16))
    acc[...] = jnp.zeros_like(acc)

    def one_block(at, masked):
        begin = pl.multiple_of(at * block, block)
        keys = k2[pl.ds(begin, block), :]
        values = vo[pl.ds(begin, block), :]
        if masked:
            key_place = begin + lax.broadcasted_iota(jnp.int32, (block, block), 1)
            query_place = step * block + lax.broadcasted_iota(jnp.int32, (block, block), 0)
            allowed = (key_place <= query_place) & (key_place < length)
        for h in range(group):
            weights = jnp.exp2(dot_nt(queries[h], keys) * SCALE2)
            if masked:
                weights = jnp.where(allowed, weights, 0.0)
            acc[h] += dot_nn(weights.astype(BF16), values)

    full = jnp.minimum(step, lax.div(length, block))

    def body(at, carry):
        one_block(at, False)
        return carry

    lax.fori_loop(0, full, body, 0)

    @pl.when(full * block < length)
    def _():
        one_block(full, True)

    for g in range(group // 2):
        even, odd = acc[2 * g], acc[2 * g + 1]
        even_turned, odd_turned = pltpu.roll(even, HEAD, 1), pltpu.roll(odd, HEAD, 1)
        mixed = jnp.where(low_half, even_turned / even, odd / odd_turned)
        out_ref[0, :, g * 128 : (g + 1) * 128] = mixed
        low_ref[0, 0, :, g * 128 : (g + 1) * 128] = mixed.astype(BF16)
        log_ref[0, 2 * g : 2 * g + 1, :] = jnp.log2(even.T[0:1, :])
        log_ref[0, 2 * g + 1 : 2 * g + 2, :] = jnp.log2(odd.T[0:1, :])
    log_ref[0, group:, :] = jnp.zeros((8 - group, block), F32)


def attend_call(lengths, q, kv, block):
    rows, total, width = q.shape
    seq = total // block
    return pl.pallas_call(
        attend_kernel,
        grid_spec=pltpu.PrefetchScalarGridSpec(
            num_scalar_prefetch=1,
            grid=(rows, seq),
            in_specs=[
                pl.BlockSpec((1, block, width), lambda r, i, n: (r, i, 0)),
                pl.BlockSpec((1, total, 128), lambda r, i, n: (r, 0, 0)),
            ],
            out_specs=[
                pl.BlockSpec((1, block, width), lambda r, i, n: (r, i, 0)),
                pl.BlockSpec((1, 1, block, width), lambda r, i, n: (i, r, 0, 0)),
                pl.BlockSpec((1, 8, block), lambda r, i, n: (r, 0, i)),
            ],
            scratch_shapes=[
                pltpu.VMEM((total, 128), BF16),
                pltpu.VMEM((total, 128), BF16),
                pltpu.VMEM((width // HEAD, block, 128), F32),
            ],
        ),
        out_shape=[
            jax.ShapeDtypeStruct((rows, total, width), F32),
            jax.ShapeDtypeStruct((seq, rows, block, width), BF16),
            jax.ShapeDtypeStruct((rows, 8, total), F32),
        ],
        compiler_params=pltpu.CompilerParams(vmem_limit_bytes=VMEM),
        name="attend",
    )(lengths, q, kv)


def attend_back_kernel(
    lengths, q_ref, kv_ref, out_ref, grad_ref, log_ref, dq_ref, dkv_ref, delta, dqt, kacc, vacc
):
    row, step = pl.program_id(0), pl.program_id(1)
    block = kv_ref.shape[1]
    count = q_ref.shape[1] // block
    width = q_ref.shape[2]
    group = width // HEAD
    length = lengths[row]

    @pl.when(step == 0)
    def _():
        dqt[...] = jnp.zeros_like(dqt)
        heads = lax.broadcasted_iota(jnp.int32, (8, width), 0)
        pick = jnp.where(lane_of((8, width)) // HEAD == heads, 1.0, 0.0).astype(F32)
        for i in range(count):
            product = grad_ref[i, 0].astype(F32) * out_ref[0, i * block : (i + 1) * block, :]
            delta[:, i * block : (i + 1) * block] = dot_nt(pick, product, HIGHEST)

    kacc[...] = jnp.zeros_like(kacc)
    vacc[...] = jnp.zeros_like(vacc)
    begin = step * block
    kv = kv_ref[0].astype(F32)
    turned = pltpu.roll(kv, HEAD, 1)
    low_half = lane_of((block, 128)) < HEAD
    keys = [
        jnp.where(low_half, kv, 0.0).astype(BF16),
        jnp.where(low_half, 0.0, turned).astype(BF16),
    ]
    values = [
        jnp.where(low_half, turned, 0.0).astype(BF16),
        jnp.where(low_half, 0.0, kv).astype(BF16),
    ]
    keys_turned = [
        jnp.where(low_half, kv, 0.0).T.astype(BF16),
        jnp.where(low_half, 0.0, turned).T.astype(BF16),
    ]

    def one_block(at, masked):
        first = pl.multiple_of(at * block, block)
        if masked:
            key_place = begin + lax.broadcasted_iota(jnp.int32, (block, block), 0)
            query_place = first + lax.broadcasted_iota(jnp.int32, (block, block), 1)
            allowed = (key_place <= query_place) & (key_place < length)
        for g in range(group // 2):
            queries = q_ref[0, pl.ds(first, block), g * 128 : (g + 1) * 128]
            grads = grad_ref[at, 0, :, g * 128 : (g + 1) * 128]
            turned_sum = None
            for side in range(2):
                h = 2 * g + side
                logs = log_ref[0, h : h + 1, pl.ds(first, block)]
                deltas = delta[h : h + 1, pl.ds(first, block)]
                weights = jnp.exp2(dot_nt(keys[side], queries) * SCALE2 - logs)
                if masked:
                    weights = jnp.where(allowed, weights, 0.0)
                d_weights = dot_nt(values[side], grads)
                d_scores = (weights * (d_weights - deltas)).astype(BF16)
                vacc[side] += dot_nn(weights.astype(BF16), grads)
                kacc[side] += dot_nn(d_scores, queries)
                term = dot_nn(keys_turned[side], d_scores)
                turned_sum = term if turned_sum is None else turned_sum + term
            dqt[g, :, pl.ds(first, block)] += turned_sum

    @pl.when(begin < length)
    def _():
        inside = begin + block <= length

        @pl.when(inside)
        def _():
            one_block(step, True)

            def body(at, carry):
                one_block(at, False)
                return carry

            lax.fori_loop(step + 1, count, body, 0)

        @pl.when(jnp.logical_not(inside))
        def _():
            def body(at, carry):
                one_block(at, True)
                return carry

            lax.fori_loop(step, count, body, 0)

    ksum = jnp.where(low_half, kacc[0], 0.0) + pltpu.roll(jnp.where(low_half, 0.0, kacc[1]), HEAD, 1)
    vsum = pltpu.roll(jnp.where(low_half, vacc[0], 0.0), HEAD, 1) + jnp.where(
        low_half, 0.0, vacc[1]
    )
    dkv_ref[0] = jnp.where(low_half, ksum * SCALE, vsum)

    @pl.when(step == count - 1)
    def _():
        for g in range(group // 2):
            for i in range(count):
                dq_ref[0, i * block : (i + 1) * block, g * 128 : (g + 1) * 128] = (
                    dqt[g, :, i * block : (i + 1) * block].T * SCALE
                )


def attend_back_call(lengths, q, kv, attended, grads, logs):
    rows, total, width = q.shape
    seq, block = grads.shape[0], grads.shape[2]
    return pl.pallas_call(
        attend_back_kernel,
        grid_spec=pltpu.PrefetchScalarGridSpec(
            num_scalar_prefetch=1,
            grid=(rows, seq),
            in_specs=[
                pl.BlockSpec((1, total, width), lambda r, i, n: (r, 0, 0)),
                pl.BlockSpec((1, block, 128), lambda r, i, n: (r, i, 0)),
                pl.BlockSpec((1, total, width), lambda r, i, n: (r, 0, 0)),
                pl.BlockSpec((seq, 1, block, width), lambda r, i, n: (0, r, 0, 0)),
                pl.BlockSpec((1, 8, total), lambda r, i, n: (r, 0, 0)),
            ],
            out_specs=[
                pl.BlockSpec((1, total, width), lambda r, i, n: (r, 0, 0)),
                pl.BlockSpec((1, block, 128), lambda r, i, n: (r, i, 0)),
            ],
            scratch_shapes=[
                pltpu.VMEM((8, total), F32),
                pltpu.VMEM((width // 128, 128, total), F32),
                pltpu.VMEM((2, block, 128), F32),
                pltpu.VMEM((2, block, 128), F32),
            ],
        ),
        out_shape=[
            jax.ShapeDtypeStruct((rows, total, width), F32),
            jax.ShapeDtypeStruct((rows, total, 128), F32),
        ],
        compiler_params=pltpu.CompilerParams(vmem_limit_bytes=VMEM),
        name="attend_back",
    )(lengths, q, kv, attended, grads, logs)


def prepare_back_kernel(
    me, raw_ref, dq_ref, dkv_ref, cos_ref, sin_ref, gain_ref, out_ref, gain_grad_ref
):
    rows, slots = dq_ref.shape[0], dq_ref.shape[1]
    cos, sin = cos_ref[...], sin_ref[...]
    keys = lane_of((slots, 128)) < HEAD
    last = raw_ref.shape[2] // 128 - 1

    @pl.when(pl.program_id(0) == 0)
    def _():
        gain_grad_ref[...] = jnp.zeros_like(gain_grad_ref)

    for r in range(rows):
        for s in range(last + 1):
            lanes = slice(s * 128, (s + 1) * 128)
            raw = raw_ref[r, :, lanes]
            grad = dq_ref[r, :, lanes] if s < last else dkv_ref[r]
            gain = gain_ref[:, lanes]
            turned = grad * cos + swap_halves(grad * sin)
            factor = lax.rsqrt(head_mean(raw * raw) + EPSILON)
            gain_grad_ref[:, lanes] += jnp.sum(turned * raw * factor, axis=0, keepdims=True)
            u = turned * gain
            mean = head_mean(u * raw)
            result = factor * u - raw * (factor * factor * factor) * mean
            if s == last:
                result = jnp.where(keys, result, grad)
            out_ref[r * slots : (r + 1) * slots, lanes] = result.astype(BF16)


def prepare_back_call(me, raw, dq, dkv, cos, sin, gains, slots):
    rows, total, width = raw.shape
    seq = total // slots
    return pl.pallas_call(
        prepare_back_kernel,
        grid_spec=pltpu.PrefetchScalarGridSpec(
            num_scalar_prefetch=1,
            grid=(seq,),
            in_specs=[
                pl.BlockSpec((rows, slots, width), lambda i, me: (0, natural(i, me, seq), 0)),
                pl.BlockSpec((rows, slots, width - 128), lambda i, me: (0, natural(i, me, seq), 0)),
                pl.BlockSpec((rows, slots, 128), lambda i, me: (0, natural(i, me, seq), 0)),
                pl.BlockSpec((slots, 128), lambda i, me: (natural(i, me, seq), 0)),
                pl.BlockSpec((slots, 128), lambda i, me: (natural(i, me, seq), 0)),
                pl.BlockSpec((1, width), lambda i, me: (0, 0)),
            ],
            out_specs=[
                pl.BlockSpec((rows * slots, width), lambda i, me: (i, 0)),
                pl.BlockSpec((1, width), lambda i, me: (0, 0)),
            ],
        ),
        out_shape=[
            jax.ShapeDtypeStruct((rows * total, width), BF16),
            jax.ShapeDtypeStruct((1, width), F32),
        ],
        compiler_params=pltpu.CompilerParams(vmem_limit_bytes=VMEM),
        name="prepare_back",
    )(me, raw, dq, dkv, cos, sin, gains)


def ffn_kernel(hidden_ref, grad_ref, gu_ref, down_ref, act_ref, dgu_ref):
    part = down_ref.shape[1]
    hidden = hidden_ref[...]
    gate = dot_nn(hidden, gu_ref[:, :part])
    up = dot_nn(hidden, gu_ref[:, part:])
    d_act = dot_nn(grad_ref[...], down_ref[...])
    sigmoid = 1.0 / (1.0 + jnp.exp(-gate))
    silu = gate * sigmoid
    act_ref[...] = (silu * up).astype(BF16)
    dgu_ref[:, :part] = (d_act * up * (sigmoid + silu * (1.0 - sigmoid))).astype(BF16)
    dgu_ref[:, part:] = (d_act * silu).astype(BF16)


def ffn_call(hidden, grad, gu, down):
    count, width = hidden.shape
    part = down.shape[1]
    block = 256
    return pl.pallas_call(
        ffn_kernel,
        grid=(count // block,),
        in_specs=[
            pl.BlockSpec((block, width), lambda i: (i, 0)),
            pl.BlockSpec((block, width), lambda i: (i, 0)),
            pl.BlockSpec(gu.shape, lambda i: (0, 0), pipeline_mode=pl.Buffered(1)),
            pl.BlockSpec(down.shape, lambda i: (0, 0), pipeline_mode=pl.Buffered(1)),
        ],
        out_specs=[
            pl.BlockSpec((block, part), lambda i: (i, 0)),
            pl.BlockSpec((block, 2 * part), lambda i: (i, 0)),
        ],
        out_shape=[
            jax.ShapeDtypeStruct((count, part), BF16),
            jax.ShapeDtypeStruct((count, 2 * part), BF16),
        ],
        compiler_params=pltpu.CompilerParams(vmem_limit_bytes=VMEM),
        name="ffn",
    )(hidden, grad, gu, down)


def all_to_all(block):
    return lax.all_to_all(block, "seq", 0, 0, tiled=True)


def gather_z(block):
    full = lax.all_gather(block, "rows", axis=1, tiled=True)
    return full.reshape(-1, full.shape[-1])


def scatter_z(grad):
    grad = grad.reshape(lax.axis_size("seq"), -1, grad.shape[-1])
    return lax.psum_scatter(grad, "rows", scatter_dimension=1, tiled=True)


def shards(
    tokens,
    lengths,
    norm_gains,
    qk_gains,
    qkv_weight,
    out_weight,
    gate_up_weight,
    down_weight,
    cotangent,
):
    rows, slots, width = tokens.shape
    count = rows * slots
    seq = lax.axis_size("seq")
    group = QUERY_HEADS // seq
    query_width = group * HEAD
    sharing = seq // KEY_VALUE_HEADS
    total = seq * slots
    depth = qkv_weight.shape[0]
    kv_at = QUERY_HEADS * HEAD
    part = down_weight.shape[1] // seq
    me = lax.axis_index("seq").astype(jnp.int32)[None]
    gains = norm_gains.astype(F32)

    qkv_scaled = (qkv_weight.astype(F32) * gains[0][:, None]).astype(BF16)
    kv_scaled = qkv_scaled[:, kv_at:].reshape(depth, 2, KEY_VALUE_HEADS, HEAD)
    qkv_blocks = jnp.concatenate(
        [
            qkv_scaled[:, :kv_at].reshape(depth, seq, query_width),
            jnp.repeat(kv_scaled[:, 0], sharing, axis=1),
            jnp.repeat(kv_scaled[:, 1], sharing, axis=1),
        ],
        axis=2,
    ).transpose(1, 0, 2)
    qkv_mine = gather_z(all_to_all(qkv_blocks))
    out_full = lax.all_gather(out_weight, ("seq", "rows"), axis=0, tiled=True)
    gu_scaled = (gate_up_weight.astype(F32) * gains[1][:, None]).astype(BF16)
    gu_blocks = gu_scaled.reshape(depth, 2, seq, part).transpose(2, 0, 1, 3)
    gu_mine = gather_z(all_to_all(gu_blocks.reshape(seq, depth, 2 * part)))
    down_blocks = down_weight.reshape(depth, seq, part).transpose(1, 0, 2)
    down_mine = gather_z(all_to_all(down_blocks))

    lane = jnp.arange(128) % HEAD
    frequency = jnp.exp(
        -math.log(10000.0) * ((lane % (HEAD // 2)).astype(F32) * (2.0 / HEAD))
    )
    angles = jnp.arange(total).astype(F32)[:, None] * frequency[None, :]
    cos = jnp.cos(angles)
    sin = jnp.where(lane < HEAD // 2, -1.0, 1.0)[None, :] * jnp.sin(angles)
    qk = qk_gains.astype(F32)
    head_gains = jnp.concatenate([jnp.tile(qk[0], group), qk[1], jnp.ones((HEAD,), F32)])[None, :]

    inputs = tokens.reshape(count, width).astype(F32)
    r0 = lax.rsqrt(jnp.mean(inputs * inputs, axis=-1, keepdims=True) + EPSILON)
    unit0 = gather_plane((inputs * r0).astype(BF16))
    raw, q, kv = qkv_call(me, unit0, qkv_mine, cos, sin, head_gains, rows, slots)
    attended_mine, attended_low, logs = attend_call(lengths, q, kv, slots)
    attended = all_to_all(attended_low).transpose(1, 2, 0, 3).reshape(count, kv_at)
    middle = inputs + dot_nt(attended, out_full)
    r1 = lax.rsqrt(jnp.mean(middle * middle, axis=-1, keepdims=True) + EPSILON)

    grad_low = cotangent.reshape(count, width)
    grad_all = gather_plane(grad_low)
    unit1 = gather_plane((middle * r1).astype(BF16))
    act, d_gu = ffn_call(unit1, grad_all, gu_mine, down_mine)
    half = seq * count // 2
    u_odd = dot_nt(d_gu[half:], gu_mine).astype(BF16)
    u = scatter_plane(u_odd, dot_nt(d_gu[:half], gu_mine))
    down_sum = scatter_z(dot_tn(grad_all, act).astype(BF16))
    gu_sum = scatter_z(dot_tn(unit1, d_gu).astype(BF16))
    branch_odd = dot_nt(act[half:], down_mine).astype(BF16)
    branch = scatter_plane(branch_odd, dot_nt(act[:half], down_mine))
    output = (middle + branch).astype(BF16).reshape(rows, slots, width)

    d_middle = (
        grad_low.astype(F32)
        + r1 * u
        - middle * (r1 * r1 * r1) * jnp.mean(u * middle, axis=-1, keepdims=True)
    )
    d_branch = d_middle.astype(BF16)
    d_attended = dot_nn(d_branch, out_full).astype(BF16)
    d_attended = d_attended.reshape(rows, slots, seq, query_width).transpose(2, 0, 1, 3)
    d_attended = all_to_all(d_attended)
    out_sum = lax.psum_scatter(
        dot_tn(d_branch, attended).astype(BF16), "seq", scatter_dimension=0, tiled=True
    )
    out_sum = lax.psum_scatter(out_sum, "rows", scatter_dimension=0, tiled=True)
    dq, dkv = attend_back_call(lengths, q, kv, attended_mine, d_attended, logs)
    d_qkv, head_gain_grad = prepare_back_call(me, raw, dq, dkv, cos, sin, head_gains, slots)
    u0_odd = dot_nt(d_qkv[half:], qkv_mine).astype(BF16)
    u0 = scatter_plane(u0_odd, dot_nt(d_qkv[:half], qkv_mine))
    qkv_sum = scatter_z(dot_tn(unit0, d_qkv).astype(BF16))
    input_grad = (
        d_middle + r0 * u0 - inputs * (r0 * r0 * r0) * jnp.mean(u0 * inputs, axis=-1, keepdims=True)
    )
    input_grad = input_grad.astype(BF16).reshape(rows, slots, width)
    qk_grad = jnp.stack(
        [head_gain_grad[0, :query_width].reshape(group, HEAD).sum(0), head_gain_grad[0, query_width : query_width + HEAD]]
    )
    qk_grad = lax.psum(qk_grad, ("seq", "rows"))

    gu_sum = all_to_all(gu_sum).reshape(seq, depth, 2, part).transpose(1, 2, 0, 3)
    gu_sum = gu_sum.reshape(depth, 2 * seq * part).astype(F32)
    down_sum = all_to_all(down_sum).transpose(1, 0, 2).reshape(depth, seq * part).astype(F32)
    qkv_sum = all_to_all(qkv_sum).transpose(1, 0, 2).astype(F32)
    kv_sum = qkv_sum[:, :, query_width:].reshape(depth, KEY_VALUE_HEADS, sharing, 2 * HEAD).sum(2)
    qkv_sum = jnp.concatenate(
        [
            qkv_sum[:, :, :query_width].reshape(depth, -1),
            kv_sum[:, :, :HEAD].reshape(depth, -1),
            kv_sum[:, :, HEAD:].reshape(depth, -1),
        ],
        axis=1,
    )
    norm_gain_grad = jnp.stack(
        [
            jnp.sum(qkv_weight.astype(F32) * qkv_sum, axis=1),
            jnp.sum(gate_up_weight.astype(F32) * gu_sum, axis=1),
        ]
    )
    return (
        output,
        input_grad,
        norm_gain_grad,
        qk_grad,
        qkv_sum * gains[0][:, None],
        out_sum.astype(F32),
        gu_sum * gains[1][:, None],
        down_sum,
    )


def solution(mesh):
    in_specs = (
        P("rows", "seq", None),
        P("rows"),
        P(None, ("seq", "rows")),
        P(),
        P(("seq", "rows"), None),
        P(("seq", "rows"), None),
        P(("seq", "rows"), None),
        P(("seq", "rows"), None),
        P("rows", "seq", None),
    )
    out_specs = (
        P("rows", "seq", None),
        P("rows", "seq", None),
        P(None, ("seq", "rows")),
        P(),
        P(("seq", "rows"), None),
        P(("seq", "rows"), None),
        P(("seq", "rows"), None),
        P(("seq", "rows"), None),
    )
    return jax.shard_map(shards, mesh=mesh, in_specs=in_specs, out_specs=out_specs, check_vma=False)
```

```python
from functools import partial
import math

import jax
import jax.numpy as jnp
from jax import lax
from jax.experimental import pallas as pl
from jax.experimental.pallas import tpu as pltpu
from jax.sharding import PartitionSpec as P

QUERY_HEADS = 32
KEY_VALUE_HEADS = 8
HEAD = 64
EPSILON = 1e-06
F32 = jnp.float32
BF16 = jnp.bfloat16
HIGHEST = lax.Precision.HIGHEST
SCALE = HEAD ** (-0.5)
SCALE2 = SCALE * math.log2(math.e)
VMEM = 56 * 1024 * 1024


def swap(block, mask):
    return lax.ppermute(block, "seq", [(i, i ^ mask) for i in range(lax.axis_size("seq"))])


def masks_between_chips():
    return [1 << bit for bit in range(1, lax.axis_size("seq").bit_length() - 1)]


def natural(place, me, seq):
    return me[0] ^ (2 * lax.rem(place, seq // 2) + lax.div(place, seq // 2))


def dot_nn(a, b):
    return jnp.dot(a, b, preferred_element_type=F32)


def dot_nt(a, b, precision=None):
    return lax.dot_general(
        a, b, (((1,), (1,)), ((), ())), preferred_element_type=F32, precision=precision
    )


def dot_tn(a, b):
    return lax.dot_general(a, b, (((0,), (0,)), ((), ())), preferred_element_type=F32)


def corner(result):
    flat = result.reshape(-1, result.shape[-1])
    return flat[:16, :128]


def after(value, *results):
    zero = sum(result.reshape(-1)[0].astype(F32) for result in results) * 0.0
    return value + zero.astype(value.dtype)


def gather_pieces(chunk, earlier):
    half = chunk.shape[0] // 2
    along_x, along_y = swap(chunk, 2), swap(chunk, 4)
    through_x, through_y = after(along_y[:half], earlier), after(along_x[half:], earlier)
    return [chunk, along_x, along_y, swap(through_x, 2), swap(through_y, 4)]


def gather_plane(chunk):
    own = [chunk]
    for mask in masks_between_chips():
        own = own + [swap(part, mask) for part in own]
    return jnp.concatenate(own + [swap(part, 1) for part in own], axis=0)


def gather_natural(block):
    seq, me, size = lax.axis_size("seq"), lax.axis_index("seq"), block.shape[0]
    parts = {mask: swap(block, mask) if mask > 0 else block for mask in range(0, seq, 2)}
    parts.update({mask + 1: swap(part, 1) for mask, part in list(parts.items())})
    whole = jnp.zeros((seq * size,) + block.shape[1:], block.dtype)
    for m, part in parts.items():
        whole = lax.dynamic_update_slice_in_dim(whole, part, (me ^ m) * size, 0)
    return whole


def scatter_chips(parts):
    if len(parts) == 4:
        mine, to_x, to_y, diagonal = parts
        half = mine.shape[0] // 2
        diagonal = diagonal.astype(BF16)
        from_x = swap(diagonal[:half], 2).astype(F32)
        from_y = swap(diagonal[half:], 4).astype(F32)
        to_x = jnp.concatenate([to_x[:half], to_x[half:] + from_y], axis=0).astype(BF16)
        to_y = jnp.concatenate([to_y[:half] + from_x, to_y[half:]], axis=0).astype(BF16)
        return mine + swap(to_x, 2).astype(F32) + swap(to_y, 4).astype(F32)
    for mask in reversed(masks_between_chips()):
        kept = len(parts) // 2
        parts = [
            parts[i] + swap(parts[kept + i].astype(BF16), mask).astype(F32) for i in range(kept)
        ]
    return parts[0]


def scatter_direct(parts, earlier):
    total = after(parts[0].astype(F32), earlier)
    for i in range(1, len(parts)):
        total = total + swap(parts[i].astype(BF16), 2 * i).astype(F32)
    return total


def scatter_plane(odd, even, scatter=scatter_chips):
    count = 1 << len(masks_between_chips())
    size = even.shape[0] // count
    both = even + swap(odd, 1).astype(F32)
    return scatter([both[i * size : (i + 1) * size] for i in range(count)])


def sum_everywhere(value):
    for axis in ("seq", "rows"):
        size = lax.axis_size(axis)
        mask = 1
        while mask < size:
            value = value + lax.ppermute(value, axis, [(i, i ^ mask) for i in range(size)])
            mask *= 2
    return value


def lane_of(shape):
    return lax.broadcasted_iota(jnp.int32, shape, len(shape) - 1)


def swap_halves(v):
    first = lane_of(v.shape) % HEAD < HEAD // 2
    return jnp.where(first, pltpu.roll(v, 96, 1), pltpu.roll(v, 32, 1))


def head_mean(v):
    rows = lax.broadcasted_iota(jnp.int32, (128, 128), 0) // HEAD
    cols = lax.broadcasted_iota(jnp.int32, (128, 128), 1) // HEAD
    block = jnp.where(rows == cols, 1.0 / HEAD, 0.0).astype(F32)
    return jnp.dot(v, block, preferred_element_type=F32, precision=HIGHEST)


def qkv_kernel(me, x_ref, w_ref, cos_ref, sin_ref, gain_ref, raw_ref, q_ref, kv_ref):
    rows, slots = q_ref.shape[0], q_ref.shape[1]
    raw = dot_nn(x_ref[...], w_ref[...])
    cos, sin = cos_ref[...], sin_ref[...]
    keys = lane_of((slots, 128)) < HEAD
    for r in range(rows):
        part = raw[r * slots : (r + 1) * slots]
        raw_ref[r] = part
        last = part.shape[1] // 128 - 1
        for s in range(last + 1):
            v = part[:, s * 128 : (s + 1) * 128]
            out = normed_rotated(v, cos, sin, gain_ref[:, s * 128 : (s + 1) * 128])
            if s < last:
                q_ref[r, :, s * 128 : (s + 1) * 128] = out.astype(BF16)
            else:
                kv_ref[r] = jnp.where(keys, out, v).astype(BF16)


def qkv_call(me, x, w, cos, sin, gains, rows, slots):
    chunk = rows * slots
    width = w.shape[1]
    query_width = width - 128
    seq = x.shape[0] // chunk
    total = seq * slots
    return pl.pallas_call(
        qkv_kernel,
        grid_spec=pltpu.PrefetchScalarGridSpec(
            num_scalar_prefetch=1,
            grid=(seq,),
            in_specs=[
                pl.BlockSpec((chunk, x.shape[1]), lambda i, me: (i, 0)),
                pl.BlockSpec(w.shape, lambda i, me: (0, 0)),
                pl.BlockSpec((slots, 128), lambda i, me: (natural(i, me, seq), 0)),
                pl.BlockSpec((slots, 128), lambda i, me: (natural(i, me, seq), 0)),
                pl.BlockSpec((1, width), lambda i, me: (0, 0)),
            ],
            out_specs=[
                pl.BlockSpec((rows, slots, width), lambda i, me: (0, natural(i, me, seq), 0)),
                pl.BlockSpec((rows, slots, query_width), lambda i, me: (0, natural(i, me, seq), 0)),
                pl.BlockSpec((rows, slots, 128), lambda i, me: (0, natural(i, me, seq), 0)),
            ],
        ),
        out_shape=[
            jax.ShapeDtypeStruct((rows, total, width), F32),
            jax.ShapeDtypeStruct((rows, total, query_width), BF16),
            jax.ShapeDtypeStruct((rows, total, 128), BF16),
        ],
        compiler_params=pltpu.CompilerParams(vmem_limit_bytes=VMEM),
        name="qkv_prepare",
    )(me, x, w, cos, sin, gains)


def attend_kernel(lengths, q_ref, kv_ref, out_ref, low_ref, log_ref, k2, vo, acc):
    row, step = pl.program_id(0), pl.program_id(1)
    block = q_ref.shape[1]
    group = q_ref.shape[2] // HEAD
    length = lengths[row]

    @pl.when(step == 0)
    def _():
        kv = kv_ref[0].astype(F32)
        keys = lane_of(kv.shape) < HEAD
        k2[...] = jnp.where(keys, kv, pltpu.roll(kv, HEAD, 1)).astype(BF16)
        vo[...] = jnp.where(keys, 1.0, kv).astype(BF16)

    low_half = lane_of((block, 128)) < HEAD
    queries = []
    for h in range(group):
        part = q_ref[0, :, (h // 2) * 128 : (h // 2 + 1) * 128].astype(F32)
        kept = low_half if h % 2 == 0 else jnp.logical_not(low_half)
        queries.append(jnp.where(kept, part, 0.0).astype(BF16))
    acc[...] = jnp.zeros_like(acc)

    def one_block(at, masked):
        begin = pl.multiple_of(at * block, block)
        keys = k2[pl.ds(begin, block), :]
        values = vo[pl.ds(begin, block), :]
        if masked:
            key_place = begin + lax.broadcasted_iota(jnp.int32, (block, block), 1)
            query_place = step * block + lax.broadcasted_iota(jnp.int32, (block, block), 0)
            allowed = (key_place <= query_place) & (key_place < length)
        for h in range(group):
            weights = jnp.exp2(dot_nt(queries[h], keys) * SCALE2)
            if masked:
                weights = jnp.where(allowed, weights, 0.0)
            acc[h] += dot_nn(weights.astype(BF16), values)

    full = jnp.minimum(step, lax.div(length, block))

    def body(at, carry):
        one_block(at, False)
        return carry

    lax.fori_loop(0, full, body, 0)

    @pl.when(full * block < length)
    def _():
        one_block(full, True)

    for g in range(group // 2):
        even, odd = acc[2 * g], acc[2 * g + 1]
        even_turned, odd_turned = pltpu.roll(even, HEAD, 1), pltpu.roll(odd, HEAD, 1)
        mixed = jnp.where(low_half, even_turned / even, odd / odd_turned)
        out_ref[0, :, g * 128 : (g + 1) * 128] = mixed
        low_ref[0, 0, :, g * 128 : (g + 1) * 128] = mixed.astype(BF16)
        log_ref[0, 2 * g : 2 * g + 1, :] = jnp.log2(even.T[0:1, :])
        log_ref[0, 2 * g + 1 : 2 * g + 2, :] = jnp.log2(odd.T[0:1, :])
    log_ref[0, group:, :] = jnp.zeros((8 - group, block), F32)


def attend_call(lengths, q, kv, block):
    rows, total, width = q.shape
    seq = total // block
    return pl.pallas_call(
        attend_kernel,
        grid_spec=pltpu.PrefetchScalarGridSpec(
            num_scalar_prefetch=1,
            grid=(rows, seq),
            in_specs=[
                pl.BlockSpec((1, block, width), lambda r, i, n: (r, i, 0)),
                pl.BlockSpec((1, total, 128), lambda r, i, n: (r, 0, 0)),
            ],
            out_specs=[
                pl.BlockSpec((1, block, width), lambda r, i, n: (r, i, 0)),
                pl.BlockSpec((1, 1, block, width), lambda r, i, n: (i, r, 0, 0)),
                pl.BlockSpec((1, 8, block), lambda r, i, n: (r, 0, i)),
            ],
            scratch_shapes=[
                pltpu.VMEM((total, 128), BF16),
                pltpu.VMEM((total, 128), BF16),
                pltpu.VMEM((width // HEAD, block, 128), F32),
            ],
        ),
        out_shape=[
            jax.ShapeDtypeStruct((rows, total, width), F32),
            jax.ShapeDtypeStruct((seq, rows, block, width), BF16),
            jax.ShapeDtypeStruct((rows, 8, total), F32),
        ],
        compiler_params=pltpu.CompilerParams(vmem_limit_bytes=VMEM),
        cost_estimate=pl.CostEstimate(
            flops=rows * total * total * width * 16, bytes_accessed=rows * total * width * 8, transcendentals=0
        ),
        name="attend",
    )(lengths, q, kv)


def attend_back_kernel(
    lengths, q_ref, kv_ref, out_ref, grad_ref, log_ref, dq_ref, dkv_ref, delta, dqt, kacc, vacc
):
    row, step = pl.program_id(0), pl.program_id(1)
    block = kv_ref.shape[1]
    count = q_ref.shape[1] // block
    width = q_ref.shape[2]
    group = width // HEAD
    length = lengths[row]

    @pl.when(step == 0)
    def _():
        dqt[...] = jnp.zeros_like(dqt)
        heads = lax.broadcasted_iota(jnp.int32, (8, width), 0)
        pick = jnp.where(lane_of((8, width)) // HEAD == heads, 1.0, 0.0).astype(F32)
        for i in range(count):
            product = grad_ref[i, 0].astype(F32) * out_ref[0, i * block : (i + 1) * block, :]
            delta[:, i * block : (i + 1) * block] = dot_nt(pick, product, HIGHEST)

    kacc[...] = jnp.zeros_like(kacc)
    vacc[...] = jnp.zeros_like(vacc)
    begin = step * block
    kv = kv_ref[0].astype(F32)
    turned = pltpu.roll(kv, HEAD, 1)
    low_half = lane_of((block, 128)) < HEAD
    keys = [
        jnp.where(low_half, kv, 0.0).astype(BF16),
        jnp.where(low_half, 0.0, turned).astype(BF16),
    ]
    values = [
        jnp.where(low_half, turned, 0.0).astype(BF16),
        jnp.where(low_half, 0.0, kv).astype(BF16),
    ]
    keys_turned = [
        jnp.where(low_half, kv, 0.0).T.astype(BF16),
        jnp.where(low_half, 0.0, turned).T.astype(BF16),
    ]

    def one_block(at, masked):
        first = pl.multiple_of(at * block, block)
        if masked:
            key_place = begin + lax.broadcasted_iota(jnp.int32, (block, block), 0)
            query_place = first + lax.broadcasted_iota(jnp.int32, (block, block), 1)
            allowed = (key_place <= query_place) & (key_place < length)
        for g in range(group // 2):
            queries = q_ref[0, pl.ds(first, block), g * 128 : (g + 1) * 128]
            grads = grad_ref[at, 0, :, g * 128 : (g + 1) * 128]
            turned_sum = None
            for side in range(2):
                h = 2 * g + side
                logs = log_ref[0, h : h + 1, pl.ds(first, block)]
                deltas = delta[h : h + 1, pl.ds(first, block)]
                weights = jnp.exp2(dot_nt(keys[side], queries) * SCALE2 - logs)
                if masked:
                    weights = jnp.where(allowed, weights, 0.0)
                d_weights = dot_nt(values[side], grads)
                d_scores = (weights * (d_weights - deltas)).astype(BF16)
                vacc[side] += dot_nn(weights.astype(BF16), grads)
                kacc[side] += dot_nn(d_scores, queries)
                term = dot_nn(keys_turned[side], d_scores)
                turned_sum = term if turned_sum is None else turned_sum + term
            dqt[g, :, pl.ds(first, block)] += turned_sum

    @pl.when(begin < length)
    def _():
        inside = begin + block <= length

        @pl.when(inside)
        def _():
            one_block(step, True)

            def body(at, carry):
                one_block(at, False)
                return carry

            lax.fori_loop(step + 1, count, body, 0)

        @pl.when(jnp.logical_not(inside))
        def _():
            def body(at, carry):
                one_block(at, True)
                return carry

            lax.fori_loop(step, count, body, 0)

    ksum = jnp.where(low_half, kacc[0], 0.0) + pltpu.roll(jnp.where(low_half, 0.0, kacc[1]), HEAD, 1)
    vsum = pltpu.roll(jnp.where(low_half, vacc[0], 0.0), HEAD, 1) + jnp.where(
        low_half, 0.0, vacc[1]
    )
    dkv_ref[0] = jnp.where(low_half, ksum * SCALE, vsum)

    @pl.when(step == count - 1)
    def _():
        for g in range(group // 2):
            for i in range(count):
                dq_ref[0, i * block : (i + 1) * block, g * 128 : (g + 1) * 128] = (
                    dqt[g, :, i * block : (i + 1) * block].T * SCALE
                )


def attend_back_call(lengths, q, kv, attended, grads, logs):
    rows, total, width = q.shape
    seq, block = grads.shape[0], grads.shape[2]
    return pl.pallas_call(
        attend_back_kernel,
        grid_spec=pltpu.PrefetchScalarGridSpec(
            num_scalar_prefetch=1,
            grid=(rows, seq),
            in_specs=[
                pl.BlockSpec((1, total, width), lambda r, i, n: (r, 0, 0)),
                pl.BlockSpec((1, block, 128), lambda r, i, n: (r, i, 0)),
                pl.BlockSpec((1, total, width), lambda r, i, n: (r, 0, 0)),
                pl.BlockSpec((seq, 1, block, width), lambda r, i, n: (0, r, 0, 0)),
                pl.BlockSpec((1, 8, total), lambda r, i, n: (r, 0, 0)),
            ],
            out_specs=[
                pl.BlockSpec((1, total, width), lambda r, i, n: (r, 0, 0)),
                pl.BlockSpec((1, block, 128), lambda r, i, n: (r, i, 0)),
            ],
            scratch_shapes=[
                pltpu.VMEM((8, total), F32),
                pltpu.VMEM((width // 128, 128, total), F32),
                pltpu.VMEM((2, block, 128), F32),
                pltpu.VMEM((2, block, 128), F32),
            ],
        ),
        out_shape=[
            jax.ShapeDtypeStruct((rows, total, width), F32),
            jax.ShapeDtypeStruct((rows, total, 128), F32),
        ],
        compiler_params=pltpu.CompilerParams(vmem_limit_bytes=VMEM),
        cost_estimate=pl.CostEstimate(
            flops=rows * total * total * width * 28, bytes_accessed=rows * total * width * 14, transcendentals=0
        ),
        name="attend_back",
    )(lengths, q, kv, attended, grads, logs)


def prepare_back_kernel(
    me, raw_ref, dq_ref, dkv_ref, cos_ref, sin_ref, gain_ref, out_ref, gain_grad_ref
):
    rows, slots = dq_ref.shape[0], dq_ref.shape[1]
    cos, sin = cos_ref[...], sin_ref[...]
    keys = lane_of((slots, 128)) < HEAD
    last = raw_ref.shape[2] // 128 - 1

    @pl.when(pl.program_id(0) == 0)
    def _():
        gain_grad_ref[...] = jnp.zeros_like(gain_grad_ref)

    for r in range(rows):
        for s in range(last + 1):
            lanes = slice(s * 128, (s + 1) * 128)
            raw = raw_ref[r, :, lanes]
            grad = dq_ref[r, :, lanes] if s < last else dkv_ref[r]
            gain = gain_ref[:, lanes]
            turned = grad * cos + swap_halves(grad * sin)
            factor = lax.rsqrt(head_mean(raw * raw) + EPSILON)
            gain_grad_ref[:, lanes] += jnp.sum(turned * raw * factor, axis=0, keepdims=True)
            u = turned * gain
            mean = head_mean(u * raw)
            result = factor * u - raw * (factor * factor * factor) * mean
            if s == last:
                result = jnp.where(keys, result, grad)
            out_ref[r * slots : (r + 1) * slots, lanes] = result.astype(BF16)


def prepare_back_call(me, raw, dq, dkv, cos, sin, gains, slots):
    rows, total, width = raw.shape
    seq = total // slots
    return pl.pallas_call(
        prepare_back_kernel,
        grid_spec=pltpu.PrefetchScalarGridSpec(
            num_scalar_prefetch=1,
            grid=(seq,),
            in_specs=[
                pl.BlockSpec((rows, slots, width), lambda i, me: (0, natural(i, me, seq), 0)),
                pl.BlockSpec((rows, slots, width - 128), lambda i, me: (0, natural(i, me, seq), 0)),
                pl.BlockSpec((rows, slots, 128), lambda i, me: (0, natural(i, me, seq), 0)),
                pl.BlockSpec((slots, 128), lambda i, me: (natural(i, me, seq), 0)),
                pl.BlockSpec((slots, 128), lambda i, me: (natural(i, me, seq), 0)),
                pl.BlockSpec((1, width), lambda i, me: (0, 0)),
            ],
            out_specs=[
                pl.BlockSpec((rows * slots, width), lambda i, me: (i, 0)),
                pl.BlockSpec((1, width), lambda i, me: (0, 0)),
            ],
        ),
        out_shape=[
            jax.ShapeDtypeStruct((rows * total, width), BF16),
            jax.ShapeDtypeStruct((1, width), F32),
        ],
        compiler_params=pltpu.CompilerParams(vmem_limit_bytes=VMEM),
        name="prepare_back",
    )(me, raw, dq, dkv, cos, sin, gains)


def neighbours(me):
    return {
        "core": me + 1 - 2 * lax.rem(me, 2),
        "x": me + 2 - 4 * lax.rem(lax.div(me, 2), 2),
        "y": me + 4 - 8 * lax.div(me, 4),
    }


def remote(source, target, device, send, recv):
    return pltpu.make_async_remote_copy(
        src_ref=source,
        dst_ref=target,
        send_sem=send,
        recv_sem=recv,
        device_id=device,
        device_id_type=pl.DeviceIdType.MESH,
    )


def greet(devices):
    barrier = pltpu.get_barrier_semaphore()
    for device in devices:
        pl.semaphore_signal(barrier, inc=1, device_id=device, device_id_type=pl.DeviceIdType.MESH)
    pl.semaphore_wait(barrier, len(devices))


def greet_neighbours(to, rows):
    greet([(to[device], rows) for device in ("core", "x", "y")])


def flipped(index, mask, size):
    result, bit = index, 1
    while bit < size:
        if mask & bit:
            result = result + bit - 2 * bit * lax.rem(lax.div(index, bit), 2)
        bit *= 2
    return result


class PlaneExchange:
    def __init__(self, block, target, send, recv, local):
        self.seq, self.rows = lax.axis_index("seq"), lax.axis_index("rows")
        self.size = lax.axis_size("seq")
        self.block, self.target, self.send, self.recv, self.local = block, target, send, recv, local

    @staticmethod
    def scratch():
        others = lax.axis_size("seq") - 1
        return [
            pltpu.SemaphoreType.DMA((others,)),
            pltpu.SemaphoreType.DMA((others,)),
            pltpu.SemaphoreType.DMA,
        ]

    def peers(self):
        return [(flipped(self.seq, mask, self.size), self.rows) for mask in range(1, self.size)]

    def copies(self):
        remotes = [
            remote(self.block(peer[0]), self.target.at[self.seq], peer, self.send.at[i], self.recv.at[i])
            for i, peer in enumerate(self.peers())
        ]
        own = pltpu.make_async_copy(self.block(self.seq), self.target.at[self.seq], self.local)
        return remotes, own

    def start(self):
        remotes, own = self.copies()
        for copy in remotes:
            copy.start()
        own.start()

    def finish(self):
        remotes, own = self.copies()
        for copy in remotes:
            copy.wait()
        own.wait()


class PlaneGather:
    COPIES = 14

    def __init__(self, own, whole, send, recv):
        self.seq, self.rows = lax.axis_index("seq"), lax.axis_index("rows")
        self.half = own.shape[0] // 2
        self.own, self.whole, self.send, self.recv = own, whole, send, recv
        self.to = neighbours(self.seq)

    def place(self, at, half):
        return pl.ds((2 * at + half) * self.half, self.half)

    def copy(self, i):
        half, own, whole = self.half, self.own, self.whole
        first, second = own.at[pl.ds(0, half)], own.at[pl.ds(half, half)]

        def moved(at, h, to):
            return whole.at[self.place(at, h)], whole.at[self.place(to, h)]

        source, target, device = (
            (second, whole.at[self.place(1, 1)], "x"),
            (first, whole.at[self.place(2, 0)], "y"),
            (first, whole.at[self.place(1, 0)], "x"),
            (second, whole.at[self.place(2, 1)], "y"),
            (first, whole.at[self.place(4, 0)], "core"),
            (second, whole.at[self.place(4, 1)], "core"),
            moved(1, 1, 3) + ("y",),
            moved(2, 0, 3) + ("x",),
            moved(1, 1, 5) + ("core",),
            moved(2, 0, 6) + ("core",),
            moved(1, 0, 5) + ("core",),
            moved(2, 1, 6) + ("core",),
            moved(3, 0, 7) + ("core",),
            moved(3, 1, 7) + ("core",),
        )[i]
        return remote(
            source, target, (self.to[device], self.rows), self.send.at[i], self.recv.at[i]
        )

    def fetch(self, unit, target, sem):
        begin = pl.multiple_of(unit_place(unit) * self.half, self.half)
        return pltpu.make_async_copy(self.whole.at[pl.ds(begin, self.half)], target, sem)

    def start_fetch(self, unit, target, sem):
        @pl.when(unit < 2)
        def _():
            begin = pl.multiple_of(lax.rem(unit, 2) * self.half, self.half)
            pltpu.make_async_copy(self.own.at[pl.ds(begin, self.half)], target, sem).start()

        @pl.when(unit >= 2)
        def _():
            self.fetch(unit, target, sem).start()

    def keep(self, unit, source, sem):
        begin = pl.multiple_of(lax.rem(unit, 2) * self.half, self.half)
        return pltpu.make_async_copy(source, self.whole.at[pl.ds(begin, self.half)], sem)

    def start(self):
        for i in (0, 1, 2, 3, 4, 5):
            self.copy(i).start()

    def open_group(self, group):
        if group == 1:
            self.copy(0).wait_recv()
            self.copy(6).start()
            self.copy(8).start()
            self.copy(1).wait_recv()
            self.copy(7).start()
            self.copy(9).start()
        if group == 2:
            self.copy(2).wait_recv()
            self.copy(10).start()
            self.copy(3).wait_recv()
            self.copy(11).start()
        if group == 3:
            self.copy(7).wait_recv()
            self.copy(12).start()
            self.copy(6).wait_recv()
            self.copy(13).start()

    def open_second(self, group):
        for i in ((4, 5), (8, 9), (10, 11), (12, 13))[group]:
            self.copy(i).wait_recv()

    def finish(self):
        for i in range(self.COPIES):
            self.copy(i).wait_send()


def unit_place(unit):
    group, k = lax.div(unit, 4), lax.rem(unit, 4)
    odd, late = lax.rem(group, 2), lax.div(group, 2)
    base = 3 * odd + 2 * late + odd * late
    stride = 1 + 2 * late * (1 - odd)
    return 8 * lax.div(k, 2) + base + stride * lax.rem(k, 2)


def at_unit(unit, value, action):
    @pl.when(unit == value)
    def _():
        action()


def normed_rotated(raw, cos, sin, gain):
    factor = lax.rsqrt(head_mean(raw * raw) + EPSILON)
    n = raw * factor * gain
    return n * cos + swap_halves(n) * sin


def gather_qkv_kernel(
    x_ref, w_ref, cos_ref, sin_ref, gain_ref, whole, raw_ref, q_ref, kv_ref,
    xbuf, rawbuf, qbuf, kvbuf, load, store, keep, send, recv,
):
    gather = PlaneGather(x_ref, whole, send, recv)
    half = gather.half
    me = gather.seq
    last = w_ref.shape[1] // 128 - 1
    greet_neighbours(gather.to, gather.rows)
    gather.start()

    def stores(unit, slot):
        place = unit_place(unit)
        at, row = lax.rem(lax.div(place, 2), 4), lax.rem(place, 2)
        core = lax.rem(lax.rem(me, 2) + lax.div(place, 8), 2)
        x = lax.rem(lax.div(me, 2) + at, 2)
        y = lax.rem(lax.div(me, 4) + lax.div(at, 2), 2)
        block = core + 2 * x + 4 * y
        begin = pl.ds(pl.multiple_of(block * half, half), half)
        return [
            pltpu.make_async_copy(rawbuf.at[slot], raw_ref.at[row, begin], store.at[0, slot]),
            pltpu.make_async_copy(qbuf.at[slot], q_ref.at[row, begin], store.at[1, slot]),
            pltpu.make_async_copy(kvbuf.at[slot], kv_ref.at[row, begin], store.at[2, slot]),
        ], block

    def body(unit, carry):
        slot = lax.rem(unit, 2)
        for group in range(4):
            at_unit(unit, 4 * group, partial(gather.open_group, group))
            at_unit(unit, 4 * group + 1, partial(gather.open_second, group))

        @pl.when(lax.rem(unit, 4) == 0)
        def _():
            gather.start_fetch(unit, xbuf.at[slot], load.at[slot])

        gather.fetch(unit, xbuf.at[slot], load.at[slot]).wait()

        @pl.when(unit < 2)
        def _():
            gather.keep(unit, xbuf.at[slot], keep.at[slot]).start()

        @pl.when((unit == 1) | (unit == 2))
        def _():
            gather.keep(unit - 1, xbuf.at[1 - slot], keep.at[1 - slot]).wait()

        @pl.when(lax.rem(unit, 4) != 3)
        def _():
            gather.start_fetch(unit + 1, xbuf.at[1 - slot], load.at[1 - slot])

        copies, block = stores(unit, slot)

        @pl.when(unit >= 2)
        def _():
            for copy in stores(unit - 2, slot)[0]:
                copy.wait()

        raw = dot_nn(xbuf[slot], w_ref[...])
        rawbuf[slot] = raw
        turn = pl.ds(pl.multiple_of(block * half, half), half)
        cos, sin = cos_ref[turn, :], sin_ref[turn, :]
        for s in range(last + 1):
            lanes = slice(s * 128, (s + 1) * 128)
            v = raw[:, lanes]
            out = normed_rotated(v, cos, sin, gain_ref[:, lanes])
            if s < last:
                qbuf[slot, :, lanes] = out.astype(BF16)
            else:
                kvbuf[slot] = jnp.where(lane_of(v.shape) < HEAD, out, v).astype(BF16)
        for copy in copies:
            copy.start()
        return carry

    lax.fori_loop(0, 16, body, 0)
    for slot in range(2):
        for copy in stores(14 + slot, slot)[0]:
            copy.wait()
    gather.finish()


def gather_qkv_call(x, w, cos, sin, gains, rows, slots):
    count, width = x.shape
    seq = lax.axis_size("seq")
    total = seq * slots
    cols = w.shape[1]
    here, there = pl.BlockSpec(memory_space=pltpu.VMEM), pl.BlockSpec(memory_space=pl.ANY)
    return pl.pallas_call(
        gather_qkv_kernel,
        in_specs=[there, here, here, here, here],
        out_specs=[there] * 4,
        out_shape=[
            jax.ShapeDtypeStruct((seq * count, width), BF16),
            jax.ShapeDtypeStruct((rows, total, cols), F32),
            jax.ShapeDtypeStruct((rows, total, cols - 128), BF16),
            jax.ShapeDtypeStruct((rows, total, 128), BF16),
        ],
        scratch_shapes=[
            pltpu.VMEM((2, slots, width), BF16),
            pltpu.VMEM((2, slots, cols), F32),
            pltpu.VMEM((2, slots, cols - 128), BF16),
            pltpu.VMEM((2, slots, 128), BF16),
            pltpu.SemaphoreType.DMA((2,)),
            pltpu.SemaphoreType.DMA((3, 2)),
            pltpu.SemaphoreType.DMA((2,)),
            pltpu.SemaphoreType.DMA((PlaneGather.COPIES,)),
            pltpu.SemaphoreType.DMA((PlaneGather.COPIES,)),
        ],
        compiler_params=pltpu.CompilerParams(
            collective_id=1, has_side_effects=True, vmem_limit_bytes=VMEM
        ),
        cost_estimate=pl.CostEstimate(
            flops=2 * seq * count * width * cols * 8, bytes_accessed=seq * count * width * 4, transcendentals=0
        ),
        name="gather_qkv",
    )(x, w, cos, sin, gains)


class PlaneScatter:
    def __init__(self, own, from_x, from_y, odd, even, held, other, diagonal, sems):
        self.seq, self.rows = lax.axis_index("seq"), lax.axis_index("rows")
        self.to = neighbours(self.seq)
        self.half = odd.shape[1]
        self.own, self.from_x, self.from_y = own, from_x, from_y
        self.odd, self.even, self.held, self.other, self.diagonal = odd, even, held, other, diagonal
        self.odd_send, self.odd_recv, self.send, self.recv, self.store = sems

    @staticmethod
    def scratch(half, width):
        return [
            pltpu.VMEM((2, half, width), BF16),
            pltpu.VMEM((6, half, width), BF16),
            pltpu.VMEM((2, half, width), F32),
            pltpu.VMEM((8, half, width), BF16),
            pltpu.VMEM((2, half, width), BF16),
            pltpu.SemaphoreType.DMA((2,)),
            pltpu.SemaphoreType.DMA((8,)),
            pltpu.SemaphoreType.DMA((6,)),
            pltpu.SemaphoreType.DMA((6,)),
            pltpu.SemaphoreType.DMA((2,)),
        ]

    @staticmethod
    def place(pair):
        two, b = lax.div(pair, 2), lax.rem(pair, 2)
        odd, late = lax.rem(two, 2), lax.div(two, 2)
        base = 6 * (1 - odd) * (1 - late) + 2 * odd * (1 - late) + 3 * (1 - odd) * late
        return base + b * (1 + 2 * odd * (1 - late))

    def hand_over(self, pair):
        slot = lax.rem(pair, 2)
        return remote(
            self.odd.at[slot],
            self.other.at[pair],
            (self.to["core"], self.rows),
            self.odd_send.at[slot],
            self.odd_recv.at[pair],
        )

    def copy(self, i):
        first, second = pl.ds(0, self.half), pl.ds(self.half, self.half)
        target, device = (
            (self.diagonal.at[0], "x"),
            (self.diagonal.at[1], "y"),
            (self.from_x.at[first], "x"),
            (self.from_y.at[second], "y"),
            (self.from_x.at[second], "x"),
            (self.from_y.at[first], "y"),
        )[i]
        return remote(
            self.even.at[i], target, (self.to[device], self.rows), self.send.at[i], self.recv.at[i]
        )

    def keep(self, i):
        return pltpu.make_async_copy(
            self.held.at[i], self.own.at[pl.ds(i * self.half, self.half)], self.store.at[i]
        )

    def give_odd(self, pair, value):
        @pl.when(pair >= 2)
        def _():
            self.hand_over(pair - 2).wait_send()

        self.odd[lax.rem(pair, 2)] = value.astype(BF16)
        self.hand_over(pair).start()

    def give_even(self, pair, value_ref):
        self.hand_over(pair).wait_recv()
        for at, i in ((0, 0), (1, 1), (2, 2), (3, 3), (4, 4), (5, 5)):

            @pl.when(pair == at)
            def _(at=at, i=i):
                total = value_ref[...] + self.other[at].astype(F32)
                if i >= 4:
                    self.copy(5 - i).wait_recv()
                    total = total + self.diagonal[5 - i].astype(F32)
                self.even[i] = total.astype(BF16)
                self.copy(i).start()

        for at, i in ((6, 0), (7, 1)):

            @pl.when(pair == at)
            def _(at=at, i=i):
                self.held[i] = value_ref[...] + self.other[at].astype(F32)
                self.keep(i).start()

    def finish(self):
        for pair in (6, 7):
            self.hand_over(pair).wait_send()
        for i in range(6):
            self.copy(i).wait_send()
        for i in (2, 3, 4, 5):
            self.copy(i).wait_recv()
        for i in range(2):
            self.keep(i).wait()


def gate_and_up(hidden, gu_ref):
    part = gu_ref.shape[1] // 2
    gate = dot_nn(hidden, gu_ref[:, :part])
    up = dot_nn(hidden, gu_ref[:, part:])
    return gate, up, (gate / (1.0 + jnp.exp(-gate)) * up).astype(BF16)


def gate_and_up_back(gate, up, d_act):
    sigmoid = 1.0 / (1.0 + jnp.exp(-gate))
    silu = gate * sigmoid
    d_gate = d_act * up * (sigmoid + silu * (1.0 - sigmoid))
    return d_gate.astype(BF16), (d_act * silu).astype(BF16)


def gather_ffn_kernel(
    x_ref, c0_ref, cx_ref, cy_ref, cd0_ref, cd1_ref, gu_hbm,
    whole, near_ref, far_ref, gate_up_ref, act_ref,
    gu, hbuf, cbuf, gbuf, abuf, weight_sem, load, store, keep, send, recv, piece_send, piece_recv,
):
    gather = PlaneGather(x_ref, whole, send, recv)
    half = gather.half
    part = gu.shape[1] // 2
    weights = pltpu.make_async_copy(gu_hbm, gu, weight_sem)
    weights.start()
    greet_neighbours(gather.to, gather.rows)
    gather.start()

    def stores(unit, slot):
        begin = pl.ds(pl.multiple_of(unit_place(unit) * half, half), half)
        return [
            pltpu.make_async_copy(abuf.at[slot], act_ref.at[begin], store.at[0, slot]),
            pltpu.make_async_copy(gbuf.at[slot], gate_up_ref.at[begin], store.at[1, slot]),
        ]

    piece_refs = (c0_ref, cx_ref, cy_ref, cd0_ref, cd1_ref)
    piece_at = ((0, 2), (2, 2), (4, 2), (6, 1), (7, 1))

    def piece(i):
        begin, size = piece_at[i]
        target = far_ref.at[pl.ds(begin * half, size * half)]
        return remote(
            piece_refs[i],
            target,
            (gather.to["core"], gather.rows),
            piece_send.at[i],
            piece_recv.at[i],
        )

    for i in range(5):
        piece(i).start()

    def passing(at):
        i = (0, 0, 1, 1, 2, 2, 3, 4)[at]
        source = piece_refs[i].at[pl.ds((at - piece_at[i][0]) * half, half)]
        return (
            pltpu.make_async_copy(source, cbuf.at[at % 2], keep.at[1, 0]),
            pltpu.make_async_copy(
                cbuf.at[at % 2], near_ref.at[pl.ds(at * half, half)], keep.at[1, 1]
            ),
        )

    def read_piece(at):
        passing(at)[0].start()

    def write_piece(at):
        passing(at)[0].wait()
        passing(at)[1].start()

    def end_piece(at):
        passing(at)[1].wait()

    def body(unit, carry):
        slot = lax.rem(unit, 2)
        for at in range(8):
            at_unit(unit, 2 * at, partial(read_piece, at))
            at_unit(unit, 2 * at + 1, partial(write_piece, at))
            if at < 7:
                at_unit(unit, 2 * at + 2, partial(end_piece, at))
        for group in range(4):
            at_unit(unit, 4 * group, partial(gather.open_group, group))
            at_unit(unit, 4 * group + 1, partial(gather.open_second, group))

        @pl.when(lax.rem(unit, 4) == 0)
        def _():
            gather.start_fetch(unit, hbuf.at[slot], load.at[slot])

        at_unit(unit, 0, weights.wait)
        gather.fetch(unit, hbuf.at[slot], load.at[slot]).wait()

        @pl.when(unit < 2)
        def _():
            gather.keep(unit, hbuf.at[slot], keep.at[0, slot]).start()

        @pl.when((unit == 1) | (unit == 2))
        def _():
            gather.keep(unit - 1, hbuf.at[1 - slot], keep.at[0, 1 - slot]).wait()

        @pl.when(lax.rem(unit, 4) != 3)
        def _():
            gather.start_fetch(unit + 1, hbuf.at[1 - slot], load.at[1 - slot])

        @pl.when(unit >= 2)
        def _():
            for copy in stores(unit - 2, slot):
                copy.wait()

        gate, up, act = gate_and_up(hbuf[slot], gu)
        abuf[slot] = act
        gbuf[slot, :, :part] = gate.astype(BF16)
        gbuf[slot, :, part:] = up.astype(BF16)
        for copy in stores(unit, slot):
            copy.start()
        return carry

    lax.fori_loop(0, 16, body, 0)
    for slot in range(2):
        for copy in stores(14 + slot, slot):
            copy.wait()
    end_piece(7)
    for i in range(5):
        piece(i).wait_recv()
        piece(i).wait_send()
    gather.finish()


def gather_ffn_call(x, pieces, gu):
    count, width = x.shape
    seq = lax.axis_size("seq")
    cols = gu.shape[1]
    half = count // 2
    there = pl.BlockSpec(memory_space=pl.ANY)
    return pl.pallas_call(
        gather_ffn_kernel,
        in_specs=[there] * 7,
        out_specs=[there] * 5,
        out_shape=[
            jax.ShapeDtypeStruct((seq * count, width), BF16),
            jax.ShapeDtypeStruct((seq * half, width), BF16),
            jax.ShapeDtypeStruct((seq * half, width), BF16),
            jax.ShapeDtypeStruct((seq * count, cols), BF16),
            jax.ShapeDtypeStruct((seq * count, cols // 2), BF16),
        ],
        scratch_shapes=[
            pltpu.VMEM(gu.shape, BF16),
            pltpu.VMEM((2, half, width), BF16),
            pltpu.VMEM((2, half, width), BF16),
            pltpu.VMEM((2, half, cols), BF16),
            pltpu.VMEM((2, half, cols // 2), BF16),
            pltpu.SemaphoreType.DMA,
            pltpu.SemaphoreType.DMA((2,)),
            pltpu.SemaphoreType.DMA((2, 2)),
            pltpu.SemaphoreType.DMA((2, 2)),
            pltpu.SemaphoreType.DMA((PlaneGather.COPIES,)),
            pltpu.SemaphoreType.DMA((PlaneGather.COPIES,)),
            pltpu.SemaphoreType.DMA((5,)),
            pltpu.SemaphoreType.DMA((5,)),
        ],
        compiler_params=pltpu.CompilerParams(
            collective_id=2, has_side_effects=True, vmem_limit_bytes=VMEM
        ),
        cost_estimate=pl.CostEstimate(
            flops=4 * seq * count * width * cols, bytes_accessed=seq * count * width * 8, transcendentals=0
        ),
        name="gather_ffn",
    )(x, *pieces, gu)


def ffn_back_kernel(
    near_ref, far_ref, gate_up_ref, gu_hbm, down_hbm, _, own, from_x, from_y, dgu_ref,
    gu, down, cbuf, gbuf, dbuf, total, odd, even, held, other, diagonal,
    odd_send, odd_recv, send, recv, keep, weight_sem, load, store,
):
    scatter = PlaneScatter(
        own, from_x, from_y, odd, even, held, other, diagonal, (odd_send, odd_recv, send, recv, keep)
    )
    half = scatter.half
    part = down.shape[1]
    weights = [
        pltpu.make_async_copy(down_hbm, down, weight_sem.at[0]),
        pltpu.make_async_copy(gu_hbm, gu, weight_sem.at[1]),
    ]
    for copy in weights:
        copy.start()

    def row_of(unit, whole):
        side = 8 * (1 - lax.rem(unit, 2)) if whole else 0
        place = PlaneScatter.place(lax.div(unit, 2)) + side
        return pl.ds(pl.multiple_of(place * half, half), half)

    def fetch(unit, slot):
        return [
            pltpu.make_async_copy(near_ref.at[row_of(unit, False)], cbuf.at[slot], load.at[0, slot]),
            pltpu.make_async_copy(
                gate_up_ref.at[row_of(unit, True)], gbuf.at[slot], load.at[1, slot]
            ),
        ]

    def start_fetch(unit, slot):
        near, gates = fetch(unit, slot)
        gates.start()

        @pl.when(lax.rem(unit, 2) == 0)
        def _():
            pltpu.make_async_copy(
                far_ref.at[row_of(unit, False)], cbuf.at[slot], load.at[0, slot]
            ).start()

        @pl.when(lax.rem(unit, 2) == 1)
        def _():
            near.start()

    def stores(unit, slot):
        return pltpu.make_async_copy(dbuf.at[slot], dgu_ref.at[row_of(unit, True)], store.at[slot])

    start_fetch(0, 0)
    greet_neighbours(scatter.to, scatter.rows)

    def body(unit, carry):
        slot = lax.rem(unit, 2)
        pair = lax.div(unit, 2)
        at_unit(unit, 0, weights[0].wait)
        for copy in fetch(unit, slot):
            copy.wait()

        @pl.when(unit < 15)
        def _():
            start_fetch(unit + 1, 1 - slot)

        @pl.when(unit >= 2)
        def _():
            stores(unit - 2, slot).wait()

        d_act = dot_nn(cbuf[slot], down[...])
        gate, up = gbuf[slot, :, :part].astype(F32), gbuf[slot, :, part:].astype(F32)
        d_gate, d_up = gate_and_up_back(gate, up, d_act)
        dbuf[slot, :, :part] = d_gate
        dbuf[slot, :, part:] = d_up
        stores(unit, slot).start()
        at_unit(unit, 0, weights[1].wait)
        total[...] = dot_nt(dbuf[slot], gu[...])

        @pl.when(slot == 0)
        def _():
            scatter.give_odd(pair, total[...])

        @pl.when(slot == 1)
        def _():
            scatter.give_even(pair, total)

        return carry

    lax.fori_loop(0, 16, body, 0)
    for slot in range(2):
        stores(14 + slot, slot).wait()
    scatter.finish()


def weight_grad_kernel(*refs):
    lefts, right_ref, out_ref = refs[:-3], refs[-3], refs[-1]
    depth = out_ref.shape[1]
    size = right_ref.shape[0] // len(lefts)
    grad = None
    for i, left in enumerate(lefts):
        term = dot_tn(left[...], right_ref[i * size : (i + 1) * size, :])
        grad = term if grad is None else grad + term
    for z in range(out_ref.shape[0]):
        out_ref[z] = grad[z * depth : (z + 1) * depth].astype(BF16)


def weight_grad_call(lefts, right, earlier, depth, name):
    seq, parts = lax.axis_size("seq"), lax.axis_size("rows")
    width = lefts[0].shape[1]
    block = width // seq
    tokens, cols = right.shape
    return pl.pallas_call(
        weight_grad_kernel,
        grid=(seq,),
        in_specs=[pl.BlockSpec((left.shape[0], block), lambda i: (0, i)) for left in lefts]
        + [
            pl.BlockSpec(right.shape, lambda i: (0, 0), pipeline_mode=pl.Buffered(1)),
            pl.BlockSpec(memory_space=pl.ANY),
        ],
        out_specs=pl.BlockSpec((parts, depth, cols), lambda i: (0, i, 0)),
        out_shape=jax.ShapeDtypeStruct((parts, seq * depth, cols), BF16),
        compiler_params=pltpu.CompilerParams(vmem_limit_bytes=VMEM),
        cost_estimate=pl.CostEstimate(
            flops=2 * tokens * width * cols,
            bytes_accessed=2 * tokens * (width + cols),
            transcendentals=0,
        ),
        name=name,
    )(*lefts, right, earlier)


def grad_exchange_kernel(
    left_ref, right_ref, spread_ref, blocks_ref, _, out_ref, spread_out, blocks_out, *sems
):
    width = spread_out.shape[2]

    def columns(i):
        return spread_ref.at[:, pl.ds(pl.multiple_of(i * width, width), width)]

    spread = PlaneExchange(columns, spread_out, *sems[:3])
    blocks = PlaneExchange(lambda i: blocks_ref.at[i], blocks_out, *sems[3:])

    @pl.when(pl.program_id(0) == 0)
    def _():
        greet(spread.peers())
        spread.start()
        blocks.start()

    depth = out_ref.shape[1]
    grad = dot_tn(left_ref[...], right_ref[...])
    for z in range(out_ref.shape[0]):
        out_ref[z] = grad[z * depth : (z + 1) * depth].astype(BF16)

    @pl.when(pl.program_id(0) == pl.num_programs(0) - 1)
    def _():
        spread.finish()
        blocks.finish()


def grad_exchange_call(left, right, spread, blocks, earlier, depth):
    seq, parts = lax.axis_size("seq"), lax.axis_size("rows")
    tokens, cols = right.shape
    width = left.shape[1]
    block = width // seq
    there = pl.BlockSpec(memory_space=pl.ANY)
    return pl.pallas_call(
        grad_exchange_kernel,
        grid=(seq,),
        in_specs=[
            pl.BlockSpec((tokens, block), lambda i: (0, i)),
            pl.BlockSpec(right.shape, lambda i: (0, 0), pipeline_mode=pl.Buffered(1)),
            there,
            there,
            there,
        ],
        out_specs=[pl.BlockSpec((parts, depth, cols), lambda i: (0, i, 0)), there, there],
        out_shape=[
            jax.ShapeDtypeStruct((parts, seq * depth, cols), BF16),
            jax.ShapeDtypeStruct((seq, spread.shape[0], spread.shape[1] // seq), BF16),
            jax.ShapeDtypeStruct(blocks.shape, BF16),
        ],
        scratch_shapes=PlaneExchange.scratch() + PlaneExchange.scratch(),
        compiler_params=pltpu.CompilerParams(
            collective_id=5, has_side_effects=True, vmem_limit_bytes=VMEM
        ),
        cost_estimate=pl.CostEstimate(
            flops=2 * tokens * width * cols,
            bytes_accessed=2 * tokens * (width + cols),
            transcendentals=0,
        ),
        name="gate_up_grad",
    )(left, right, spread, blocks, earlier)


def branch_kernel(near_ref, far_ref, w_ref, _, near_out, far_out):
    near_out[...] = dot_nt(near_ref[...], w_ref[...]).astype(BF16)
    far_out[...] = dot_nt(far_ref[...], w_ref[...]).astype(BF16)


def branch_call(act, w, earlier):
    tokens, part = act.shape
    width = w.shape[0]
    block = 256
    steps = tokens // 2 // block
    shape = jax.ShapeDtypeStruct((tokens // 2, width), BF16)
    return pl.pallas_call(
        branch_kernel,
        grid=(steps,),
        in_specs=[
            pl.BlockSpec((block, part), lambda i: (i, 0)),
            pl.BlockSpec((block, part), lambda i: (i + steps, 0)),
            pl.BlockSpec(w.shape, lambda i: (0, 0), pipeline_mode=pl.Buffered(1)),
            pl.BlockSpec(memory_space=pl.ANY),
        ],
        out_specs=[pl.BlockSpec((block, width), lambda i: (i, 0))] * 2,
        out_shape=[shape, shape],
        compiler_params=pltpu.CompilerParams(vmem_limit_bytes=VMEM),
        cost_estimate=pl.CostEstimate(
            flops=2 * tokens * width * part, bytes_accessed=2 * tokens * width, transcendentals=0
        ),
        name="branch",
    )(act, act, w, earlier)


def out_grad_kernel(me, near_ref, far_ref, right_ref, _, near_out, far_out):
    near_out[...] = dot_tn(near_ref[...], right_ref[...]).astype(BF16)
    far_out[...] = dot_tn(far_ref[...], right_ref[...]).astype(BF16)


def out_grad_call(me, left, right, earlier):
    seq = lax.axis_size("seq")
    tokens, width = left.shape
    block, cols = width // seq, right.shape[1]
    shape = jax.ShapeDtypeStruct((width // 2, cols), BF16)
    return pl.pallas_call(
        out_grad_kernel,
        grid_spec=pltpu.PrefetchScalarGridSpec(
            num_scalar_prefetch=1,
            grid=(seq // 2,),
            in_specs=[
                pl.BlockSpec((tokens, block), lambda i, me: (0, natural(i, me, seq))),
                pl.BlockSpec((tokens, block), lambda i, me: (0, natural(i + seq // 2, me, seq))),
                pl.BlockSpec(right.shape, lambda i, me: (0, 0)),
                pl.BlockSpec(memory_space=pl.ANY),
            ],
            out_specs=[pl.BlockSpec((block, cols), lambda i, me: (i, 0))] * 2,
        ),
        out_shape=[shape, shape],
        compiler_params=pltpu.CompilerParams(vmem_limit_bytes=VMEM),
        cost_estimate=pl.CostEstimate(
            flops=2 * tokens * width * cols, bytes_accessed=2 * width * cols, transcendentals=0
        ),
        name="out_grad",
    )(me, left, left, right, earlier)


def scatter_shapes(count, width):
    return [
        jax.ShapeDtypeStruct((count, width), F32),
        jax.ShapeDtypeStruct((count, width), BF16),
        jax.ShapeDtypeStruct((count, width), BF16),
    ]


def ffn_back_call(near, far, gate_up, gu, down, count, earlier):
    width, part = down.shape
    half = count // 2
    there = pl.BlockSpec(memory_space=pl.ANY)
    own, from_x, from_y, d_gu = pl.pallas_call(
        ffn_back_kernel,
        in_specs=[there] * 6,
        out_specs=[there] * 4,
        out_shape=scatter_shapes(count, width) + [jax.ShapeDtypeStruct(gate_up.shape, BF16)],
        scratch_shapes=[
            pltpu.VMEM(gu.shape, BF16),
            pltpu.VMEM(down.shape, BF16),
            pltpu.VMEM((2, half, width), BF16),
            pltpu.VMEM((2, half, 2 * part), BF16),
            pltpu.VMEM((2, half, 2 * part), BF16),
            pltpu.VMEM((half, width), F32),
        ]
        + PlaneScatter.scratch(half, width)
        + [
            pltpu.SemaphoreType.DMA((2,)),
            pltpu.SemaphoreType.DMA((2, 2)),
            pltpu.SemaphoreType.DMA((2,)),
        ],
        compiler_params=pltpu.CompilerParams(
            collective_id=3, has_side_effects=True, vmem_limit_bytes=VMEM
        ),
        cost_estimate=pl.CostEstimate(
            flops=8 * gate_up.shape[0] * width * part, bytes_accessed=gate_up.shape[0] * width * 8, transcendentals=0
        ),
        name="ffn_back",
    )(near, far, gate_up, gu, down, earlier)
    return own + from_x.astype(F32) + from_y.astype(F32), d_gu


def project_back_kernel(
    d_ref, w_ref, gain_ref, blocks_ref, own, from_x, from_y, gain_out, blocks_out,
    gain_sum, gain_from, gain_send, gain_recv, block_send, block_recv, block_local,
    total, odd, even, held, other, diagonal, odd_send, odd_recv, send, recv, keep,
):
    scatter = PlaneScatter(
        own, from_x, from_y, odd, even, held, other, diagonal, (odd_send, odd_recv, send, recv, keep)
    )
    half = scatter.half
    blocks = PlaneExchange(
        lambda i: blocks_ref.at[i], blocks_out, block_send, block_recv, block_local
    )
    partners = [(scatter.to[device], scatter.rows) for device in ("core", "x", "y")]
    size = lax.axis_size("rows")
    mask = 1
    others = []
    while mask < size:
        others.append((scatter.seq, flipped(scatter.rows, mask, size)))
        mask *= 2
    partners = partners + others
    greet(blocks.peers() + others)
    gain_sum[0] = gain_ref[...]

    def exchange(i):
        return remote(
            gain_sum.at[i], gain_from.at[i], partners[i], gain_send.at[i], gain_recv.at[i]
        )

    def add_gains(i):
        exchange(i).wait_recv()
        gain_sum[i + 1] = gain_sum[i] + gain_from[i]

    def body(unit, carry):
        for i in range(len(partners)):
            at_unit(unit, 2 * i + 1, exchange(i).start)
            at_unit(unit, 2 * i + 2, partial(add_gains, i))
        at_unit(unit, 8, blocks.start)
        pair, side = lax.div(unit, 2), 1 - lax.rem(unit, 2)
        begin = pl.multiple_of((PlaneScatter.place(pair) + 8 * side) * half, half)
        total[...] = dot_nt(d_ref[pl.ds(begin, half), :], w_ref[...])

        @pl.when(side == 1)
        def _():
            scatter.give_odd(pair, total[...])

        @pl.when(side == 0)
        def _():
            scatter.give_even(pair, total)

        return carry

    lax.fori_loop(0, 16, body, 0)
    gain_out[...] = gain_sum[len(partners)]
    blocks.finish()
    for i in range(len(partners)):
        exchange(i).wait_send()
    scatter.finish()


def project_back_call(d, w, gains, blocks, count):
    width = w.shape[0]
    half = count // 2
    here, there = pl.BlockSpec(memory_space=pltpu.VMEM), pl.BlockSpec(memory_space=pl.ANY)
    rounds = 3 + (lax.axis_size("rows") - 1).bit_length()
    own, from_x, from_y, gains, blocks = pl.pallas_call(
        project_back_kernel,
        in_specs=[here] * 3 + [there],
        out_specs=[there] * 3 + [here, there],
        out_shape=scatter_shapes(count, width) + [
            jax.ShapeDtypeStruct(gains.shape, F32),
            jax.ShapeDtypeStruct(blocks.shape, BF16),
        ],
        scratch_shapes=[
            pltpu.VMEM((rounds + 1,) + gains.shape, F32),
            pltpu.VMEM((rounds,) + gains.shape, F32),
            pltpu.SemaphoreType.DMA((rounds,)),
            pltpu.SemaphoreType.DMA((rounds,)),
        ]
        + PlaneExchange.scratch()
        + [
            pltpu.VMEM((half, width), F32),
        ]
        + PlaneScatter.scratch(half, width),
        compiler_params=pltpu.CompilerParams(
            collective_id=4, has_side_effects=True, vmem_limit_bytes=VMEM
        ),
        cost_estimate=pl.CostEstimate(
            flops=16 * d.shape[0] * width * w.shape[1], bytes_accessed=d.shape[0] * width * 8, transcendentals=0
        ),
        name="project_back",
    )(d, w, gains, blocks)
    return own + from_x.astype(F32) + from_y.astype(F32), gains, blocks


def ffn_kernel(hidden_ref, grad_ref, gu_ref, down_ref, act_ref, dgu_ref):
    part = down_ref.shape[1]
    gate, up, act = gate_and_up(hidden_ref[...], gu_ref)
    d_gate, d_up = gate_and_up_back(gate, up, dot_nn(grad_ref[...], down_ref[...]))
    act_ref[...] = act
    dgu_ref[:, :part] = d_gate
    dgu_ref[:, part:] = d_up


def ffn_call(hidden, grad, gu, down):
    count, width = hidden.shape
    part = down.shape[1]
    block = 256
    return pl.pallas_call(
        ffn_kernel,
        grid=(count // block,),
        in_specs=[
            pl.BlockSpec((block, width), lambda i: (i, 0)),
            pl.BlockSpec((block, width), lambda i: (i, 0)),
            pl.BlockSpec(gu.shape, lambda i: (0, 0), pipeline_mode=pl.Buffered(1)),
            pl.BlockSpec(down.shape, lambda i: (0, 0), pipeline_mode=pl.Buffered(1)),
        ],
        out_specs=[
            pl.BlockSpec((block, part), lambda i: (i, 0)),
            pl.BlockSpec((block, 2 * part), lambda i: (i, 0)),
        ],
        out_shape=[
            jax.ShapeDtypeStruct((count, part), BF16),
            jax.ShapeDtypeStruct((count, 2 * part), BF16),
        ],
        compiler_params=pltpu.CompilerParams(vmem_limit_bytes=VMEM),
        name="ffn",
    )(hidden, grad, gu, down)


def all_to_all(block):
    return lax.all_to_all(block, "seq", 0, 0, tiled=True)


def gather_z(block):
    full = lax.all_gather(block, "rows", axis=1, tiled=True)
    return full.reshape(-1, full.shape[-1])


def scatter_z(grad):
    parts, lines, cols = grad.shape
    grad = lax.psum_scatter(
        grad.reshape(parts * lines, cols), "rows", scatter_dimension=0, tiled=True
    )
    return grad.reshape(lax.axis_size("seq"), -1, cols)


def shards(
    tokens,
    lengths,
    norm_gains,
    qk_gains,
    qkv_weight,
    out_weight,
    gate_up_weight,
    down_weight,
    cotangent,
):
    rows, slots, width = tokens.shape
    count = rows * slots
    seq = lax.axis_size("seq")
    group = QUERY_HEADS // seq
    query_width = group * HEAD
    sharing = seq // KEY_VALUE_HEADS
    total = seq * slots
    depth = qkv_weight.shape[0]
    kv_at = QUERY_HEADS * HEAD
    part = down_weight.shape[1] // seq
    me = lax.axis_index("seq").astype(jnp.int32)[None]
    gains = norm_gains.astype(F32)

    qkv_scaled = (qkv_weight.astype(F32) * gains[0][:, None]).astype(BF16)
    kv_scaled = qkv_scaled[:, kv_at:].reshape(depth, 2, KEY_VALUE_HEADS, HEAD)
    qkv_blocks = jnp.concatenate(
        [
            qkv_scaled[:, :kv_at].reshape(depth, seq, query_width),
            jnp.repeat(kv_scaled[:, 0], sharing, axis=1),
            jnp.repeat(kv_scaled[:, 1], sharing, axis=1),
        ],
        axis=2,
    ).transpose(1, 0, 2)
    qkv_mine = gather_z(all_to_all(qkv_blocks))
    out_block = lax.all_gather(out_weight, "rows", axis=0, tiled=True)
    gu_scaled = (gate_up_weight.astype(F32) * gains[1][:, None]).astype(BF16)
    gu_blocks = gu_scaled.reshape(depth, 2, seq, part).transpose(2, 0, 1, 3)
    gu_mine = gather_z(all_to_all(gu_blocks.reshape(seq, depth, 2 * part)))
    down_blocks = down_weight.reshape(depth, seq, part).transpose(1, 0, 2)

    lane = jnp.arange(128) % HEAD
    frequency = jnp.exp(
        -math.log(10000.0) * ((lane % (HEAD // 2)).astype(F32) * (2.0 / HEAD))
    )
    angles = jnp.arange(total).astype(F32)[:, None] * frequency[None, :]
    cos = jnp.cos(angles)
    sin = jnp.where(lane < HEAD // 2, -1.0, 1.0)[None, :] * jnp.sin(angles)
    qk = qk_gains.astype(F32)
    head_gains = jnp.concatenate([jnp.tile(qk[0], group), qk[1], jnp.ones((HEAD,), F32)])[None, :]

    inputs = tokens.reshape(count, width).astype(F32)
    r0 = lax.rsqrt(jnp.mean(inputs * inputs, axis=-1, keepdims=True) + EPSILON)
    unit0 = (inputs * r0).astype(BF16)
    if seq == 8:
        unit0, raw, q, kv = gather_qkv_call(unit0, qkv_mine, cos, sin, head_gains, rows, slots)
    else:
        unit0 = gather_plane(unit0)
        raw, q, kv = qkv_call(me, unit0, qkv_mine, cos, sin, head_gains, rows, slots)
    out_full = gather_natural(after(out_block, q))
    down_mine = gather_z(after(all_to_all(down_blocks), q))
    attended_mine, attended_low, logs = attend_call(lengths, q, kv, slots)
    attended = all_to_all(attended_low).transpose(1, 2, 0, 3).reshape(count, kv_at)
    middle = inputs + dot_nt(attended, out_full)
    r1 = lax.rsqrt(jnp.mean(middle * middle, axis=-1, keepdims=True) + EPSILON)

    grad_low = cotangent.reshape(count, width)
    unit1 = (middle * r1).astype(BF16)
    half = seq * count // 2
    if seq == 8:
        unit1, near, far, gate_up, act = gather_ffn_call(
            unit1, gather_pieces(grad_low, q), gu_mine
        )
        down_grad = weight_grad_call([near, far], act, corner(act), depth, "down_grad")
        u, d_gu = ffn_back_call(near, far, gate_up, gu_mine, down_mine, count, corner(down_grad))
    else:
        grad_all = gather_plane(grad_low)
        unit1 = gather_plane(unit1)
        act, d_gu = ffn_call(unit1, grad_all, gu_mine, down_mine)
        u_odd = dot_nt(d_gu[half:], gu_mine).astype(BF16)
        u = scatter_plane(u_odd, dot_nt(d_gu[:half], gu_mine))
        near, far = grad_all[:half], grad_all[half:]
        down_grad = weight_grad_call([near, far], act, corner(act), depth, "down_grad")
    down_sum = scatter_z(down_grad)

    d_middle = (
        grad_low.astype(F32)
        + r1 * u
        - middle * (r1 * r1 * r1) * jnp.mean(u * middle, axis=-1, keepdims=True)
    )
    d_branch = d_middle.astype(BF16)
    d_attended = dot_nn(d_branch, out_full).astype(BF16)
    branch_near, branch_far = branch_call(act, down_mine, corner(d_attended))
    if seq == 8:
        gu_grad, d_attended, down_sum = grad_exchange_call(
            unit1, d_gu, d_attended, down_sum, corner(branch_near), depth
        )
        d_attended = d_attended.reshape(seq, rows, slots, query_width)
    else:
        gu_grad = weight_grad_call([unit1], d_gu, corner(branch_near), depth, "gate_up_grad")
        d_attended = d_attended.reshape(rows, slots, seq, query_width).transpose(2, 0, 1, 3)
        d_attended = all_to_all(d_attended)
        down_sum = all_to_all(down_sum)
    gu_sum = scatter_z(gu_grad)
    features = width // seq
    out_near, out_far = out_grad_call(me, d_branch, attended, corner(gu_grad))
    chips = seq // 2
    branch_all = (branch_near.astype(F32) + swap(branch_far, 1).astype(F32)).astype(BF16)
    out_all = (out_near.astype(F32) + swap(out_far, 1).astype(F32)).astype(BF16)
    branch_parts = [branch_all[i * count : (i + 1) * count] for i in range(chips)]
    out_parts = [out_all[i * features : (i + 1) * features] for i in range(chips)]
    ready = after(lengths, gu_grad, *branch_parts, *out_parts)
    dq, dkv = attend_back_call(ready, q, kv, attended_mine, d_attended, logs)
    d_qkv, head_gain_grad = prepare_back_call(me, raw, dq, dkv, cos, sin, head_gains, slots)
    qkv_grad = weight_grad_call([unit0], d_qkv, corner(d_qkv), depth, "qkv_grad")
    branch = scatter_direct(branch_parts, d_qkv)
    output = (middle + branch).astype(BF16).reshape(rows, slots, width)
    out_sum = scatter_direct(out_parts, d_qkv)
    if seq == 8:
        gain_rows = after(head_gain_grad, qkv_grad, output, out_sum)
        gain_rows = jnp.broadcast_to(gain_rows, (8, gain_rows.shape[1]))
        u0, head_gain_grad, gu_owned = project_back_call(
            d_qkv, qkv_mine, gain_rows, gu_sum, count
        )
    else:
        u0_odd = dot_nt(d_qkv[half:], qkv_mine).astype(BF16)
        u0 = scatter_plane(u0_odd, dot_nt(d_qkv[:half], qkv_mine))
        head_gain_grad = sum_everywhere(head_gain_grad)
        gu_owned = all_to_all(gu_sum)
    parts = lax.axis_size("rows")
    out_blocks = after(out_sum, gu_sum).astype(BF16).reshape(parts, depth * seq, kv_at // seq)
    attn_sum = scatter_z(jnp.concatenate([qkv_grad, out_blocks], axis=2))
    qkv_sum = attn_sum[:, :, : query_width + 2 * HEAD]
    out_sum = attn_sum[:, :, query_width + 2 * HEAD :].reshape(depth, kv_at)
    input_grad = (
        d_middle + r0 * u0 - inputs * (r0 * r0 * r0) * jnp.mean(u0 * inputs, axis=-1, keepdims=True)
    )
    input_grad = input_grad.astype(BF16).reshape(rows, slots, width)
    qk_grad = jnp.stack(
        [head_gain_grad[0, :query_width].reshape(group, HEAD).sum(0), head_gain_grad[0, query_width : query_width + HEAD]]
    )

    gu_sum = gu_owned.reshape(seq, depth, 2, part).transpose(1, 2, 0, 3)
    gu_sum = gu_sum.reshape(depth, 2 * seq * part).astype(F32)
    down_sum = down_sum.transpose(1, 0, 2).reshape(depth, seq * part).astype(F32)
    qkv_sum = all_to_all(qkv_sum).transpose(1, 0, 2).astype(F32)
    kv_sum = qkv_sum[:, :, query_width:].reshape(depth, KEY_VALUE_HEADS, sharing, 2 * HEAD).sum(2)
    qkv_sum = jnp.concatenate(
        [
            qkv_sum[:, :, :query_width].reshape(depth, -1),
            kv_sum[:, :, :HEAD].reshape(depth, -1),
            kv_sum[:, :, HEAD:].reshape(depth, -1),
        ],
        axis=1,
    )
    norm_gain_grad = jnp.stack(
        [
            jnp.sum(qkv_weight.astype(F32) * qkv_sum, axis=1),
            jnp.sum(gate_up_weight.astype(F32) * gu_sum, axis=1),
        ]
    )
    return (
        output,
        input_grad,
        norm_gain_grad,
        qk_grad,
        qkv_sum * gains[0][:, None],
        out_sum.astype(F32),
        gu_sum * gains[1][:, None],
        down_sum,
    )


def solution(mesh):
    in_specs = (
        P("rows", "seq", None),
        P("rows"),
        P(None, ("seq", "rows")),
        P(),
        P(("seq", "rows"), None),
        P(("seq", "rows"), None),
        P(("seq", "rows"), None),
        P(("seq", "rows"), None),
        P("rows", "seq", None),
    )
    out_specs = (
        P("rows", "seq", None),
        P("rows", "seq", None),
        P(None, ("seq", "rows")),
        P(),
        P(("seq", "rows"), None),
        P(("seq", "rows"), None),
        P(("seq", "rows"), None),
        P(("seq", "rows"), None),
    )
    return jax.shard_map(shards, mesh=mesh, in_specs=in_specs, out_specs=out_specs, check_vma=False)
```

```python
from functools import partial
import math

import jax
import jax.numpy as jnp
from jax import lax
from jax.experimental import pallas as pl
from jax.experimental.pallas import tpu as pltpu
from jax.sharding import PartitionSpec as P

QUERY_HEADS = 32
KEY_VALUE_HEADS = 8
HEAD = 64
EPSILON = 1e-06
F32 = jnp.float32
BF16 = jnp.bfloat16
HIGHEST = lax.Precision.HIGHEST
SCALE = HEAD ** (-0.5)
SCALE2 = SCALE * math.log2(math.e)
VMEM = 56 * 1024 * 1024


def swap(block, mask):
    return lax.ppermute(block, "seq", [(i, i ^ mask) for i in range(lax.axis_size("seq"))])


def masks_between_chips():
    return [1 << bit for bit in range(1, lax.axis_size("seq").bit_length() - 1)]


def natural(place, me, seq):
    return me[0] ^ (2 * lax.rem(place, seq // 2) + lax.div(place, seq // 2))


def dot_nn(a, b):
    return jnp.dot(a, b, preferred_element_type=F32)


def dot_nt(a, b, precision=None):
    return lax.dot_general(
        a, b, (((1,), (1,)), ((), ())), preferred_element_type=F32, precision=precision
    )


def dot_tn(a, b):
    return lax.dot_general(a, b, (((0,), (0,)), ((), ())), preferred_element_type=F32)


def after(value, *results):
    zero = sum(result[(0,) * result.ndim].astype(F32) for result in results) * 0.0
    return value + zero.astype(value.dtype)


def gather_pieces(chunk, earlier):
    half = chunk.shape[0] // 2
    along_x, along_y = swap(chunk, 2), swap(chunk, 4)
    through_x, through_y = after(along_y[:half], earlier), after(along_x[half:], earlier)
    return [chunk, along_x, along_y, swap(through_x, 2), swap(through_y, 4)]


def gather_plane(chunk):
    own = [chunk]
    for mask in masks_between_chips():
        own = own + [swap(part, mask) for part in own]
    return jnp.concatenate(own + [swap(part, 1) for part in own], axis=0)


def gather_natural(block):
    seq, me, size = lax.axis_size("seq"), lax.axis_index("seq"), block.shape[0]
    parts = {mask: swap(block, mask) if mask > 0 else block for mask in range(0, seq, 2)}
    parts.update({mask + 1: swap(part, 1) for mask, part in list(parts.items())})
    whole = jnp.zeros((seq * size,) + block.shape[1:], block.dtype)
    for m, part in parts.items():
        whole = lax.dynamic_update_slice_in_dim(whole, part, (me ^ m) * size, 0)
    return whole


def scatter_chips(parts):
    if len(parts) == 4:
        mine, to_x, to_y, diagonal = parts
        half = mine.shape[0] // 2
        diagonal = diagonal.astype(BF16)
        from_x = swap(diagonal[:half], 2).astype(F32)
        from_y = swap(diagonal[half:], 4).astype(F32)
        to_x = jnp.concatenate([to_x[:half], to_x[half:] + from_y], axis=0).astype(BF16)
        to_y = jnp.concatenate([to_y[:half] + from_x, to_y[half:]], axis=0).astype(BF16)
        return mine + swap(to_x, 2).astype(F32) + swap(to_y, 4).astype(F32)
    for mask in reversed(masks_between_chips()):
        kept = len(parts) // 2
        parts = [
            parts[i] + swap(parts[kept + i].astype(BF16), mask).astype(F32) for i in range(kept)
        ]
    return parts[0]


def scatter_plane(odd, even, scatter=scatter_chips):
    count = 1 << len(masks_between_chips())
    size = even.shape[0] // count
    both = even + swap(odd, 1).astype(F32)
    return scatter([both[i * size : (i + 1) * size] for i in range(count)])


def sum_everywhere(value):
    for axis in ("seq", "rows"):
        size = lax.axis_size(axis)
        mask = 1
        while mask < size:
            value = value + lax.ppermute(value, axis, [(i, i ^ mask) for i in range(size)])
            mask *= 2
    return value


def lane_of(shape):
    return lax.broadcasted_iota(jnp.int32, shape, len(shape) - 1)


def swap_halves(v):
    first = lane_of(v.shape) % HEAD < HEAD // 2
    return jnp.where(first, pltpu.roll(v, 96, 1), pltpu.roll(v, 32, 1))


def head_mean(v):
    rows = lax.broadcasted_iota(jnp.int32, (128, 128), 0) // HEAD
    cols = lax.broadcasted_iota(jnp.int32, (128, 128), 1) // HEAD
    block = jnp.where(rows == cols, 1.0 / HEAD, 0.0).astype(F32)
    return jnp.dot(v, block, preferred_element_type=F32, precision=HIGHEST)


def qkv_kernel(me, x_ref, w_ref, cos_ref, sin_ref, gain_ref, raw_ref, q_ref, kv_ref):
    rows, slots = q_ref.shape[0], q_ref.shape[1]
    raw = dot_nn(x_ref[...], w_ref[...])
    cos, sin = cos_ref[...], sin_ref[...]
    keys = lane_of((slots, 128)) < HEAD
    for r in range(rows):
        part = raw[r * slots : (r + 1) * slots]
        raw_ref[r] = part
        last = part.shape[1] // 128 - 1
        for s in range(last + 1):
            v = part[:, s * 128 : (s + 1) * 128]
            out = normed_rotated(v, cos, sin, gain_ref[:, s * 128 : (s + 1) * 128])
            if s < last:
                q_ref[r, :, s * 128 : (s + 1) * 128] = out.astype(BF16)
            else:
                kv_ref[r] = jnp.where(keys, out, v).astype(BF16)


def qkv_call(me, x, w, cos, sin, gains, rows, slots):
    chunk = rows * slots
    width = w.shape[1]
    query_width = width - 128
    seq = x.shape[0] // chunk
    total = seq * slots
    return pl.pallas_call(
        qkv_kernel,
        grid_spec=pltpu.PrefetchScalarGridSpec(
            num_scalar_prefetch=1,
            grid=(seq,),
            in_specs=[
                pl.BlockSpec((chunk, x.shape[1]), lambda i, me: (i, 0)),
                pl.BlockSpec(w.shape, lambda i, me: (0, 0)),
                pl.BlockSpec((slots, 128), lambda i, me: (natural(i, me, seq), 0)),
                pl.BlockSpec((slots, 128), lambda i, me: (natural(i, me, seq), 0)),
                pl.BlockSpec((1, width), lambda i, me: (0, 0)),
            ],
            out_specs=[
                pl.BlockSpec((rows, slots, width), lambda i, me: (0, natural(i, me, seq), 0)),
                pl.BlockSpec((rows, slots, query_width), lambda i, me: (0, natural(i, me, seq), 0)),
                pl.BlockSpec((rows, slots, 128), lambda i, me: (0, natural(i, me, seq), 0)),
            ],
        ),
        out_shape=[
            jax.ShapeDtypeStruct((rows, total, width), F32),
            jax.ShapeDtypeStruct((rows, total, query_width), BF16),
            jax.ShapeDtypeStruct((rows, total, 128), BF16),
        ],
        compiler_params=pltpu.CompilerParams(vmem_limit_bytes=VMEM),
        name="qkv_prepare",
    )(me, x, w, cos, sin, gains)


def attend_kernel(lengths, q_ref, kv_ref, out_ref, low_ref, log_ref, k2, vo, acc):
    row, step = pl.program_id(0), pl.program_id(1)
    block = q_ref.shape[1]
    group = q_ref.shape[2] // HEAD
    length = lengths[row]

    @pl.when(step == 0)
    def _():
        kv = kv_ref[0].astype(F32)
        keys = lane_of(kv.shape) < HEAD
        k2[...] = jnp.where(keys, kv, pltpu.roll(kv, HEAD, 1)).astype(BF16)
        vo[...] = jnp.where(keys, 1.0, kv).astype(BF16)

    low_half = lane_of((block, 128)) < HEAD
    queries = []
    for h in range(group):
        part = q_ref[0, :, (h // 2) * 128 : (h // 2 + 1) * 128].astype(F32)
        kept = low_half if h % 2 == 0 else jnp.logical_not(low_half)
        queries.append(jnp.where(kept, part, 0.0).astype(BF16))
    acc[...] = jnp.zeros_like(acc)

    def one_block(at, masked):
        begin = pl.multiple_of(at * block, block)
        keys = k2[pl.ds(begin, block), :]
        values = vo[pl.ds(begin, block), :]
        if masked:
            key_place = begin + lax.broadcasted_iota(jnp.int32, (block, block), 1)
            query_place = step * block + lax.broadcasted_iota(jnp.int32, (block, block), 0)
            allowed = (key_place <= query_place) & (key_place < length)
        for h in range(group):
            weights = jnp.exp2(dot_nt(queries[h], keys) * SCALE2)
            if masked:
                weights = jnp.where(allowed, weights, 0.0)
            acc[h] += dot_nn(weights.astype(BF16), values)

    full = jnp.minimum(step, lax.div(length, block))

    def body(at, carry):
        one_block(at, False)
        return carry

    lax.fori_loop(0, full, body, 0)

    @pl.when(full * block < length)
    def _():
        one_block(full, True)

    for g in range(group // 2):
        even, odd = acc[2 * g], acc[2 * g + 1]
        even_turned, odd_turned = pltpu.roll(even, HEAD, 1), pltpu.roll(odd, HEAD, 1)
        mixed = jnp.where(low_half, even_turned / even, odd / odd_turned)
        out_ref[0, :, g * 128 : (g + 1) * 128] = mixed
        low_ref[0, 0, :, g * 128 : (g + 1) * 128] = mixed.astype(BF16)
        log_ref[0, 2 * g : 2 * g + 1, :] = jnp.log2(even.T[0:1, :])
        log_ref[0, 2 * g + 1 : 2 * g + 2, :] = jnp.log2(odd.T[0:1, :])
    log_ref[0, group:, :] = jnp.zeros((8 - group, block), F32)


def attend_call(lengths, q, kv, block):
    rows, total, width = q.shape
    seq = total // block
    return pl.pallas_call(
        attend_kernel,
        grid_spec=pltpu.PrefetchScalarGridSpec(
            num_scalar_prefetch=1,
            grid=(rows, seq),
            in_specs=[
                pl.BlockSpec((1, block, width), lambda r, i, n: (r, i, 0)),
                pl.BlockSpec((1, total, 128), lambda r, i, n: (r, 0, 0)),
            ],
            out_specs=[
                pl.BlockSpec((1, block, width), lambda r, i, n: (r, i, 0)),
                pl.BlockSpec((1, 1, block, width), lambda r, i, n: (i, r, 0, 0)),
                pl.BlockSpec((1, 8, block), lambda r, i, n: (r, 0, i)),
            ],
            scratch_shapes=[
                pltpu.VMEM((total, 128), BF16),
                pltpu.VMEM((total, 128), BF16),
                pltpu.VMEM((width // HEAD, block, 128), F32),
            ],
        ),
        out_shape=[
            jax.ShapeDtypeStruct((rows, total, width), F32),
            jax.ShapeDtypeStruct((seq, rows, block, width), BF16),
            jax.ShapeDtypeStruct((rows, 8, total), F32),
        ],
        compiler_params=pltpu.CompilerParams(vmem_limit_bytes=VMEM),
        cost_estimate=pl.CostEstimate(
            flops=rows * total * total * width * 16, bytes_accessed=rows * total * width * 8, transcendentals=0
        ),
        name="attend",
    )(lengths, q, kv)


def attend_back_kernel(
    lengths, q_ref, kv_ref, out_ref, grad_ref, log_ref, *refs
):
    dq_ref, dkv_ref, delta, dqt, kacc, vacc = refs[-6:]
    row, step = pl.program_id(0), pl.program_id(1)
    block = kv_ref.shape[1]
    count = q_ref.shape[1] // block
    width = q_ref.shape[2]
    group = width // HEAD
    length = lengths[row]

    @pl.when(step == 0)
    def _():
        dqt[...] = jnp.zeros_like(dqt)
        heads = lax.broadcasted_iota(jnp.int32, (8, width), 0)
        pick = jnp.where(lane_of((8, width)) // HEAD == heads, 1.0, 0.0).astype(F32)
        for i in range(count):
            product = grad_ref[i, 0].astype(F32) * out_ref[0, i * block : (i + 1) * block, :]
            delta[:, i * block : (i + 1) * block] = dot_nt(pick, product, HIGHEST)

    kacc[...] = jnp.zeros_like(kacc)
    vacc[...] = jnp.zeros_like(vacc)
    begin = step * block
    kv = kv_ref[0].astype(F32)
    turned = pltpu.roll(kv, HEAD, 1)
    low_half = lane_of((block, 128)) < HEAD
    keys = [
        jnp.where(low_half, kv, 0.0).astype(BF16),
        jnp.where(low_half, 0.0, turned).astype(BF16),
    ]
    values = [
        jnp.where(low_half, turned, 0.0).astype(BF16),
        jnp.where(low_half, 0.0, kv).astype(BF16),
    ]
    keys_turned = [
        jnp.where(low_half, kv, 0.0).T.astype(BF16),
        jnp.where(low_half, 0.0, turned).T.astype(BF16),
    ]

    def one_block(at, masked):
        first = pl.multiple_of(at * block, block)
        if masked:
            key_place = begin + lax.broadcasted_iota(jnp.int32, (block, block), 0)
            query_place = first + lax.broadcasted_iota(jnp.int32, (block, block), 1)
            allowed = (key_place <= query_place) & (key_place < length)
        for g in range(group // 2):
            queries = q_ref[0, pl.ds(first, block), g * 128 : (g + 1) * 128]
            grads = grad_ref[at, 0, :, g * 128 : (g + 1) * 128]
            turned_sum = None
            for side in range(2):
                h = 2 * g + side
                logs = log_ref[0, h : h + 1, pl.ds(first, block)]
                deltas = delta[h : h + 1, pl.ds(first, block)]
                weights = jnp.exp2(dot_nt(keys[side], queries) * SCALE2 - logs)
                if masked:
                    weights = jnp.where(allowed, weights, 0.0)
                d_weights = dot_nt(values[side], grads)
                d_scores = (weights * (d_weights - deltas)).astype(BF16)
                vacc[side] += dot_nn(weights.astype(BF16), grads)
                kacc[side] += dot_nn(d_scores, queries)
                term = dot_nn(keys_turned[side], d_scores)
                turned_sum = term if turned_sum is None else turned_sum + term
            dqt[g, :, pl.ds(first, block)] += turned_sum

    @pl.when(begin < length)
    def _():
        inside = begin + block <= length

        @pl.when(inside)
        def _():
            one_block(step, True)

            def body(at, carry):
                one_block(at, False)
                return carry

            lax.fori_loop(step + 1, count, body, 0)

        @pl.when(jnp.logical_not(inside))
        def _():
            def body(at, carry):
                one_block(at, True)
                return carry

            lax.fori_loop(step, count, body, 0)

    ksum = jnp.where(low_half, kacc[0], 0.0) + pltpu.roll(jnp.where(low_half, 0.0, kacc[1]), HEAD, 1)
    vsum = pltpu.roll(jnp.where(low_half, vacc[0], 0.0), HEAD, 1) + jnp.where(
        low_half, 0.0, vacc[1]
    )
    dkv_ref[0] = jnp.where(low_half, ksum * SCALE, vsum)

    @pl.when(step == count - 1)
    def _():
        for g in range(group // 2):
            for i in range(count):
                dq_ref[0, i * block : (i + 1) * block, g * 128 : (g + 1) * 128] = (
                    dqt[g, :, i * block : (i + 1) * block].T * SCALE
                )


def attend_back_call(lengths, q, kv, attended, grads, logs, earlier):
    rows, total, width = q.shape
    seq, block = grads.shape[0], grads.shape[2]
    return pl.pallas_call(
        attend_back_kernel,
        grid_spec=pltpu.PrefetchScalarGridSpec(
            num_scalar_prefetch=1,
            grid=(rows, seq),
            in_specs=[
                pl.BlockSpec((1, total, width), lambda r, i, n: (r, 0, 0)),
                pl.BlockSpec((1, block, 128), lambda r, i, n: (r, i, 0)),
                pl.BlockSpec((1, total, width), lambda r, i, n: (r, 0, 0)),
                pl.BlockSpec((seq, 1, block, width), lambda r, i, n: (0, r, 0, 0)),
                pl.BlockSpec((1, 8, total), lambda r, i, n: (r, 0, 0)),
            ]
            + [pl.BlockSpec(memory_space=pl.ANY)] * len(earlier),
            out_specs=[
                pl.BlockSpec((1, total, width), lambda r, i, n: (r, 0, 0)),
                pl.BlockSpec((1, block, 128), lambda r, i, n: (r, i, 0)),
            ],
            scratch_shapes=[
                pltpu.VMEM((8, total), F32),
                pltpu.VMEM((width // 128, 128, total), F32),
                pltpu.VMEM((2, block, 128), F32),
                pltpu.VMEM((2, block, 128), F32),
            ],
        ),
        out_shape=[
            jax.ShapeDtypeStruct((rows, total, width), F32),
            jax.ShapeDtypeStruct((rows, total, 128), F32),
        ],
        compiler_params=pltpu.CompilerParams(vmem_limit_bytes=VMEM),
        cost_estimate=pl.CostEstimate(
            flops=rows * total * total * width * 28, bytes_accessed=rows * total * width * 14, transcendentals=0
        ),
        name="attend_back",
    )(lengths, q, kv, attended, grads, logs, *earlier)


def prepare_back_kernel(
    me, raw_ref, dq_ref, dkv_ref, cos_ref, sin_ref, gain_ref, _, out_ref, gain_grad_ref
):
    rows, slots = dq_ref.shape[0], dq_ref.shape[1]
    cos, sin = cos_ref[...], sin_ref[...]
    keys = lane_of((slots, 128)) < HEAD
    last = raw_ref.shape[2] // 128 - 1

    @pl.when(pl.program_id(0) == 0)
    def _():
        gain_grad_ref[...] = jnp.zeros_like(gain_grad_ref)

    for r in range(rows):
        for s in range(last + 1):
            lanes = slice(s * 128, (s + 1) * 128)
            raw = raw_ref[r, :, lanes]
            grad = dq_ref[r, :, lanes] if s < last else dkv_ref[r]
            gain = gain_ref[:, lanes]
            turned = grad * cos + swap_halves(grad * sin)
            factor = lax.rsqrt(head_mean(raw * raw) + EPSILON)
            gain_grad_ref[:, lanes] += jnp.sum(turned * raw * factor, axis=0, keepdims=True)
            u = turned * gain
            mean = head_mean(u * raw)
            result = factor * u - raw * (factor * factor * factor) * mean
            if s == last:
                result = jnp.where(keys, result, grad)
            out_ref[r * slots : (r + 1) * slots, lanes] = result.astype(BF16)


def prepare_back_call(me, raw, dq, dkv, cos, sin, gains, slots, earlier):
    rows, total, width = raw.shape
    seq = total // slots
    return pl.pallas_call(
        prepare_back_kernel,
        grid_spec=pltpu.PrefetchScalarGridSpec(
            num_scalar_prefetch=1,
            grid=(seq,),
            in_specs=[
                pl.BlockSpec((rows, slots, width), lambda i, me: (0, natural(i, me, seq), 0)),
                pl.BlockSpec((rows, slots, width - 128), lambda i, me: (0, natural(i, me, seq), 0)),
                pl.BlockSpec((rows, slots, 128), lambda i, me: (0, natural(i, me, seq), 0)),
                pl.BlockSpec((slots, 128), lambda i, me: (natural(i, me, seq), 0)),
                pl.BlockSpec((slots, 128), lambda i, me: (natural(i, me, seq), 0)),
                pl.BlockSpec((1, width), lambda i, me: (0, 0)),
                pl.BlockSpec(memory_space=pl.ANY),
            ],
            out_specs=[
                pl.BlockSpec((rows * slots, width), lambda i, me: (i, 0)),
                pl.BlockSpec((1, width), lambda i, me: (0, 0)),
            ],
        ),
        out_shape=[
            jax.ShapeDtypeStruct((rows * total, width), BF16),
            jax.ShapeDtypeStruct((1, width), F32),
        ],
        compiler_params=pltpu.CompilerParams(vmem_limit_bytes=VMEM),
        name="prepare_back",
    )(me, raw, dq, dkv, cos, sin, gains, earlier)


def neighbours(me):
    return {
        "core": me + 1 - 2 * lax.rem(me, 2),
        "x": me + 2 - 4 * lax.rem(lax.div(me, 2), 2),
        "y": me + 4 - 8 * lax.div(me, 4),
    }


def remote(source, target, device, send, recv):
    return pltpu.make_async_remote_copy(
        src_ref=source,
        dst_ref=target,
        send_sem=send,
        recv_sem=recv,
        device_id=device,
        device_id_type=pl.DeviceIdType.MESH,
    )


def greet(devices):
    barrier = pltpu.get_barrier_semaphore()
    for device in devices:
        pl.semaphore_signal(barrier, inc=1, device_id=device, device_id_type=pl.DeviceIdType.MESH)
    pl.semaphore_wait(barrier, len(devices))


def greet_neighbours(to, rows):
    greet([(to[device], rows) for device in ("core", "x", "y")])


def flipped(index, mask, size):
    result, bit = index, 1
    while bit < size:
        if mask & bit:
            result = result + bit - 2 * bit * lax.rem(lax.div(index, bit), 2)
        bit *= 2
    return result


class PlaneExchange:
    def __init__(self, block, target, send, recv, local):
        self.seq, self.rows = lax.axis_index("seq"), lax.axis_index("rows")
        self.size = lax.axis_size("seq")
        self.block, self.target, self.send, self.recv, self.local = block, target, send, recv, local

    @staticmethod
    def scratch():
        others = lax.axis_size("seq") - 1
        return [
            pltpu.SemaphoreType.DMA((others,)),
            pltpu.SemaphoreType.DMA((others,)),
            pltpu.SemaphoreType.DMA,
        ]

    def peers(self):
        return [(flipped(self.seq, mask, self.size), self.rows) for mask in range(1, self.size)]

    def copies(self):
        remotes = [
            remote(self.block(peer[0]), self.target.at[self.seq], peer, self.send.at[i], self.recv.at[i])
            for i, peer in enumerate(self.peers())
        ]
        own = pltpu.make_async_copy(self.block(self.seq), self.target.at[self.seq], self.local)
        return remotes, own

    def start(self):
        remotes, own = self.copies()
        for copy in remotes:
            copy.start()
        own.start()

    def finish(self):
        remotes, own = self.copies()
        for copy in remotes:
            copy.wait()
        own.wait()


class PlaneGather:
    COPIES = 14

    def __init__(self, own, whole, send, recv):
        self.seq, self.rows = lax.axis_index("seq"), lax.axis_index("rows")
        self.half = own.shape[0] // 2
        self.own, self.whole, self.send, self.recv = own, whole, send, recv
        self.to = neighbours(self.seq)

    def place(self, at, half):
        return pl.ds((2 * at + half) * self.half, self.half)

    def copy(self, i):
        half, own, whole = self.half, self.own, self.whole
        first, second = own.at[pl.ds(0, half)], own.at[pl.ds(half, half)]

        def moved(at, h, to):
            return whole.at[self.place(at, h)], whole.at[self.place(to, h)]

        source, target, device = (
            (second, whole.at[self.place(1, 1)], "x"),
            (first, whole.at[self.place(2, 0)], "y"),
            (first, whole.at[self.place(1, 0)], "x"),
            (second, whole.at[self.place(2, 1)], "y"),
            (first, whole.at[self.place(4, 0)], "core"),
            (second, whole.at[self.place(4, 1)], "core"),
            moved(1, 1, 3) + ("y",),
            moved(2, 0, 3) + ("x",),
            moved(1, 1, 5) + ("core",),
            moved(2, 0, 6) + ("core",),
            moved(1, 0, 5) + ("core",),
            moved(2, 1, 6) + ("core",),
            moved(3, 0, 7) + ("core",),
            moved(3, 1, 7) + ("core",),
        )[i]
        return remote(
            source, target, (self.to[device], self.rows), self.send.at[i], self.recv.at[i]
        )

    def fetch(self, unit, target, sem):
        begin = pl.multiple_of(unit_place(unit) * self.half, self.half)
        return pltpu.make_async_copy(self.whole.at[pl.ds(begin, self.half)], target, sem)

    def start_fetch(self, unit, target, sem):
        @pl.when(unit < 2)
        def _():
            begin = pl.multiple_of(lax.rem(unit, 2) * self.half, self.half)
            pltpu.make_async_copy(self.own.at[pl.ds(begin, self.half)], target, sem).start()

        @pl.when(unit >= 2)
        def _():
            self.fetch(unit, target, sem).start()

    def keep(self, unit, source, sem):
        begin = pl.multiple_of(lax.rem(unit, 2) * self.half, self.half)
        return pltpu.make_async_copy(source, self.whole.at[pl.ds(begin, self.half)], sem)

    def start(self):
        for i in (0, 1, 2, 3, 4, 5):
            self.copy(i).start()

    def open_group(self, group):
        if group == 1:
            self.copy(0).wait_recv()
            self.copy(6).start()
            self.copy(8).start()
            self.copy(1).wait_recv()
            self.copy(7).start()
            self.copy(9).start()
        if group == 2:
            self.copy(2).wait_recv()
            self.copy(10).start()
            self.copy(3).wait_recv()
            self.copy(11).start()
        if group == 3:
            self.copy(7).wait_recv()
            self.copy(12).start()
            self.copy(6).wait_recv()
            self.copy(13).start()

    def open_second(self, group):
        for i in ((4, 5), (8, 9), (10, 11), (12, 13))[group]:
            self.copy(i).wait_recv()

    def finish(self):
        for i in range(self.COPIES):
            self.copy(i).wait_send()


def unit_place(unit):
    group, k = lax.div(unit, 4), lax.rem(unit, 4)
    odd, late = lax.rem(group, 2), lax.div(group, 2)
    base = 3 * odd + 2 * late + odd * late
    stride = 1 + 2 * late * (1 - odd)
    return 8 * lax.div(k, 2) + base + stride * lax.rem(k, 2)


def at_unit(unit, value, action):
    @pl.when(unit == value)
    def _():
        action()


def normed_rotated(raw, cos, sin, gain):
    factor = lax.rsqrt(head_mean(raw * raw) + EPSILON)
    n = raw * factor * gain
    return n * cos + swap_halves(n) * sin


def gather_qkv_kernel(
    x_ref, w_ref, cos_ref, sin_ref, gain_ref, whole, raw_ref, q_ref, kv_ref,
    xbuf, rawbuf, qbuf, kvbuf, load, store, keep, send, recv,
):
    gather = PlaneGather(x_ref, whole, send, recv)
    half = gather.half
    me = gather.seq
    last = w_ref.shape[1] // 128 - 1
    greet_neighbours(gather.to, gather.rows)
    gather.start()

    def stores(unit, slot):
        place = unit_place(unit)
        at, row = lax.rem(lax.div(place, 2), 4), lax.rem(place, 2)
        core = lax.rem(lax.rem(me, 2) + lax.div(place, 8), 2)
        x = lax.rem(lax.div(me, 2) + at, 2)
        y = lax.rem(lax.div(me, 4) + lax.div(at, 2), 2)
        block = core + 2 * x + 4 * y
        begin = pl.ds(pl.multiple_of(block * half, half), half)
        return [
            pltpu.make_async_copy(rawbuf.at[slot], raw_ref.at[row, begin], store.at[0, slot]),
            pltpu.make_async_copy(qbuf.at[slot], q_ref.at[row, begin], store.at[1, slot]),
            pltpu.make_async_copy(kvbuf.at[slot], kv_ref.at[row, begin], store.at[2, slot]),
        ], block

    def body(unit, carry):
        slot = lax.rem(unit, 2)
        for group in range(4):
            at_unit(unit, 4 * group, partial(gather.open_group, group))
            at_unit(unit, 4 * group + 1, partial(gather.open_second, group))

        @pl.when(lax.rem(unit, 4) == 0)
        def _():
            gather.start_fetch(unit, xbuf.at[slot], load.at[slot])

        gather.fetch(unit, xbuf.at[slot], load.at[slot]).wait()

        @pl.when(unit < 2)
        def _():
            gather.keep(unit, xbuf.at[slot], keep.at[slot]).start()

        @pl.when((unit == 1) | (unit == 2))
        def _():
            gather.keep(unit - 1, xbuf.at[1 - slot], keep.at[1 - slot]).wait()

        @pl.when(lax.rem(unit, 4) != 3)
        def _():
            gather.start_fetch(unit + 1, xbuf.at[1 - slot], load.at[1 - slot])

        copies, block = stores(unit, slot)

        @pl.when(unit >= 2)
        def _():
            for copy in stores(unit - 2, slot)[0]:
                copy.wait()

        raw = dot_nn(xbuf[slot], w_ref[...])
        rawbuf[slot] = raw
        turn = pl.ds(pl.multiple_of(block * half, half), half)
        cos, sin = cos_ref[turn, :], sin_ref[turn, :]
        for s in range(last + 1):
            lanes = slice(s * 128, (s + 1) * 128)
            v = raw[:, lanes]
            out = normed_rotated(v, cos, sin, gain_ref[:, lanes])
            if s < last:
                qbuf[slot, :, lanes] = out.astype(BF16)
            else:
                kvbuf[slot] = jnp.where(lane_of(v.shape) < HEAD, out, v).astype(BF16)
        for copy in copies:
            copy.start()
        return carry

    lax.fori_loop(0, 16, body, 0)
    for slot in range(2):
        for copy in stores(14 + slot, slot)[0]:
            copy.wait()
    gather.finish()


def gather_qkv_call(x, w, cos, sin, gains, rows, slots):
    count, width = x.shape
    seq = lax.axis_size("seq")
    total = seq * slots
    cols = w.shape[1]
    here, there = pl.BlockSpec(memory_space=pltpu.VMEM), pl.BlockSpec(memory_space=pl.ANY)
    return pl.pallas_call(
        gather_qkv_kernel,
        in_specs=[there, here, here, here, here],
        out_specs=[there] * 4,
        out_shape=[
            jax.ShapeDtypeStruct((seq * count, width), BF16),
            jax.ShapeDtypeStruct((rows, total, cols), F32),
            jax.ShapeDtypeStruct((rows, total, cols - 128), BF16),
            jax.ShapeDtypeStruct((rows, total, 128), BF16),
        ],
        scratch_shapes=[
            pltpu.VMEM((2, slots, width), BF16),
            pltpu.VMEM((2, slots, cols), F32),
            pltpu.VMEM((2, slots, cols - 128), BF16),
            pltpu.VMEM((2, slots, 128), BF16),
            pltpu.SemaphoreType.DMA((2,)),
            pltpu.SemaphoreType.DMA((3, 2)),
            pltpu.SemaphoreType.DMA((2,)),
            pltpu.SemaphoreType.DMA((PlaneGather.COPIES,)),
            pltpu.SemaphoreType.DMA((PlaneGather.COPIES,)),
        ],
        compiler_params=pltpu.CompilerParams(
            collective_id=1, has_side_effects=True, vmem_limit_bytes=VMEM
        ),
        cost_estimate=pl.CostEstimate(
            flops=2 * seq * count * width * cols * 8, bytes_accessed=seq * count * width * 4, transcendentals=0
        ),
        name="gather_qkv",
    )(x, w, cos, sin, gains)


class PlaneScatter:
    def __init__(self, own, from_x, from_y, odd, even, held, other, diagonal, sems):
        self.seq, self.rows = lax.axis_index("seq"), lax.axis_index("rows")
        self.to = neighbours(self.seq)
        self.half = odd.shape[1]
        self.own, self.from_x, self.from_y = own, from_x, from_y
        self.odd, self.even, self.held, self.other, self.diagonal = odd, even, held, other, diagonal
        self.odd_send, self.odd_recv, self.send, self.recv, self.store = sems

    @staticmethod
    def scratch(half, width):
        return [
            pltpu.VMEM((2, half, width), BF16),
            pltpu.VMEM((6, half, width), BF16),
            pltpu.VMEM((2, half, width), F32),
            pltpu.VMEM((8, half, width), BF16),
            pltpu.VMEM((2, half, width), BF16),
            pltpu.SemaphoreType.DMA((2,)),
            pltpu.SemaphoreType.DMA((8,)),
            pltpu.SemaphoreType.DMA((6,)),
            pltpu.SemaphoreType.DMA((6,)),
            pltpu.SemaphoreType.DMA((2,)),
        ]

    @staticmethod
    def place(pair):
        two, b = lax.div(pair, 2), lax.rem(pair, 2)
        odd, late = lax.rem(two, 2), lax.div(two, 2)
        base = 6 * (1 - odd) * (1 - late) + 2 * odd * (1 - late) + 3 * (1 - odd) * late
        return base + b * (1 + 2 * odd * (1 - late))

    def hand_over(self, pair):
        slot = lax.rem(pair, 2)
        return remote(
            self.odd.at[slot],
            self.other.at[pair],
            (self.to["core"], self.rows),
            self.odd_send.at[slot],
            self.odd_recv.at[pair],
        )

    def copy(self, i):
        first, second = pl.ds(0, self.half), pl.ds(self.half, self.half)
        target, device = (
            (self.diagonal.at[0], "x"),
            (self.diagonal.at[1], "y"),
            (self.from_x.at[first], "x"),
            (self.from_y.at[second], "y"),
            (self.from_x.at[second], "x"),
            (self.from_y.at[first], "y"),
        )[i]
        return remote(
            self.even.at[i], target, (self.to[device], self.rows), self.send.at[i], self.recv.at[i]
        )

    def keep(self, i):
        return pltpu.make_async_copy(
            self.held.at[i], self.own.at[pl.ds(i * self.half, self.half)], self.store.at[i]
        )

    def give_odd(self, pair, value):
        @pl.when(pair >= 2)
        def _():
            self.hand_over(pair - 2).wait_send()

        self.odd[lax.rem(pair, 2)] = value.astype(BF16)
        self.hand_over(pair).start()

    def give_even(self, pair, value_ref):
        self.hand_over(pair).wait_recv()
        for at, i in ((0, 0), (1, 1), (2, 2), (3, 3), (4, 4), (5, 5)):

            @pl.when(pair == at)
            def _(at=at, i=i):
                total = value_ref[...] + self.other[at].astype(F32)
                if i >= 4:
                    self.copy(5 - i).wait_recv()
                    total = total + self.diagonal[5 - i].astype(F32)
                self.even[i] = total.astype(BF16)
                self.copy(i).start()

        for at, i in ((6, 0), (7, 1)):

            @pl.when(pair == at)
            def _(at=at, i=i):
                self.held[i] = value_ref[...] + self.other[at].astype(F32)
                self.keep(i).start()

    def finish(self):
        for pair in (6, 7):
            self.hand_over(pair).wait_send()
        for i in range(6):
            self.copy(i).wait_send()
        for i in (2, 3, 4, 5):
            self.copy(i).wait_recv()
        for i in range(2):
            self.keep(i).wait()


def gate_and_up(hidden, gu_ref):
    part = gu_ref.shape[1] // 2
    gate = dot_nn(hidden, gu_ref[:, :part])
    up = dot_nn(hidden, gu_ref[:, part:])
    return gate, up, (gate / (1.0 + jnp.exp(-gate)) * up).astype(BF16)


def gate_and_up_back(gate, up, d_act):
    sigmoid = 1.0 / (1.0 + jnp.exp(-gate))
    silu = gate * sigmoid
    d_gate = d_act * up * (sigmoid + silu * (1.0 - sigmoid))
    return d_gate.astype(BF16), (d_act * silu).astype(BF16)


def gather_ffn_kernel(
    x_ref, c0_ref, cx_ref, cy_ref, cd0_ref, cd1_ref, gu_hbm,
    whole, near_ref, far_ref, gate_up_ref, act_ref,
    gu, hbuf, cbuf, gbuf, abuf, weight_sem, load, store, keep, send, recv, piece_send, piece_recv,
):
    gather = PlaneGather(x_ref, whole, send, recv)
    half = gather.half
    part = gu.shape[1] // 2
    weights = pltpu.make_async_copy(gu_hbm, gu, weight_sem)
    weights.start()
    greet_neighbours(gather.to, gather.rows)
    gather.start()

    def stores(unit, slot):
        begin = pl.ds(pl.multiple_of(unit_place(unit) * half, half), half)
        return [
            pltpu.make_async_copy(abuf.at[slot], act_ref.at[begin], store.at[0, slot]),
            pltpu.make_async_copy(gbuf.at[slot], gate_up_ref.at[begin], store.at[1, slot]),
        ]

    piece_refs = (c0_ref, cx_ref, cy_ref, cd0_ref, cd1_ref)
    piece_at = ((0, 2), (2, 2), (4, 2), (6, 1), (7, 1))

    def piece(i):
        begin, size = piece_at[i]
        target = far_ref.at[pl.ds(begin * half, size * half)]
        return remote(
            piece_refs[i],
            target,
            (gather.to["core"], gather.rows),
            piece_send.at[i],
            piece_recv.at[i],
        )

    for i in range(5):
        piece(i).start()

    def passing(at):
        i = (0, 0, 1, 1, 2, 2, 3, 4)[at]
        source = piece_refs[i].at[pl.ds((at - piece_at[i][0]) * half, half)]
        return (
            pltpu.make_async_copy(source, cbuf.at[at % 2], keep.at[1, 0]),
            pltpu.make_async_copy(
                cbuf.at[at % 2], near_ref.at[pl.ds(at * half, half)], keep.at[1, 1]
            ),
        )

    def read_piece(at):
        passing(at)[0].start()

    def write_piece(at):
        passing(at)[0].wait()
        passing(at)[1].start()

    def end_piece(at):
        passing(at)[1].wait()

    def body(unit, carry):
        slot = lax.rem(unit, 2)
        for at in range(8):
            at_unit(unit, 2 * at, partial(read_piece, at))
            at_unit(unit, 2 * at + 1, partial(write_piece, at))
            if at < 7:
                at_unit(unit, 2 * at + 2, partial(end_piece, at))
        for group in range(4):
            at_unit(unit, 4 * group, partial(gather.open_group, group))
            at_unit(unit, 4 * group + 1, partial(gather.open_second, group))

        @pl.when(lax.rem(unit, 4) == 0)
        def _():
            gather.start_fetch(unit, hbuf.at[slot], load.at[slot])

        at_unit(unit, 0, weights.wait)
        gather.fetch(unit, hbuf.at[slot], load.at[slot]).wait()

        @pl.when(unit < 2)
        def _():
            gather.keep(unit, hbuf.at[slot], keep.at[0, slot]).start()

        @pl.when((unit == 1) | (unit == 2))
        def _():
            gather.keep(unit - 1, hbuf.at[1 - slot], keep.at[0, 1 - slot]).wait()

        @pl.when(lax.rem(unit, 4) != 3)
        def _():
            gather.start_fetch(unit + 1, hbuf.at[1 - slot], load.at[1 - slot])

        @pl.when(unit >= 2)
        def _():
            for copy in stores(unit - 2, slot):
                copy.wait()

        gate, up, act = gate_and_up(hbuf[slot], gu)
        abuf[slot] = act
        gbuf[slot, :, :part] = gate.astype(BF16)
        gbuf[slot, :, part:] = up.astype(BF16)
        for copy in stores(unit, slot):
            copy.start()
        return carry

    lax.fori_loop(0, 16, body, 0)
    for slot in range(2):
        for copy in stores(14 + slot, slot):
            copy.wait()
    end_piece(7)
    for i in range(5):
        piece(i).wait_recv()
        piece(i).wait_send()
    gather.finish()


def gather_ffn_call(x, pieces, gu):
    count, width = x.shape
    seq = lax.axis_size("seq")
    cols = gu.shape[1]
    half = count // 2
    there = pl.BlockSpec(memory_space=pl.ANY)
    return pl.pallas_call(
        gather_ffn_kernel,
        in_specs=[there] * 7,
        out_specs=[there] * 5,
        out_shape=[
            jax.ShapeDtypeStruct((seq * count, width), BF16),
            jax.ShapeDtypeStruct((seq * half, width), BF16),
            jax.ShapeDtypeStruct((seq * half, width), BF16),
            jax.ShapeDtypeStruct((seq * count, cols), BF16),
            jax.ShapeDtypeStruct((seq * count, cols // 2), BF16),
        ],
        scratch_shapes=[
            pltpu.VMEM(gu.shape, BF16),
            pltpu.VMEM((2, half, width), BF16),
            pltpu.VMEM((2, half, width), BF16),
            pltpu.VMEM((2, half, cols), BF16),
            pltpu.VMEM((2, half, cols // 2), BF16),
            pltpu.SemaphoreType.DMA,
            pltpu.SemaphoreType.DMA((2,)),
            pltpu.SemaphoreType.DMA((2, 2)),
            pltpu.SemaphoreType.DMA((2, 2)),
            pltpu.SemaphoreType.DMA((PlaneGather.COPIES,)),
            pltpu.SemaphoreType.DMA((PlaneGather.COPIES,)),
            pltpu.SemaphoreType.DMA((5,)),
            pltpu.SemaphoreType.DMA((5,)),
        ],
        compiler_params=pltpu.CompilerParams(
            collective_id=2, has_side_effects=True, vmem_limit_bytes=VMEM
        ),
        cost_estimate=pl.CostEstimate(
            flops=4 * seq * count * width * cols, bytes_accessed=seq * count * width * 8, transcendentals=0
        ),
        name="gather_ffn",
    )(x, *pieces, gu)


def ffn_back_kernel(
    near_ref, far_ref, gate_up_ref, gu_hbm, down_hbm, _, own, from_x, from_y, dgu_ref,
    gu, down, cbuf, gbuf, dbuf, total, odd, even, held, other, diagonal,
    odd_send, odd_recv, send, recv, keep, weight_sem, load, store,
):
    scatter = PlaneScatter(
        own, from_x, from_y, odd, even, held, other, diagonal, (odd_send, odd_recv, send, recv, keep)
    )
    half = scatter.half
    part = down.shape[1]
    weights = [
        pltpu.make_async_copy(down_hbm, down, weight_sem.at[0]),
        pltpu.make_async_copy(gu_hbm, gu, weight_sem.at[1]),
    ]
    for copy in weights:
        copy.start()

    def row_of(unit, whole):
        side = 8 * (1 - lax.rem(unit, 2)) if whole else 0
        place = PlaneScatter.place(lax.div(unit, 2)) + side
        return pl.ds(pl.multiple_of(place * half, half), half)

    def fetch(unit, slot):
        return [
            pltpu.make_async_copy(near_ref.at[row_of(unit, False)], cbuf.at[slot], load.at[0, slot]),
            pltpu.make_async_copy(
                gate_up_ref.at[row_of(unit, True)], gbuf.at[slot], load.at[1, slot]
            ),
        ]

    def start_fetch(unit, slot):
        near, gates = fetch(unit, slot)
        gates.start()

        @pl.when(lax.rem(unit, 2) == 0)
        def _():
            pltpu.make_async_copy(
                far_ref.at[row_of(unit, False)], cbuf.at[slot], load.at[0, slot]
            ).start()

        @pl.when(lax.rem(unit, 2) == 1)
        def _():
            near.start()

    def stores(unit, slot):
        return pltpu.make_async_copy(dbuf.at[slot], dgu_ref.at[row_of(unit, True)], store.at[slot])

    start_fetch(0, 0)
    greet_neighbours(scatter.to, scatter.rows)

    def body(unit, carry):
        slot = lax.rem(unit, 2)
        pair = lax.div(unit, 2)
        at_unit(unit, 0, weights[0].wait)
        for copy in fetch(unit, slot):
            copy.wait()

        @pl.when(unit < 15)
        def _():
            start_fetch(unit + 1, 1 - slot)

        @pl.when(unit >= 2)
        def _():
            stores(unit - 2, slot).wait()

        d_act = dot_nn(cbuf[slot], down[...])
        gate, up = gbuf[slot, :, :part].astype(F32), gbuf[slot, :, part:].astype(F32)
        d_gate, d_up = gate_and_up_back(gate, up, d_act)
        dbuf[slot, :, :part] = d_gate
        dbuf[slot, :, part:] = d_up
        stores(unit, slot).start()
        at_unit(unit, 0, weights[1].wait)
        total[...] = dot_nt(dbuf[slot], gu[...])

        @pl.when(slot == 0)
        def _():
            scatter.give_odd(pair, total[...])

        @pl.when(slot == 1)
        def _():
            scatter.give_even(pair, total)

        return carry

    lax.fori_loop(0, 16, body, 0)
    for slot in range(2):
        stores(14 + slot, slot).wait()
    scatter.finish()


def weight_grad_kernel(*refs):
    lefts, right_ref, out_ref = refs[:-3], refs[-3], refs[-1]
    depth = out_ref.shape[1]
    size = right_ref.shape[0] // len(lefts)
    grad = None
    for i, left in enumerate(lefts):
        term = dot_tn(left[...], right_ref[i * size : (i + 1) * size, :])
        grad = term if grad is None else grad + term
    for z in range(out_ref.shape[0]):
        out_ref[z] = grad[z * depth : (z + 1) * depth].astype(BF16)


def weight_grad_call(lefts, right, earlier, depth, name):
    seq, parts = lax.axis_size("seq"), lax.axis_size("rows")
    width = lefts[0].shape[1]
    block = width // seq
    tokens, cols = right.shape
    return pl.pallas_call(
        weight_grad_kernel,
        grid=(seq,),
        in_specs=[pl.BlockSpec((left.shape[0], block), lambda i: (0, i)) for left in lefts]
        + [
            pl.BlockSpec(right.shape, lambda i: (0, 0), pipeline_mode=pl.Buffered(1)),
            pl.BlockSpec(memory_space=pl.ANY),
        ],
        out_specs=pl.BlockSpec((parts, depth, cols), lambda i: (0, i, 0)),
        out_shape=jax.ShapeDtypeStruct((parts, seq * depth, cols), BF16),
        compiler_params=pltpu.CompilerParams(vmem_limit_bytes=VMEM),
        cost_estimate=pl.CostEstimate(
            flops=2 * tokens * width * cols,
            bytes_accessed=2 * tokens * (width + cols),
            transcendentals=0,
        ),
        name=name,
    )(*lefts, right, earlier)


def grad_send_kernel(
    left_ref, right_ref, to_x, to_y, out_ref, from_x, from_y, send, recv
):
    seq, rows = lax.axis_index("seq"), lax.axis_index("rows")
    to = neighbours(seq)
    lines = pl.ds(0, from_x.shape[0])
    copies = [
        remote(source.at[lines], target, (to[device], rows), send.at[i], recv.at[i])
        for i, (source, target, device) in enumerate(((to_x, from_x, "x"), (to_y, from_y, "y")))
    ]

    @pl.when(pl.program_id(0) == 0)
    def _():
        greet([(to["x"], rows), (to["y"], rows)])
        for copy in copies:
            copy.start()

    depth = out_ref.shape[1]
    grad = dot_tn(left_ref[...], right_ref[...])
    for z in range(out_ref.shape[0]):
        out_ref[z] = grad[z * depth : (z + 1) * depth].astype(BF16)

    @pl.when(pl.program_id(0) == pl.num_programs(0) - 1)
    def _():
        for copy in copies:
            copy.wait()


def grad_send_call(left, right, to_x, to_y, count, depth):
    seq, parts = lax.axis_size("seq"), lax.axis_size("rows")
    tokens, cols = right.shape
    width = left.shape[1]
    there = pl.BlockSpec(memory_space=pl.ANY)
    lines = jax.ShapeDtypeStruct((count, to_x.shape[1]), BF16)
    return pl.pallas_call(
        grad_send_kernel,
        grid=(seq,),
        in_specs=[
            pl.BlockSpec((tokens, width // seq), lambda i: (0, i)),
            pl.BlockSpec(right.shape, lambda i: (0, 0), pipeline_mode=pl.Buffered(1)),
            there,
            there,
        ],
        out_specs=[pl.BlockSpec((parts, depth, cols), lambda i: (0, i, 0)), there, there],
        out_shape=[jax.ShapeDtypeStruct((parts, seq * depth, cols), BF16), lines, lines],
        scratch_shapes=[pltpu.SemaphoreType.DMA((2,)), pltpu.SemaphoreType.DMA((2,))],
        compiler_params=pltpu.CompilerParams(
            collective_id=5, has_side_effects=True, vmem_limit_bytes=VMEM
        ),
        cost_estimate=pl.CostEstimate(
            flops=2 * tokens * width * cols,
            bytes_accessed=2 * tokens * (width + cols),
            transcendentals=0,
        ),
        name="gate_up_grad",
    )(left, right, to_x, to_y)


def branch_sum_kernel(
    act_ref, w_ref, left_ref, right_ref, spread_ref, blocks_ref,
    mine, to_x, to_y, to_diagonal, spread_out, blocks_out,
    odd, even, other, odd_send, odd_recv, store, *sems,
):
    width = spread_out.shape[2]
    half = odd.shape[1]
    outs = (mine, to_x, to_y, to_diagonal)

    def columns(i):
        return spread_ref.at[:, pl.ds(pl.multiple_of(i * width, width), width)]

    spread = PlaneExchange(columns, spread_out, *sems[:3])
    blocks = PlaneExchange(lambda i: blocks_ref.at[i], blocks_out, *sems[3:])
    core = (neighbours(spread.seq)["core"], spread.rows)
    greet(spread.peers())
    spread.start()
    blocks.start()

    def hand_over(pair):
        slot = lax.rem(pair, 2)
        return remote(odd.at[slot], other.at[pair], core, odd_send.at[slot], odd_recv.at[pair])

    def keep(pair):
        at, place = (pair // 2, pair % 2) if pair < 8 else (pair - 8, 2)
        target = outs[at].at[pl.ds(place * half, half)]
        return pltpu.make_async_copy(even.at[pair % 2], target, store.at[pair % 2])

    def body(unit, carry):
        pair, side = lax.div(unit, 2), 1 - lax.rem(unit, 2)
        begin = pl.multiple_of((pair + 8 * side) * half, half)
        value = dot_nt(act_ref[pl.ds(begin, half), :], w_ref[...])

        @pl.when(side == 1)
        def _():
            @pl.when(pair >= 2)
            def _():
                hand_over(pair - 2).wait_send()

            odd[lax.rem(pair, 2)] = value.astype(BF16)
            hand_over(pair).start()

        @pl.when(side == 0)
        def _():
            hand_over(pair).wait_recv()
            for p in range(8):

                @pl.when(pair == p)
                def _(p=p):
                    if p >= 2:
                        keep(p - 2).wait()
                    even[p % 2] = (value + other[p].astype(F32)).astype(BF16)
                    keep(p).start()

        return carry

    lax.fori_loop(0, 16, body, 0)

    def columns_grad(mask):
        at = pl.multiple_of(flipped(spread.seq, mask, spread.size) * half, half)
        return dot_tn(left_ref[:, pl.ds(at, half)], right_ref[...])

    for pair in range(8, 12):
        mask = 2 * (pair - 8)
        hand_over(pair - 2).wait_send()
        odd[pair % 2] = columns_grad(mask + 1).astype(BF16)
        hand_over(pair).start()
        value = columns_grad(mask)
        hand_over(pair).wait_recv()
        keep(pair - 2).wait()
        even[pair % 2] = (value + other[pair].astype(F32)).astype(BF16)
        keep(pair).start()
    for pair in (10, 11):
        hand_over(pair).wait_send()
        keep(pair).wait()
    spread.finish()
    blocks.finish()


def branch_sum_call(act, w, left, right, spread, blocks):
    tokens, part = act.shape
    width = w.shape[0]
    seq = lax.axis_size("seq")
    count = tokens // seq
    half = count // 2
    here, there = pl.BlockSpec(memory_space=pltpu.VMEM), pl.BlockSpec(memory_space=pl.ANY)
    return pl.pallas_call(
        branch_sum_kernel,
        in_specs=[here] * 4 + [there] * 2,
        out_specs=[there] * 6,
        out_shape=[jax.ShapeDtypeStruct((count + half, width), BF16)] * 4
        + [
            jax.ShapeDtypeStruct((seq, spread.shape[0], spread.shape[1] // seq), BF16),
            jax.ShapeDtypeStruct(blocks.shape, BF16),
        ],
        scratch_shapes=[
            pltpu.VMEM((2, half, width), BF16),
            pltpu.VMEM((2, half, width), BF16),
            pltpu.VMEM((12, half, width), BF16),
            pltpu.SemaphoreType.DMA((2,)),
            pltpu.SemaphoreType.DMA((12,)),
            pltpu.SemaphoreType.DMA((2,)),
        ]
        + PlaneExchange.scratch()
        + PlaneExchange.scratch(),
        compiler_params=pltpu.CompilerParams(
            collective_id=6, has_side_effects=True, vmem_limit_bytes=VMEM
        ),
        cost_estimate=pl.CostEstimate(
            flops=2 * tokens * width * part, bytes_accessed=2 * tokens * width, transcendentals=0
        ),
        name="branch_sum",
    )(act, w, left, right, spread, blocks)


def branch_kernel(near_ref, far_ref, w_ref, _, near_out, far_out):
    near_out[...] = dot_nt(near_ref[...], w_ref[...]).astype(BF16)
    far_out[...] = dot_nt(far_ref[...], w_ref[...]).astype(BF16)


def branch_call(act, w, earlier):
    tokens, part = act.shape
    width = w.shape[0]
    block = 256
    steps = tokens // 2 // block
    shape = jax.ShapeDtypeStruct((tokens // 2, width), BF16)
    return pl.pallas_call(
        branch_kernel,
        grid=(steps,),
        in_specs=[
            pl.BlockSpec((block, part), lambda i: (i, 0)),
            pl.BlockSpec((block, part), lambda i: (i + steps, 0)),
            pl.BlockSpec(w.shape, lambda i: (0, 0), pipeline_mode=pl.Buffered(1)),
            pl.BlockSpec(memory_space=pl.ANY),
        ],
        out_specs=[pl.BlockSpec((block, width), lambda i: (i, 0))] * 2,
        out_shape=[shape, shape],
        compiler_params=pltpu.CompilerParams(vmem_limit_bytes=VMEM),
        cost_estimate=pl.CostEstimate(
            flops=2 * tokens * width * part, bytes_accessed=2 * tokens * width, transcendentals=0
        ),
        name="branch",
    )(act, act, w, earlier)


def out_grad_kernel(me, near_ref, far_ref, right_ref, _, near_out, far_out):
    near_out[...] = dot_tn(near_ref[...], right_ref[...]).astype(BF16)
    far_out[...] = dot_tn(far_ref[...], right_ref[...]).astype(BF16)


def out_grad_call(me, left, right, earlier):
    seq = lax.axis_size("seq")
    tokens, width = left.shape
    block, cols = width // seq, right.shape[1]
    shape = jax.ShapeDtypeStruct((width // 2, cols), BF16)
    return pl.pallas_call(
        out_grad_kernel,
        grid_spec=pltpu.PrefetchScalarGridSpec(
            num_scalar_prefetch=1,
            grid=(seq // 2,),
            in_specs=[
                pl.BlockSpec((tokens, block), lambda i, me: (0, natural(i, me, seq))),
                pl.BlockSpec((tokens, block), lambda i, me: (0, natural(i + seq // 2, me, seq))),
                pl.BlockSpec(right.shape, lambda i, me: (0, 0)),
                pl.BlockSpec(memory_space=pl.ANY),
            ],
            out_specs=[pl.BlockSpec((block, cols), lambda i, me: (i, 0))] * 2,
        ),
        out_shape=[shape, shape],
        compiler_params=pltpu.CompilerParams(vmem_limit_bytes=VMEM),
        cost_estimate=pl.CostEstimate(
            flops=2 * tokens * width * cols, bytes_accessed=2 * width * cols, transcendentals=0
        ),
        name="out_grad",
    )(me, left, left, right, earlier)


def finish_kernel(blocks_ref, weight_ref, gain_ref, out_ref, sum_ref):
    @pl.when((pl.program_id(0) == 0) & (pl.program_id(1) == 0))
    def _():
        sum_ref[...] = jnp.zeros_like(sum_ref)

    grad = blocks_ref[0].astype(F32)
    products = weight_ref[...].astype(F32) * grad
    sum_ref[...] += jnp.broadcast_to(jnp.sum(products, axis=1, keepdims=True), sum_ref.shape)
    out_ref[...] = grad * gain_ref[...]


def finish_call(blocks, weight, gain, groups):
    seq, depth, cols = blocks.shape
    part = cols // groups
    grad, sums = pl.pallas_call(
        finish_kernel,
        grid=(seq, groups),
        in_specs=[
            pl.BlockSpec((1, depth, part), lambda i, g: (i, 0, g)),
            pl.BlockSpec((depth, part), lambda i, g: (0, g * seq + i)),
            pl.BlockSpec((depth, 1), lambda i, g: (0, 0)),
        ],
        out_specs=[
            pl.BlockSpec((depth, part), lambda i, g: (0, g * seq + i)),
            pl.BlockSpec((depth, 128), lambda i, g: (0, 0)),
        ],
        out_shape=[
            jax.ShapeDtypeStruct((depth, seq * cols), F32),
            jax.ShapeDtypeStruct((depth, 128), F32),
        ],
        compiler_params=pltpu.CompilerParams(vmem_limit_bytes=VMEM),
        cost_estimate=pl.CostEstimate(
            flops=4 * depth * seq * cols, bytes_accessed=8 * depth * seq * cols, transcendentals=0
        ),
        name="finish_grad",
    )(blocks, weight, gain)
    return grad, sums[:, 0]


def scatter_shapes(count, width):
    return [
        jax.ShapeDtypeStruct((count, width), F32),
        jax.ShapeDtypeStruct((count, width), BF16),
        jax.ShapeDtypeStruct((count, width), BF16),
    ]


def ffn_back_call(near, far, gate_up, gu, down, count, earlier):
    width, part = down.shape
    half = count // 2
    there = pl.BlockSpec(memory_space=pl.ANY)
    own, from_x, from_y, d_gu = pl.pallas_call(
        ffn_back_kernel,
        in_specs=[there] * 6,
        out_specs=[there] * 4,
        out_shape=scatter_shapes(count, width) + [jax.ShapeDtypeStruct(gate_up.shape, BF16)],
        scratch_shapes=[
            pltpu.VMEM(gu.shape, BF16),
            pltpu.VMEM(down.shape, BF16),
            pltpu.VMEM((2, half, width), BF16),
            pltpu.VMEM((2, half, 2 * part), BF16),
            pltpu.VMEM((2, half, 2 * part), BF16),
            pltpu.VMEM((half, width), F32),
        ]
        + PlaneScatter.scratch(half, width)
        + [
            pltpu.SemaphoreType.DMA((2,)),
            pltpu.SemaphoreType.DMA((2, 2)),
            pltpu.SemaphoreType.DMA((2,)),
        ],
        compiler_params=pltpu.CompilerParams(
            collective_id=3, has_side_effects=True, vmem_limit_bytes=VMEM
        ),
        cost_estimate=pl.CostEstimate(
            flops=8 * gate_up.shape[0] * width * part, bytes_accessed=gate_up.shape[0] * width * 8, transcendentals=0
        ),
        name="ffn_back",
    )(near, far, gate_up, gu, down, earlier)
    return own + from_x.astype(F32) + from_y.astype(F32), d_gu


def project_back_kernel(
    d_ref, w_ref, gain_ref, blocks_ref, _, own, from_x, from_y, gain_out, blocks_out,
    gain_sum, gain_from, gain_send, gain_recv, block_send, block_recv, block_local,
    total, odd, even, held, other, diagonal, odd_send, odd_recv, send, recv, keep,
):
    scatter = PlaneScatter(
        own, from_x, from_y, odd, even, held, other, diagonal, (odd_send, odd_recv, send, recv, keep)
    )
    half = scatter.half
    blocks = PlaneExchange(
        lambda i: blocks_ref.at[i], blocks_out, block_send, block_recv, block_local
    )
    partners = [(scatter.to[device], scatter.rows) for device in ("core", "x", "y")]
    size = lax.axis_size("rows")
    mask = 1
    others = []
    while mask < size:
        others.append((scatter.seq, flipped(scatter.rows, mask, size)))
        mask *= 2
    partners = partners + others
    greet(blocks.peers() + others)
    gain_sum[0] = gain_ref[...]

    def exchange(i):
        return remote(
            gain_sum.at[i], gain_from.at[i], partners[i], gain_send.at[i], gain_recv.at[i]
        )

    def add_gains(i):
        exchange(i).wait_recv()
        gain_sum[i + 1] = gain_sum[i] + gain_from[i]

    def body(unit, carry):
        for i in range(len(partners)):
            at_unit(unit, 2 * i + 1, exchange(i).start)
            at_unit(unit, 2 * i + 2, partial(add_gains, i))
        at_unit(unit, 13, blocks.start)
        pair, side = lax.div(unit, 2), 1 - lax.rem(unit, 2)
        begin = pl.multiple_of((PlaneScatter.place(pair) + 8 * side) * half, half)
        total[...] = dot_nt(d_ref[pl.ds(begin, half), :], w_ref[...])

        @pl.when(side == 1)
        def _():
            scatter.give_odd(pair, total[...])

        @pl.when(side == 0)
        def _():
            scatter.give_even(pair, total)

        return carry

    lax.fori_loop(0, 16, body, 0)
    gain_out[...] = gain_sum[len(partners)]
    blocks.finish()
    for i in range(len(partners)):
        exchange(i).wait_send()
    scatter.finish()


def project_back_call(d, w, gains, blocks, count, earlier):
    width = w.shape[0]
    half = count // 2
    here, there = pl.BlockSpec(memory_space=pltpu.VMEM), pl.BlockSpec(memory_space=pl.ANY)
    rounds = 3 + (lax.axis_size("rows") - 1).bit_length()
    own, from_x, from_y, gains, blocks = pl.pallas_call(
        project_back_kernel,
        in_specs=[here] * 3 + [there] * 2,
        out_specs=[there] * 3 + [here, there],
        out_shape=scatter_shapes(count, width) + [
            jax.ShapeDtypeStruct(gains.shape, F32),
            jax.ShapeDtypeStruct(blocks.shape, BF16),
        ],
        scratch_shapes=[
            pltpu.VMEM((rounds + 1,) + gains.shape, F32),
            pltpu.VMEM((rounds,) + gains.shape, F32),
            pltpu.SemaphoreType.DMA((rounds,)),
            pltpu.SemaphoreType.DMA((rounds,)),
        ]
        + PlaneExchange.scratch()
        + [
            pltpu.VMEM((half, width), F32),
        ]
        + PlaneScatter.scratch(half, width),
        compiler_params=pltpu.CompilerParams(
            collective_id=4, has_side_effects=True, vmem_limit_bytes=VMEM
        ),
        cost_estimate=pl.CostEstimate(
            flops=16 * d.shape[0] * width * w.shape[1], bytes_accessed=d.shape[0] * width * 8, transcendentals=0
        ),
        name="project_back",
    )(d, w, gains, blocks, earlier)
    return own + from_x.astype(F32) + from_y.astype(F32), gains, blocks


def ffn_kernel(hidden_ref, grad_ref, gu_ref, down_ref, act_ref, dgu_ref):
    part = down_ref.shape[1]
    gate, up, act = gate_and_up(hidden_ref[...], gu_ref)
    d_gate, d_up = gate_and_up_back(gate, up, dot_nn(grad_ref[...], down_ref[...]))
    act_ref[...] = act
    dgu_ref[:, :part] = d_gate
    dgu_ref[:, part:] = d_up


def ffn_call(hidden, grad, gu, down):
    count, width = hidden.shape
    part = down.shape[1]
    block = 256
    return pl.pallas_call(
        ffn_kernel,
        grid=(count // block,),
        in_specs=[
            pl.BlockSpec((block, width), lambda i: (i, 0)),
            pl.BlockSpec((block, width), lambda i: (i, 0)),
            pl.BlockSpec(gu.shape, lambda i: (0, 0), pipeline_mode=pl.Buffered(1)),
            pl.BlockSpec(down.shape, lambda i: (0, 0), pipeline_mode=pl.Buffered(1)),
        ],
        out_specs=[
            pl.BlockSpec((block, part), lambda i: (i, 0)),
            pl.BlockSpec((block, 2 * part), lambda i: (i, 0)),
        ],
        out_shape=[
            jax.ShapeDtypeStruct((count, part), BF16),
            jax.ShapeDtypeStruct((count, 2 * part), BF16),
        ],
        compiler_params=pltpu.CompilerParams(vmem_limit_bytes=VMEM),
        name="ffn",
    )(hidden, grad, gu, down)


def all_to_all(block):
    return lax.all_to_all(block, "seq", 0, 0, tiled=True)


def gather_z(block):
    full = lax.all_gather(block, "rows", axis=1, tiled=True)
    return full.reshape(-1, full.shape[-1])


def scatter_z(grad):
    parts, lines, cols = grad.shape
    grad = lax.psum_scatter(
        grad.reshape(parts * lines, cols), "rows", scatter_dimension=0, tiled=True
    )
    return grad.reshape(lax.axis_size("seq"), -1, cols)


def shards(
    tokens,
    lengths,
    norm_gains,
    qk_gains,
    qkv_weight,
    out_weight,
    gate_up_weight,
    down_weight,
    cotangent,
):
    rows, slots, width = tokens.shape
    count = rows * slots
    seq = lax.axis_size("seq")
    group = QUERY_HEADS // seq
    query_width = group * HEAD
    sharing = seq // KEY_VALUE_HEADS
    total = seq * slots
    depth = qkv_weight.shape[0]
    kv_at = QUERY_HEADS * HEAD
    part = down_weight.shape[1] // seq
    me = lax.axis_index("seq").astype(jnp.int32)[None]
    gains = norm_gains.astype(F32)

    qkv_scaled = (qkv_weight.astype(F32) * gains[0][:, None]).astype(BF16)
    kv_scaled = qkv_scaled[:, kv_at:].reshape(depth, 2, KEY_VALUE_HEADS, HEAD)
    qkv_blocks = jnp.concatenate(
        [
            qkv_scaled[:, :kv_at].reshape(depth, seq, query_width),
            jnp.repeat(kv_scaled[:, 0], sharing, axis=1),
            jnp.repeat(kv_scaled[:, 1], sharing, axis=1),
        ],
        axis=2,
    ).transpose(1, 0, 2)
    qkv_mine = gather_z(all_to_all(qkv_blocks))
    out_block = lax.all_gather(out_weight, "rows", axis=0, tiled=True)
    gu_scaled = (gate_up_weight.astype(F32) * gains[1][:, None]).astype(BF16)
    gu_blocks = gu_scaled.reshape(depth, 2, seq, part).transpose(2, 0, 1, 3)
    gu_mine = gather_z(all_to_all(gu_blocks.reshape(seq, depth, 2 * part)))
    down_blocks = down_weight.reshape(depth, seq, part).transpose(1, 0, 2)

    lane = jnp.arange(128) % HEAD
    frequency = jnp.exp(
        -math.log(10000.0) * ((lane % (HEAD // 2)).astype(F32) * (2.0 / HEAD))
    )
    angles = jnp.arange(total).astype(F32)[:, None] * frequency[None, :]
    cos = jnp.cos(angles)
    sin = jnp.where(lane < HEAD // 2, -1.0, 1.0)[None, :] * jnp.sin(angles)
    qk = qk_gains.astype(F32)
    head_gains = jnp.concatenate([jnp.tile(qk[0], group), qk[1], jnp.ones((HEAD,), F32)])[None, :]

    inputs = tokens.reshape(count, width).astype(F32)
    r0 = lax.rsqrt(jnp.mean(inputs * inputs, axis=-1, keepdims=True) + EPSILON)
    unit0 = (inputs * r0).astype(BF16)
    if seq == 8:
        unit0, raw, q, kv = gather_qkv_call(unit0, qkv_mine, cos, sin, head_gains, rows, slots)
    else:
        unit0 = gather_plane(unit0)
        raw, q, kv = qkv_call(me, unit0, qkv_mine, cos, sin, head_gains, rows, slots)
    out_full = gather_natural(after(out_block, q))
    down_mine = gather_z(after(all_to_all(down_blocks), q))
    attended_mine, attended_low, logs = attend_call(lengths, q, kv, slots)
    attended = all_to_all(attended_low).transpose(1, 2, 0, 3).reshape(count, kv_at)
    middle = inputs + dot_nt(attended, out_full)
    r1 = lax.rsqrt(jnp.mean(middle * middle, axis=-1, keepdims=True) + EPSILON)

    grad_low = cotangent.reshape(count, width)
    unit1 = (middle * r1).astype(BF16)
    half = seq * count // 2
    if seq == 8:
        unit1, near, far, gate_up, act = gather_ffn_call(
            unit1, gather_pieces(grad_low, q), gu_mine
        )
        down_grad = weight_grad_call([near, far], act, act, depth, "down_grad")
        u, d_gu = ffn_back_call(near, far, gate_up, gu_mine, down_mine, count, down_grad)
    else:
        grad_all = gather_plane(grad_low)
        unit1 = gather_plane(unit1)
        act, d_gu = ffn_call(unit1, grad_all, gu_mine, down_mine)
        u_odd = dot_nt(d_gu[half:], gu_mine).astype(BF16)
        u = scatter_plane(u_odd, dot_nt(d_gu[:half], gu_mine))
        near, far = grad_all[:half], grad_all[half:]
        down_grad = weight_grad_call([near, far], act, act, depth, "down_grad")
    down_sum = scatter_z(down_grad)

    d_middle = (
        grad_low.astype(F32)
        + r1 * u
        - middle * (r1 * r1 * r1) * jnp.mean(u * middle, axis=-1, keepdims=True)
    )
    d_branch = d_middle.astype(BF16)
    d_attended = dot_nn(d_branch, out_full).astype(BF16)
    if seq == 8:
        *sums, d_attended, down_owned = branch_sum_call(
            act, down_mine, d_branch, attended, d_attended, down_sum
        )
        d_attended = d_attended.reshape(seq, rows, slots, query_width)
        gu_grad, from_x, from_y = grad_send_call(unit1, d_gu, sums[1], sums[2], count, depth)
    else:
        branch_near, branch_far = branch_call(act, down_mine, d_attended)
        branch_far = swap(branch_far, 1).astype(F32)
        branch_all = (branch_near.astype(F32) + branch_far).astype(BF16)
        branch_parts = [branch_all[i * count : (i + 1) * count] for i in range(seq // 2)]
        gu_grad = weight_grad_call([unit1], d_gu, branch_near, depth, "gate_up_grad")
        d_attended = d_attended.reshape(rows, slots, seq, query_width).transpose(2, 0, 1, 3)
        d_attended = all_to_all(d_attended)
        down_owned = all_to_all(down_sum)
    gu_sum = scatter_z(gu_grad)
    features = width // seq
    if seq != 8:
        out_near, out_far = out_grad_call(me, d_branch, attended, gu_grad)
        out_all = (out_near.astype(F32) + swap(out_far, 1).astype(F32)).astype(BF16)
        sums = [
            jnp.concatenate([branch_parts[i], out_all[i * features : (i + 1) * features]], axis=0)
            for i in range(seq // 2)
        ]
    dq, dkv = attend_back_call(
        lengths, q, kv, attended_mine, d_attended, logs, [gu_grad, *sums]
    )
    d_qkv, head_gain_grad = prepare_back_call(
        me, raw, dq, dkv, cos, sin, head_gains, slots, dq
    )
    if seq == 8:
        diagonal = swap(sums[3], 6)
        arrived = [from_x, from_y, diagonal[:count]]
        out_arrived = [swap(sums[i][count:], 2 * i) for i in (1, 2)] + [diagonal[count:]]
    else:
        arrived = [swap(sums[i], 2 * i) for i in range(1, seq // 2)]
        out_arrived = [part[count:] for part in arrived]
        arrived = [part[:count] for part in arrived]
    branch = after(sums[0][:count].astype(F32), d_qkv)
    for part_sum in arrived:
        branch = branch + part_sum.astype(F32)
    out_sum = after(sums[0][count:].astype(F32), d_qkv)
    for part_sum in out_arrived:
        out_sum = out_sum + part_sum.astype(F32)
    output = (middle + branch).astype(BF16).reshape(rows, slots, width)
    qkv_grad = weight_grad_call([unit0], d_qkv, output, depth, "qkv_grad")
    if seq == 8:
        gain_rows = jnp.broadcast_to(head_gain_grad, (8, head_gain_grad.shape[1]))
        u0, head_gain_grad, gu_owned = project_back_call(
            d_qkv, qkv_mine, gain_rows, gu_sum, count, qkv_grad
        )
    else:
        u0_odd = dot_nt(d_qkv[half:], qkv_mine).astype(BF16)
        u0 = scatter_plane(u0_odd, dot_nt(d_qkv[:half], qkv_mine))
        head_gain_grad = sum_everywhere(head_gain_grad)
        gu_owned = all_to_all(gu_sum)
    parts = lax.axis_size("rows")
    out_blocks = out_sum.astype(BF16).reshape(parts, depth * seq, kv_at // seq)
    attn_grad = after(jnp.concatenate([qkv_grad, out_blocks], axis=2), gu_sum)
    attn_sum = scatter_z(attn_grad)
    qkv_sum = attn_sum[:, :, : query_width + 2 * HEAD]
    out_sum = attn_sum[:, :, query_width + 2 * HEAD :].reshape(depth, kv_at)
    input_grad = (
        d_middle + r0 * u0 - inputs * (r0 * r0 * r0) * jnp.mean(u0 * inputs, axis=-1, keepdims=True)
    )
    input_grad = input_grad.astype(BF16).reshape(rows, slots, width)
    qk_grad = jnp.stack(
        [head_gain_grad[0, :query_width].reshape(group, HEAD).sum(0), head_gain_grad[0, query_width : query_width + HEAD]]
    )

    gu_out, gu_rows = finish_call(gu_owned, gate_up_weight, gains[1][:, None], 2)
    down_out, _ = finish_call(down_owned, down_weight, jnp.ones((depth, 1), F32), 1)
    qkv_sum = all_to_all(qkv_sum).transpose(1, 0, 2).astype(F32)
    kv_sum = qkv_sum[:, :, query_width:].reshape(depth, KEY_VALUE_HEADS, sharing, 2 * HEAD).sum(2)
    qkv_sum = jnp.concatenate(
        [
            qkv_sum[:, :, :query_width].reshape(depth, -1),
            kv_sum[:, :, :HEAD].reshape(depth, -1),
            kv_sum[:, :, HEAD:].reshape(depth, -1),
        ],
        axis=1,
    )
    norm_gain_grad = jnp.stack(
        [
            jnp.sum(qkv_weight.astype(F32) * qkv_sum, axis=1),
            gu_rows,
        ]
    )
    return (
        output,
        input_grad,
        norm_gain_grad,
        qk_grad,
        qkv_sum * gains[0][:, None],
        out_sum.astype(F32),
        gu_out,
        down_out,
    )


def solution(mesh):
    in_specs = (
        P("rows", "seq", None),
        P("rows"),
        P(None, ("seq", "rows")),
        P(),
        P(("seq", "rows"), None),
        P(("seq", "rows"), None),
        P(("seq", "rows"), None),
        P(("seq", "rows"), None),
        P("rows", "seq", None),
    )
    out_specs = (
        P("rows", "seq", None),
        P("rows", "seq", None),
        P(None, ("seq", "rows")),
        P(),
        P(("seq", "rows"), None),
        P(("seq", "rows"), None),
        P(("seq", "rows"), None),
        P(("seq", "rows"), None),
    )
    return jax.shard_map(shards, mesh=mesh, in_specs=in_specs, out_specs=out_specs, check_vma=False)
```

```python
from functools import partial
import math

import jax
import jax.numpy as jnp
from jax import lax
from jax.experimental import pallas as pl
from jax.experimental.pallas import tpu as pltpu
from jax.sharding import PartitionSpec as P

QUERY_HEADS = 32
KEY_VALUE_HEADS = 8
HEAD = 64
EPSILON = 1e-06
F32 = jnp.float32
BF16 = jnp.bfloat16
HIGHEST = lax.Precision.HIGHEST
SCALE = HEAD ** (-0.5)
SCALE2 = SCALE * math.log2(math.e)
VMEM = 56 * 1024 * 1024


def swap(block, mask):
    return lax.ppermute(block, "seq", [(i, i ^ mask) for i in range(lax.axis_size("seq"))])


def masks_between_chips():
    return [1 << bit for bit in range(1, lax.axis_size("seq").bit_length() - 1)]


def natural(place, me, seq):
    return me[0] ^ (2 * lax.rem(place, seq // 2) + lax.div(place, seq // 2))


def dot_nn(a, b):
    return jnp.dot(a, b, preferred_element_type=F32)


def dot_nt(a, b, precision=None):
    return lax.dot_general(
        a, b, (((1,), (1,)), ((), ())), preferred_element_type=F32, precision=precision
    )


def dot_tn(a, b):
    return lax.dot_general(a, b, (((0,), (0,)), ((), ())), preferred_element_type=F32)


def after(value, *results):
    zero = sum(result[(0,) * result.ndim].astype(F32) for result in results) * 0.0
    return value + zero.astype(value.dtype)


def gather_pieces(chunk, earlier):
    half = chunk.shape[0] // 2
    along_x, along_y = swap(chunk, 2), swap(chunk, 4)
    through_x, through_y = after(along_y[:half], earlier), after(along_x[half:], earlier)
    return [chunk, along_x, along_y, swap(through_x, 2), swap(through_y, 4)]


def gather_plane(chunk):
    own = [chunk]
    for mask in masks_between_chips():
        own = own + [swap(part, mask) for part in own]
    return jnp.concatenate(own + [swap(part, 1) for part in own], axis=0)


def gather_natural(block):
    seq, me, size = lax.axis_size("seq"), lax.axis_index("seq"), block.shape[0]
    parts = {mask: swap(block, mask) if mask > 0 else block for mask in range(0, seq, 2)}
    parts.update({mask + 1: swap(part, 1) for mask, part in list(parts.items())})
    whole = jnp.zeros((seq * size,) + block.shape[1:], block.dtype)
    for m, part in parts.items():
        whole = lax.dynamic_update_slice_in_dim(whole, part, (me ^ m) * size, 0)
    return whole


def scatter_chips(parts):
    if len(parts) == 4:
        mine, to_x, to_y, diagonal = parts
        half = mine.shape[0] // 2
        diagonal = diagonal.astype(BF16)
        from_x = swap(diagonal[:half], 2).astype(F32)
        from_y = swap(diagonal[half:], 4).astype(F32)
        to_x = jnp.concatenate([to_x[:half], to_x[half:] + from_y], axis=0).astype(BF16)
        to_y = jnp.concatenate([to_y[:half] + from_x, to_y[half:]], axis=0).astype(BF16)
        return mine + swap(to_x, 2).astype(F32) + swap(to_y, 4).astype(F32)
    for mask in reversed(masks_between_chips()):
        kept = len(parts) // 2
        parts = [
            parts[i] + swap(parts[kept + i].astype(BF16), mask).astype(F32) for i in range(kept)
        ]
    return parts[0]


def scatter_plane(odd, even, scatter=scatter_chips):
    count = 1 << len(masks_between_chips())
    size = even.shape[0] // count
    both = even + swap(odd, 1).astype(F32)
    return scatter([both[i * size : (i + 1) * size] for i in range(count)])


def sum_everywhere(value):
    for axis in ("seq", "rows"):
        size = lax.axis_size(axis)
        mask = 1
        while mask < size:
            value = value + lax.ppermute(value, axis, [(i, i ^ mask) for i in range(size)])
            mask *= 2
    return value


def lane_of(shape):
    return lax.broadcasted_iota(jnp.int32, shape, len(shape) - 1)


def swap_halves(v):
    first = lane_of(v.shape) % HEAD < HEAD // 2
    return jnp.where(first, pltpu.roll(v, 96, 1), pltpu.roll(v, 32, 1))


def head_mean(v):
    rows = lax.broadcasted_iota(jnp.int32, (128, 128), 0) // HEAD
    cols = lax.broadcasted_iota(jnp.int32, (128, 128), 1) // HEAD
    block = jnp.where(rows == cols, 1.0 / HEAD, 0.0).astype(F32)
    return jnp.dot(v, block, preferred_element_type=F32, precision=HIGHEST)


def qkv_kernel(me, x_ref, w_ref, cos_ref, sin_ref, gain_ref, raw_ref, q_ref, kv_ref):
    rows, slots = q_ref.shape[0], q_ref.shape[1]
    raw = dot_nn(x_ref[...], w_ref[...])
    cos, sin = cos_ref[...], sin_ref[...]
    keys = lane_of((slots, 128)) < HEAD
    for r in range(rows):
        part = raw[r * slots : (r + 1) * slots]
        raw_ref[r] = part
        last = part.shape[1] // 128 - 1
        for s in range(last + 1):
            v = part[:, s * 128 : (s + 1) * 128]
            out = normed_rotated(v, cos, sin, gain_ref[:, s * 128 : (s + 1) * 128])
            if s < last:
                q_ref[r, :, s * 128 : (s + 1) * 128] = out.astype(BF16)
            else:
                kv_ref[r] = jnp.where(keys, out, v).astype(BF16)


def qkv_call(me, x, w, cos, sin, gains, rows, slots):
    chunk = rows * slots
    width = w.shape[1]
    query_width = width - 128
    seq = x.shape[0] // chunk
    total = seq * slots
    return pl.pallas_call(
        qkv_kernel,
        grid_spec=pltpu.PrefetchScalarGridSpec(
            num_scalar_prefetch=1,
            grid=(seq,),
            in_specs=[
                pl.BlockSpec((chunk, x.shape[1]), lambda i, me: (i, 0)),
                pl.BlockSpec(w.shape, lambda i, me: (0, 0)),
                pl.BlockSpec((slots, 128), lambda i, me: (natural(i, me, seq), 0)),
                pl.BlockSpec((slots, 128), lambda i, me: (natural(i, me, seq), 0)),
                pl.BlockSpec((1, width), lambda i, me: (0, 0)),
            ],
            out_specs=[
                pl.BlockSpec((rows, slots, width), lambda i, me: (0, natural(i, me, seq), 0)),
                pl.BlockSpec((rows, slots, query_width), lambda i, me: (0, natural(i, me, seq), 0)),
                pl.BlockSpec((rows, slots, 128), lambda i, me: (0, natural(i, me, seq), 0)),
            ],
        ),
        out_shape=[
            jax.ShapeDtypeStruct((rows, total, width), F32),
            jax.ShapeDtypeStruct((rows, total, query_width), BF16),
            jax.ShapeDtypeStruct((rows, total, 128), BF16),
        ],
        compiler_params=pltpu.CompilerParams(vmem_limit_bytes=VMEM),
        name="qkv_prepare",
    )(me, x, w, cos, sin, gains)


def attend_kernel(lengths, q_ref, kv_ref, out_ref, low_ref, log_ref, k2, vo, acc):
    row, step = pl.program_id(0), pl.program_id(1)
    block = q_ref.shape[1]
    group = q_ref.shape[2] // HEAD
    length = lengths[row]

    @pl.when(step == 0)
    def _():
        kv = kv_ref[0].astype(F32)
        keys = lane_of(kv.shape) < HEAD
        k2[...] = jnp.where(keys, kv, pltpu.roll(kv, HEAD, 1)).astype(BF16)
        vo[...] = jnp.where(keys, 1.0, kv).astype(BF16)

    low_half = lane_of((block, 128)) < HEAD
    queries = []
    for h in range(group):
        part = q_ref[0, :, (h // 2) * 128 : (h // 2 + 1) * 128].astype(F32)
        kept = low_half if h % 2 == 0 else jnp.logical_not(low_half)
        queries.append(jnp.where(kept, part, 0.0).astype(BF16))
    acc[...] = jnp.zeros_like(acc)

    def one_block(at, masked):
        begin = pl.multiple_of(at * block, block)
        keys = k2[pl.ds(begin, block), :]
        values = vo[pl.ds(begin, block), :]
        if masked:
            key_place = begin + lax.broadcasted_iota(jnp.int32, (block, block), 1)
            query_place = step * block + lax.broadcasted_iota(jnp.int32, (block, block), 0)
            allowed = (key_place <= query_place) & (key_place < length)
        for h in range(group):
            weights = jnp.exp2(dot_nt(queries[h], keys) * SCALE2)
            if masked:
                weights = jnp.where(allowed, weights, 0.0)
            acc[h] += dot_nn(weights.astype(BF16), values)

    full = jnp.minimum(step, lax.div(length, block))

    def body(at, carry):
        one_block(at, False)
        return carry

    lax.fori_loop(0, full, body, 0)

    @pl.when(full * block < length)
    def _():
        one_block(full, True)

    for g in range(group // 2):
        even, odd = acc[2 * g], acc[2 * g + 1]
        even_turned, odd_turned = pltpu.roll(even, HEAD, 1), pltpu.roll(odd, HEAD, 1)
        mixed = jnp.where(low_half, even_turned / even, odd / odd_turned)
        out_ref[0, :, g * 128 : (g + 1) * 128] = mixed
        low_ref[0, 0, :, g * 128 : (g + 1) * 128] = mixed.astype(BF16)
        log_ref[0, 2 * g : 2 * g + 1, :] = jnp.log2(even.T[0:1, :])
        log_ref[0, 2 * g + 1 : 2 * g + 2, :] = jnp.log2(odd.T[0:1, :])
    log_ref[0, group:, :] = jnp.zeros((8 - group, block), F32)


def attend_call(lengths, q, kv, block):
    rows, total, width = q.shape
    seq = total // block
    return pl.pallas_call(
        attend_kernel,
        grid_spec=pltpu.PrefetchScalarGridSpec(
            num_scalar_prefetch=1,
            grid=(rows, seq),
            in_specs=[
                pl.BlockSpec((1, block, width), lambda r, i, n: (r, i, 0)),
                pl.BlockSpec((1, total, 128), lambda r, i, n: (r, 0, 0)),
            ],
            out_specs=[
                pl.BlockSpec((1, block, width), lambda r, i, n: (r, i, 0)),
                pl.BlockSpec((1, 1, block, width), lambda r, i, n: (i, r, 0, 0)),
                pl.BlockSpec((1, 8, block), lambda r, i, n: (r, 0, i)),
            ],
            scratch_shapes=[
                pltpu.VMEM((total, 128), BF16),
                pltpu.VMEM((total, 128), BF16),
                pltpu.VMEM((width // HEAD, block, 128), F32),
            ],
        ),
        out_shape=[
            jax.ShapeDtypeStruct((rows, total, width), F32),
            jax.ShapeDtypeStruct((seq, rows, block, width), BF16),
            jax.ShapeDtypeStruct((rows, 8, total), F32),
        ],
        compiler_params=pltpu.CompilerParams(vmem_limit_bytes=VMEM),
        cost_estimate=pl.CostEstimate(
            flops=rows * total * total * width * 16, bytes_accessed=rows * total * width * 8, transcendentals=0
        ),
        name="attend",
    )(lengths, q, kv)


def attend_back_kernel(
    lengths, q_ref, kv_ref, out_ref, grad_ref, log_ref, *refs
):
    dq_ref, dkv_ref, delta, dqt, kacc, vacc = refs[-6:]
    row, step = pl.program_id(0), pl.program_id(1)
    block = kv_ref.shape[1]
    count = q_ref.shape[1] // block
    width = q_ref.shape[2]
    group = width // HEAD
    length = lengths[row]

    @pl.when(step == 0)
    def _():
        dqt[...] = jnp.zeros_like(dqt)
        heads = lax.broadcasted_iota(jnp.int32, (8, width), 0)
        pick = jnp.where(lane_of((8, width)) // HEAD == heads, 1.0, 0.0).astype(F32)
        for i in range(count):
            product = grad_ref[i, 0].astype(F32) * out_ref[0, i * block : (i + 1) * block, :]
            delta[:, i * block : (i + 1) * block] = dot_nt(pick, product, HIGHEST)

    kacc[...] = jnp.zeros_like(kacc)
    vacc[...] = jnp.zeros_like(vacc)
    begin = step * block
    kv = kv_ref[0].astype(F32)
    turned = pltpu.roll(kv, HEAD, 1)
    low_half = lane_of((block, 128)) < HEAD
    keys = [
        jnp.where(low_half, kv, 0.0).astype(BF16),
        jnp.where(low_half, 0.0, turned).astype(BF16),
    ]
    values = [
        jnp.where(low_half, turned, 0.0).astype(BF16),
        jnp.where(low_half, 0.0, kv).astype(BF16),
    ]
    keys_turned = [
        jnp.where(low_half, kv, 0.0).T.astype(BF16),
        jnp.where(low_half, 0.0, turned).T.astype(BF16),
    ]

    def one_block(at, masked):
        first = pl.multiple_of(at * block, block)
        if masked:
            key_place = begin + lax.broadcasted_iota(jnp.int32, (block, block), 0)
            query_place = first + lax.broadcasted_iota(jnp.int32, (block, block), 1)
            allowed = (key_place <= query_place) & (key_place < length)
        for g in range(group // 2):
            queries = q_ref[0, pl.ds(first, block), g * 128 : (g + 1) * 128]
            grads = grad_ref[at, 0, :, g * 128 : (g + 1) * 128]
            turned_sum = None
            for side in range(2):
                h = 2 * g + side
                logs = log_ref[0, h : h + 1, pl.ds(first, block)]
                deltas = delta[h : h + 1, pl.ds(first, block)]
                weights = jnp.exp2(dot_nt(keys[side], queries) * SCALE2 - logs)
                if masked:
                    weights = jnp.where(allowed, weights, 0.0)
                d_weights = dot_nt(values[side], grads)
                d_scores = (weights * (d_weights - deltas)).astype(BF16)
                vacc[side] += dot_nn(weights.astype(BF16), grads)
                kacc[side] += dot_nn(d_scores, queries)
                term = dot_nn(keys_turned[side], d_scores)
                turned_sum = term if turned_sum is None else turned_sum + term
            dqt[g, :, pl.ds(first, block)] += turned_sum

    @pl.when(begin < length)
    def _():
        inside = begin + block <= length

        @pl.when(inside)
        def _():
            one_block(step, True)

            def body(at, carry):
                one_block(at, False)
                return carry

            lax.fori_loop(step + 1, count, body, 0)

        @pl.when(jnp.logical_not(inside))
        def _():
            def body(at, carry):
                one_block(at, True)
                return carry

            lax.fori_loop(step, count, body, 0)

    ksum = jnp.where(low_half, kacc[0], 0.0) + pltpu.roll(jnp.where(low_half, 0.0, kacc[1]), HEAD, 1)
    vsum = pltpu.roll(jnp.where(low_half, vacc[0], 0.0), HEAD, 1) + jnp.where(
        low_half, 0.0, vacc[1]
    )
    dkv_ref[0] = jnp.where(low_half, ksum * SCALE, vsum)

    @pl.when(step == count - 1)
    def _():
        for g in range(group // 2):
            for i in range(count):
                dq_ref[0, i * block : (i + 1) * block, g * 128 : (g + 1) * 128] = (
                    dqt[g, :, i * block : (i + 1) * block].T * SCALE
                )


def attend_back_call(lengths, q, kv, attended, grads, logs, earlier):
    rows, total, width = q.shape
    seq, block = grads.shape[0], grads.shape[2]
    return pl.pallas_call(
        attend_back_kernel,
        grid_spec=pltpu.PrefetchScalarGridSpec(
            num_scalar_prefetch=1,
            grid=(rows, seq),
            in_specs=[
                pl.BlockSpec((1, total, width), lambda r, i, n: (r, 0, 0)),
                pl.BlockSpec((1, block, 128), lambda r, i, n: (r, i, 0)),
                pl.BlockSpec((1, total, width), lambda r, i, n: (r, 0, 0)),
                pl.BlockSpec((seq, 1, block, width), lambda r, i, n: (0, r, 0, 0)),
                pl.BlockSpec((1, 8, total), lambda r, i, n: (r, 0, 0)),
            ]
            + [pl.BlockSpec(memory_space=pl.ANY)] * len(earlier),
            out_specs=[
                pl.BlockSpec((1, total, width), lambda r, i, n: (r, 0, 0)),
                pl.BlockSpec((1, block, 128), lambda r, i, n: (r, i, 0)),
            ],
            scratch_shapes=[
                pltpu.VMEM((8, total), F32),
                pltpu.VMEM((width // 128, 128, total), F32),
                pltpu.VMEM((2, block, 128), F32),
                pltpu.VMEM((2, block, 128), F32),
            ],
        ),
        out_shape=[
            jax.ShapeDtypeStruct((rows, total, width), F32),
            jax.ShapeDtypeStruct((rows, total, 128), F32),
        ],
        compiler_params=pltpu.CompilerParams(vmem_limit_bytes=VMEM),
        cost_estimate=pl.CostEstimate(
            flops=rows * total * total * width * 28, bytes_accessed=rows * total * width * 14, transcendentals=0
        ),
        name="attend_back",
    )(lengths, q, kv, attended, grads, logs, *earlier)


def prepare_back_kernel(
    me, raw_ref, dq_ref, dkv_ref, cos_ref, sin_ref, gain_ref, _, out_ref, gain_grad_ref
):
    rows, slots = dq_ref.shape[0], dq_ref.shape[1]
    cos, sin = cos_ref[...], sin_ref[...]
    keys = lane_of((slots, 128)) < HEAD
    last = raw_ref.shape[2] // 128 - 1

    @pl.when(pl.program_id(0) == 0)
    def _():
        gain_grad_ref[...] = jnp.zeros_like(gain_grad_ref)

    for r in range(rows):
        for s in range(last + 1):
            lanes = slice(s * 128, (s + 1) * 128)
            raw = raw_ref[r, :, lanes]
            grad = dq_ref[r, :, lanes] if s < last else dkv_ref[r]
            gain = gain_ref[:, lanes]
            turned = grad * cos + swap_halves(grad * sin)
            factor = lax.rsqrt(head_mean(raw * raw) + EPSILON)
            gain_grad_ref[:, lanes] += jnp.sum(turned * raw * factor, axis=0, keepdims=True)
            u = turned * gain
            mean = head_mean(u * raw)
            result = factor * u - raw * (factor * factor * factor) * mean
            if s == last:
                result = jnp.where(keys, result, grad)
            out_ref[r * slots : (r + 1) * slots, lanes] = result.astype(BF16)


def prepare_back_call(me, raw, dq, dkv, cos, sin, gains, slots, earlier):
    rows, total, width = raw.shape
    seq = total // slots
    return pl.pallas_call(
        prepare_back_kernel,
        grid_spec=pltpu.PrefetchScalarGridSpec(
            num_scalar_prefetch=1,
            grid=(seq,),
            in_specs=[
                pl.BlockSpec((rows, slots, width), lambda i, me: (0, natural(i, me, seq), 0)),
                pl.BlockSpec((rows, slots, width - 128), lambda i, me: (0, natural(i, me, seq), 0)),
                pl.BlockSpec((rows, slots, 128), lambda i, me: (0, natural(i, me, seq), 0)),
                pl.BlockSpec((slots, 128), lambda i, me: (natural(i, me, seq), 0)),
                pl.BlockSpec((slots, 128), lambda i, me: (natural(i, me, seq), 0)),
                pl.BlockSpec((1, width), lambda i, me: (0, 0)),
                pl.BlockSpec(memory_space=pl.ANY),
            ],
            out_specs=[
                pl.BlockSpec((rows * slots, width), lambda i, me: (i, 0)),
                pl.BlockSpec((1, width), lambda i, me: (0, 0)),
            ],
        ),
        out_shape=[
            jax.ShapeDtypeStruct((rows * total, width), BF16),
            jax.ShapeDtypeStruct((1, width), F32),
        ],
        compiler_params=pltpu.CompilerParams(vmem_limit_bytes=VMEM),
        name="prepare_back",
    )(me, raw, dq, dkv, cos, sin, gains, earlier)


def neighbours(me):
    return {
        "core": me + 1 - 2 * lax.rem(me, 2),
        "x": me + 2 - 4 * lax.rem(lax.div(me, 2), 2),
        "y": me + 4 - 8 * lax.div(me, 4),
    }


def remote(source, target, device, send, recv):
    return pltpu.make_async_remote_copy(
        src_ref=source,
        dst_ref=target,
        send_sem=send,
        recv_sem=recv,
        device_id=device,
        device_id_type=pl.DeviceIdType.MESH,
    )


def greet(devices):
    barrier = pltpu.get_barrier_semaphore()
    for device in devices:
        pl.semaphore_signal(barrier, inc=1, device_id=device, device_id_type=pl.DeviceIdType.MESH)
    pl.semaphore_wait(barrier, len(devices))


def greet_neighbours(to, rows):
    greet([(to[device], rows) for device in ("core", "x", "y")])


def flipped(index, mask, size):
    result, bit = index, 1
    while bit < size:
        if mask & bit:
            result = result + bit - 2 * bit * lax.rem(lax.div(index, bit), 2)
        bit *= 2
    return result


class PlaneExchange:
    def __init__(self, block, target, send, recv, local):
        self.seq, self.rows = lax.axis_index("seq"), lax.axis_index("rows")
        self.size = lax.axis_size("seq")
        self.block, self.target, self.send, self.recv, self.local = block, target, send, recv, local

    @staticmethod
    def scratch():
        others = lax.axis_size("seq") - 1
        return [
            pltpu.SemaphoreType.DMA((others,)),
            pltpu.SemaphoreType.DMA((others,)),
            pltpu.SemaphoreType.DMA,
        ]

    def peers(self):
        return [(flipped(self.seq, mask, self.size), self.rows) for mask in range(1, self.size)]

    def copies(self):
        remotes = [
            remote(self.block(peer[0]), self.target.at[self.seq], peer, self.send.at[i], self.recv.at[i])
            for i, peer in enumerate(self.peers())
        ]
        own = pltpu.make_async_copy(self.block(self.seq), self.target.at[self.seq], self.local)
        return remotes, own

    def start(self):
        remotes, own = self.copies()
        for copy in remotes:
            copy.start()
        own.start()

    def finish(self):
        remotes, own = self.copies()
        for copy in remotes:
            copy.wait()
        own.wait()


class PlaneGather:
    COPIES = 14

    def __init__(self, own, whole, send, recv):
        self.seq, self.rows = lax.axis_index("seq"), lax.axis_index("rows")
        self.half = own.shape[0] // 2
        self.own, self.whole, self.send, self.recv = own, whole, send, recv
        self.to = neighbours(self.seq)

    def place(self, at, half):
        return pl.ds((2 * at + half) * self.half, self.half)

    def copy(self, i):
        half, own, whole = self.half, self.own, self.whole
        first, second = own.at[pl.ds(0, half)], own.at[pl.ds(half, half)]

        def moved(at, h, to):
            return whole.at[self.place(at, h)], whole.at[self.place(to, h)]

        source, target, device = (
            (second, whole.at[self.place(1, 1)], "x"),
            (first, whole.at[self.place(2, 0)], "y"),
            (first, whole.at[self.place(1, 0)], "x"),
            (second, whole.at[self.place(2, 1)], "y"),
            (first, whole.at[self.place(4, 0)], "core"),
            (second, whole.at[self.place(4, 1)], "core"),
            moved(1, 1, 3) + ("y",),
            moved(2, 0, 3) + ("x",),
            moved(1, 1, 5) + ("core",),
            moved(2, 0, 6) + ("core",),
            moved(1, 0, 5) + ("core",),
            moved(2, 1, 6) + ("core",),
            moved(3, 0, 7) + ("core",),
            moved(3, 1, 7) + ("core",),
        )[i]
        return remote(
            source, target, (self.to[device], self.rows), self.send.at[i], self.recv.at[i]
        )

    def fetch(self, unit, target, sem):
        begin = pl.multiple_of(unit_place(unit) * self.half, self.half)
        return pltpu.make_async_copy(self.whole.at[pl.ds(begin, self.half)], target, sem)

    def start_fetch(self, unit, target, sem):
        @pl.when(unit < 2)
        def _():
            begin = pl.multiple_of(lax.rem(unit, 2) * self.half, self.half)
            pltpu.make_async_copy(self.own.at[pl.ds(begin, self.half)], target, sem).start()

        @pl.when(unit >= 2)
        def _():
            self.fetch(unit, target, sem).start()

    def keep(self, unit, source, sem):
        begin = pl.multiple_of(lax.rem(unit, 2) * self.half, self.half)
        return pltpu.make_async_copy(source, self.whole.at[pl.ds(begin, self.half)], sem)

    def start(self):
        for i in (0, 1, 2, 3, 4, 5):
            self.copy(i).start()

    def open_group(self, group):
        if group == 1:
            self.copy(0).wait_recv()
            self.copy(6).start()
            self.copy(8).start()
            self.copy(1).wait_recv()
            self.copy(7).start()
            self.copy(9).start()
        if group == 2:
            self.copy(2).wait_recv()
            self.copy(10).start()
            self.copy(3).wait_recv()
            self.copy(11).start()
        if group == 3:
            self.copy(7).wait_recv()
            self.copy(12).start()
            self.copy(6).wait_recv()
            self.copy(13).start()

    def open_second(self, group):
        for i in ((4, 5), (8, 9), (10, 11), (12, 13))[group]:
            self.copy(i).wait_recv()

    def finish(self):
        for i in range(self.COPIES):
            self.copy(i).wait_send()


def unit_place(unit):
    group, k = lax.div(unit, 4), lax.rem(unit, 4)
    odd, late = lax.rem(group, 2), lax.div(group, 2)
    base = 3 * odd + 2 * late + odd * late
    stride = 1 + 2 * late * (1 - odd)
    return 8 * lax.div(k, 2) + base + stride * lax.rem(k, 2)


def at_unit(unit, value, action):
    @pl.when(unit == value)
    def _():
        action()


def normed_rotated(raw, cos, sin, gain):
    factor = lax.rsqrt(head_mean(raw * raw) + EPSILON)
    n = raw * factor * gain
    return n * cos + swap_halves(n) * sin


def gather_qkv_kernel(
    x_ref, w_ref, cos_ref, sin_ref, gain_ref, whole, raw_ref, q_ref, kv_ref,
    xbuf, rawbuf, qbuf, kvbuf, load, store, keep, send, recv,
):
    gather = PlaneGather(x_ref, whole, send, recv)
    half = gather.half
    me = gather.seq
    last = w_ref.shape[1] // 128 - 1
    greet_neighbours(gather.to, gather.rows)
    gather.start()

    def stores(unit, slot):
        place = unit_place(unit)
        at, row = lax.rem(lax.div(place, 2), 4), lax.rem(place, 2)
        core = lax.rem(lax.rem(me, 2) + lax.div(place, 8), 2)
        x = lax.rem(lax.div(me, 2) + at, 2)
        y = lax.rem(lax.div(me, 4) + lax.div(at, 2), 2)
        block = core + 2 * x + 4 * y
        begin = pl.ds(pl.multiple_of(block * half, half), half)
        return [
            pltpu.make_async_copy(rawbuf.at[slot], raw_ref.at[row, begin], store.at[0, slot]),
            pltpu.make_async_copy(qbuf.at[slot], q_ref.at[row, begin], store.at[1, slot]),
            pltpu.make_async_copy(kvbuf.at[slot], kv_ref.at[row, begin], store.at[2, slot]),
        ], block

    def body(unit, carry):
        slot = lax.rem(unit, 2)
        for group in range(4):
            at_unit(unit, 4 * group, partial(gather.open_group, group))
            at_unit(unit, 4 * group + 1, partial(gather.open_second, group))

        @pl.when(lax.rem(unit, 4) == 0)
        def _():
            gather.start_fetch(unit, xbuf.at[slot], load.at[slot])

        gather.fetch(unit, xbuf.at[slot], load.at[slot]).wait()

        @pl.when(unit < 2)
        def _():
            gather.keep(unit, xbuf.at[slot], keep.at[slot]).start()

        @pl.when((unit == 1) | (unit == 2))
        def _():
            gather.keep(unit - 1, xbuf.at[1 - slot], keep.at[1 - slot]).wait()

        @pl.when(lax.rem(unit, 4) != 3)
        def _():
            gather.start_fetch(unit + 1, xbuf.at[1 - slot], load.at[1 - slot])

        copies, block = stores(unit, slot)

        @pl.when(unit >= 2)
        def _():
            for copy in stores(unit - 2, slot)[0]:
                copy.wait()

        raw = dot_nn(xbuf[slot], w_ref[...])
        rawbuf[slot] = raw
        turn = pl.ds(pl.multiple_of(block * half, half), half)
        cos, sin = cos_ref[turn, :], sin_ref[turn, :]
        for s in range(last + 1):
            lanes = slice(s * 128, (s + 1) * 128)
            v = raw[:, lanes]
            out = normed_rotated(v, cos, sin, gain_ref[:, lanes])
            if s < last:
                qbuf[slot, :, lanes] = out.astype(BF16)
            else:
                kvbuf[slot] = jnp.where(lane_of(v.shape) < HEAD, out, v).astype(BF16)
        for copy in copies:
            copy.start()
        return carry

    lax.fori_loop(0, 16, body, 0)
    for slot in range(2):
        for copy in stores(14 + slot, slot)[0]:
            copy.wait()
    gather.finish()


def gather_qkv_call(x, w, cos, sin, gains, rows, slots):
    count, width = x.shape
    seq = lax.axis_size("seq")
    total = seq * slots
    cols = w.shape[1]
    here, there = pl.BlockSpec(memory_space=pltpu.VMEM), pl.BlockSpec(memory_space=pl.ANY)
    return pl.pallas_call(
        gather_qkv_kernel,
        in_specs=[there, here, here, here, here],
        out_specs=[there] * 4,
        out_shape=[
            jax.ShapeDtypeStruct((seq * count, width), BF16),
            jax.ShapeDtypeStruct((rows, total, cols), F32),
            jax.ShapeDtypeStruct((rows, total, cols - 128), BF16),
            jax.ShapeDtypeStruct((rows, total, 128), BF16),
        ],
        scratch_shapes=[
            pltpu.VMEM((2, slots, width), BF16),
            pltpu.VMEM((2, slots, cols), F32),
            pltpu.VMEM((2, slots, cols - 128), BF16),
            pltpu.VMEM((2, slots, 128), BF16),
            pltpu.SemaphoreType.DMA((2,)),
            pltpu.SemaphoreType.DMA((3, 2)),
            pltpu.SemaphoreType.DMA((2,)),
            pltpu.SemaphoreType.DMA((PlaneGather.COPIES,)),
            pltpu.SemaphoreType.DMA((PlaneGather.COPIES,)),
        ],
        compiler_params=pltpu.CompilerParams(
            collective_id=1, has_side_effects=True, vmem_limit_bytes=VMEM
        ),
        cost_estimate=pl.CostEstimate(
            flops=2 * seq * count * width * cols * 8, bytes_accessed=seq * count * width * 4, transcendentals=0
        ),
        name="gather_qkv",
    )(x, w, cos, sin, gains)


class PlaneScatter:
    def __init__(self, own, from_x, from_y, odd, even, held, other, diagonal, sems):
        self.seq, self.rows = lax.axis_index("seq"), lax.axis_index("rows")
        self.to = neighbours(self.seq)
        self.half = odd.shape[1]
        self.own, self.from_x, self.from_y = own, from_x, from_y
        self.odd, self.even, self.held, self.other, self.diagonal = odd, even, held, other, diagonal
        self.odd_send, self.odd_recv, self.send, self.recv, self.store = sems

    @staticmethod
    def scratch(half, width):
        return [
            pltpu.VMEM((2, half, width), BF16),
            pltpu.VMEM((6, half, width), BF16),
            pltpu.VMEM((2, half, width), F32),
            pltpu.VMEM((8, half, width), BF16),
            pltpu.VMEM((2, half, width), BF16),
            pltpu.SemaphoreType.DMA((2,)),
            pltpu.SemaphoreType.DMA((8,)),
            pltpu.SemaphoreType.DMA((6,)),
            pltpu.SemaphoreType.DMA((6,)),
            pltpu.SemaphoreType.DMA((2,)),
        ]

    @staticmethod
    def place(pair):
        two, b = lax.div(pair, 2), lax.rem(pair, 2)
        odd, late = lax.rem(two, 2), lax.div(two, 2)
        base = 6 * (1 - odd) * (1 - late) + 2 * odd * (1 - late) + 3 * (1 - odd) * late
        return base + b * (1 + 2 * odd * (1 - late))

    def hand_over(self, pair):
        slot = lax.rem(pair, 2)
        return remote(
            self.odd.at[slot],
            self.other.at[pair],
            (self.to["core"], self.rows),
            self.odd_send.at[slot],
            self.odd_recv.at[pair],
        )

    def copy(self, i):
        first, second = pl.ds(0, self.half), pl.ds(self.half, self.half)
        target, device = (
            (self.diagonal.at[0], "x"),
            (self.diagonal.at[1], "y"),
            (self.from_x.at[first], "x"),
            (self.from_y.at[second], "y"),
            (self.from_x.at[second], "x"),
            (self.from_y.at[first], "y"),
        )[i]
        return remote(
            self.even.at[i], target, (self.to[device], self.rows), self.send.at[i], self.recv.at[i]
        )

    def keep(self, i):
        return pltpu.make_async_copy(
            self.held.at[i], self.own.at[pl.ds(i * self.half, self.half)], self.store.at[i]
        )

    def give_odd(self, pair, value):
        @pl.when(pair >= 2)
        def _():
            self.hand_over(pair - 2).wait_send()

        self.odd[lax.rem(pair, 2)] = value.astype(BF16)
        self.hand_over(pair).start()

    def give_even(self, pair, value_ref):
        self.hand_over(pair).wait_recv()
        for at, i in ((0, 0), (1, 1), (2, 2), (3, 3), (4, 4), (5, 5)):

            @pl.when(pair == at)
            def _(at=at, i=i):
                total = value_ref[...] + self.other[at].astype(F32)
                if i >= 4:
                    self.copy(5 - i).wait_recv()
                    total = total + self.diagonal[5 - i].astype(F32)
                self.even[i] = total.astype(BF16)
                self.copy(i).start()

        for at, i in ((6, 0), (7, 1)):

            @pl.when(pair == at)
            def _(at=at, i=i):
                self.held[i] = value_ref[...] + self.other[at].astype(F32)
                self.keep(i).start()

    def finish(self):
        for pair in (6, 7):
            self.hand_over(pair).wait_send()
        for i in range(6):
            self.copy(i).wait_send()
        for i in (2, 3, 4, 5):
            self.copy(i).wait_recv()
        for i in range(2):
            self.keep(i).wait()


def gate_and_up(hidden, gu_ref):
    part = gu_ref.shape[1] // 2
    gate = dot_nn(hidden, gu_ref[:, :part])
    up = dot_nn(hidden, gu_ref[:, part:])
    return gate, up, (gate / (1.0 + jnp.exp(-gate)) * up).astype(BF16)


def gate_and_up_back(gate, up, d_act):
    sigmoid = 1.0 / (1.0 + jnp.exp(-gate))
    silu = gate * sigmoid
    d_gate = d_act * up * (sigmoid + silu * (1.0 - sigmoid))
    return d_gate.astype(BF16), (d_act * silu).astype(BF16)


def gather_ffn_kernel(
    x_ref, c0_ref, cx_ref, cy_ref, cd0_ref, cd1_ref, gu_hbm,
    whole, near_ref, far_ref, gate_up_ref, act_ref,
    gu, hbuf, cbuf, gbuf, abuf, weight_sem, load, store, keep, send, recv, piece_send, piece_recv,
):
    gather = PlaneGather(x_ref, whole, send, recv)
    half = gather.half
    part = gu.shape[1] // 2
    weights = pltpu.make_async_copy(gu_hbm, gu, weight_sem)
    weights.start()
    greet_neighbours(gather.to, gather.rows)
    gather.start()

    def stores(unit, slot):
        begin = pl.ds(pl.multiple_of(unit_place(unit) * half, half), half)
        return [
            pltpu.make_async_copy(abuf.at[slot], act_ref.at[begin], store.at[0, slot]),
            pltpu.make_async_copy(gbuf.at[slot], gate_up_ref.at[begin], store.at[1, slot]),
        ]

    piece_refs = (c0_ref, cx_ref, cy_ref, cd0_ref, cd1_ref)
    piece_at = ((0, 2), (2, 2), (4, 2), (6, 1), (7, 1))

    def piece(i):
        begin, size = piece_at[i]
        target = far_ref.at[pl.ds(begin * half, size * half)]
        return remote(
            piece_refs[i],
            target,
            (gather.to["core"], gather.rows),
            piece_send.at[i],
            piece_recv.at[i],
        )

    for i in range(5):
        piece(i).start()

    def passing(at):
        i = (0, 0, 1, 1, 2, 2, 3, 4)[at]
        source = piece_refs[i].at[pl.ds((at - piece_at[i][0]) * half, half)]
        return (
            pltpu.make_async_copy(source, cbuf.at[at % 2], keep.at[1, 0]),
            pltpu.make_async_copy(
                cbuf.at[at % 2], near_ref.at[pl.ds(at * half, half)], keep.at[1, 1]
            ),
        )

    def read_piece(at):
        passing(at)[0].start()

    def write_piece(at):
        passing(at)[0].wait()
        passing(at)[1].start()

    def end_piece(at):
        passing(at)[1].wait()

    def body(unit, carry):
        slot = lax.rem(unit, 2)
        for at in range(8):
            at_unit(unit, 2 * at, partial(read_piece, at))
            at_unit(unit, 2 * at + 1, partial(write_piece, at))
            if at < 7:
                at_unit(unit, 2 * at + 2, partial(end_piece, at))
        for group in range(4):
            at_unit(unit, 4 * group, partial(gather.open_group, group))
            at_unit(unit, 4 * group + 1, partial(gather.open_second, group))

        @pl.when(lax.rem(unit, 4) == 0)
        def _():
            gather.start_fetch(unit, hbuf.at[slot], load.at[slot])

        at_unit(unit, 0, weights.wait)
        gather.fetch(unit, hbuf.at[slot], load.at[slot]).wait()

        @pl.when(unit < 2)
        def _():
            gather.keep(unit, hbuf.at[slot], keep.at[0, slot]).start()

        @pl.when((unit == 1) | (unit == 2))
        def _():
            gather.keep(unit - 1, hbuf.at[1 - slot], keep.at[0, 1 - slot]).wait()

        @pl.when(lax.rem(unit, 4) != 3)
        def _():
            gather.start_fetch(unit + 1, hbuf.at[1 - slot], load.at[1 - slot])

        @pl.when(unit >= 2)
        def _():
            for copy in stores(unit - 2, slot):
                copy.wait()

        gate, up, act = gate_and_up(hbuf[slot], gu)
        abuf[slot] = act
        gbuf[slot, :, :part] = gate.astype(BF16)
        gbuf[slot, :, part:] = up.astype(BF16)
        for copy in stores(unit, slot):
            copy.start()
        return carry

    lax.fori_loop(0, 16, body, 0)
    for slot in range(2):
        for copy in stores(14 + slot, slot):
            copy.wait()
    end_piece(7)
    for i in range(5):
        piece(i).wait_recv()
        piece(i).wait_send()
    gather.finish()


def gather_ffn_call(x, pieces, gu):
    count, width = x.shape
    seq = lax.axis_size("seq")
    cols = gu.shape[1]
    half = count // 2
    there = pl.BlockSpec(memory_space=pl.ANY)
    return pl.pallas_call(
        gather_ffn_kernel,
        in_specs=[there] * 7,
        out_specs=[there] * 5,
        out_shape=[
            jax.ShapeDtypeStruct((seq * count, width), BF16),
            jax.ShapeDtypeStruct((seq * half, width), BF16),
            jax.ShapeDtypeStruct((seq * half, width), BF16),
            jax.ShapeDtypeStruct((seq * count, cols), BF16),
            jax.ShapeDtypeStruct((seq * count, cols // 2), BF16),
        ],
        scratch_shapes=[
            pltpu.VMEM(gu.shape, BF16),
            pltpu.VMEM((2, half, width), BF16),
            pltpu.VMEM((2, half, width), BF16),
            pltpu.VMEM((2, half, cols), BF16),
            pltpu.VMEM((2, half, cols // 2), BF16),
            pltpu.SemaphoreType.DMA,
            pltpu.SemaphoreType.DMA((2,)),
            pltpu.SemaphoreType.DMA((2, 2)),
            pltpu.SemaphoreType.DMA((2, 2)),
            pltpu.SemaphoreType.DMA((PlaneGather.COPIES,)),
            pltpu.SemaphoreType.DMA((PlaneGather.COPIES,)),
            pltpu.SemaphoreType.DMA((5,)),
            pltpu.SemaphoreType.DMA((5,)),
        ],
        compiler_params=pltpu.CompilerParams(
            collective_id=2, has_side_effects=True, vmem_limit_bytes=VMEM
        ),
        cost_estimate=pl.CostEstimate(
            flops=4 * seq * count * width * cols, bytes_accessed=seq * count * width * 8, transcendentals=0
        ),
        name="gather_ffn",
    )(x, *pieces, gu)


def ffn_back_kernel(
    near_ref, far_ref, gate_up_ref, gu_hbm, down_hbm, _, own, from_x, from_y, dgu_ref,
    gu, down, cbuf, gbuf, dbuf, total, odd, even, held, other, diagonal,
    odd_send, odd_recv, send, recv, keep, weight_sem, load, store,
):
    scatter = PlaneScatter(
        own, from_x, from_y, odd, even, held, other, diagonal, (odd_send, odd_recv, send, recv, keep)
    )
    half = scatter.half
    part = down.shape[1]
    weights = [
        pltpu.make_async_copy(down_hbm, down, weight_sem.at[0]),
        pltpu.make_async_copy(gu_hbm, gu, weight_sem.at[1]),
    ]
    for copy in weights:
        copy.start()

    def row_of(unit, whole):
        side = 8 * (1 - lax.rem(unit, 2)) if whole else 0
        place = PlaneScatter.place(lax.div(unit, 2)) + side
        return pl.ds(pl.multiple_of(place * half, half), half)

    def fetch(unit, slot):
        return [
            pltpu.make_async_copy(near_ref.at[row_of(unit, False)], cbuf.at[slot], load.at[0, slot]),
            pltpu.make_async_copy(
                gate_up_ref.at[row_of(unit, True)], gbuf.at[slot], load.at[1, slot]
            ),
        ]

    def start_fetch(unit, slot):
        near, gates = fetch(unit, slot)
        gates.start()

        @pl.when(lax.rem(unit, 2) == 0)
        def _():
            pltpu.make_async_copy(
                far_ref.at[row_of(unit, False)], cbuf.at[slot], load.at[0, slot]
            ).start()

        @pl.when(lax.rem(unit, 2) == 1)
        def _():
            near.start()

    def stores(unit, slot):
        return pltpu.make_async_copy(dbuf.at[slot], dgu_ref.at[row_of(unit, True)], store.at[slot])

    start_fetch(0, 0)
    greet_neighbours(scatter.to, scatter.rows)

    def body(unit, carry):
        slot = lax.rem(unit, 2)
        pair = lax.div(unit, 2)
        at_unit(unit, 0, weights[0].wait)
        for copy in fetch(unit, slot):
            copy.wait()

        @pl.when(unit < 15)
        def _():
            start_fetch(unit + 1, 1 - slot)

        @pl.when(unit >= 2)
        def _():
            stores(unit - 2, slot).wait()

        d_act = dot_nn(cbuf[slot], down[...])
        gate, up = gbuf[slot, :, :part].astype(F32), gbuf[slot, :, part:].astype(F32)
        d_gate, d_up = gate_and_up_back(gate, up, d_act)
        dbuf[slot, :, :part] = d_gate
        dbuf[slot, :, part:] = d_up
        stores(unit, slot).start()
        at_unit(unit, 0, weights[1].wait)
        total[...] = dot_nt(dbuf[slot], gu[...])

        @pl.when(slot == 0)
        def _():
            scatter.give_odd(pair, total[...])

        @pl.when(slot == 1)
        def _():
            scatter.give_even(pair, total)

        return carry

    lax.fori_loop(0, 16, body, 0)
    for slot in range(2):
        stores(14 + slot, slot).wait()
    scatter.finish()


def weight_grad_kernel(*refs):
    lefts, right_ref, out_ref = refs[:-3], refs[-3], refs[-1]
    depth = out_ref.shape[1]
    size = right_ref.shape[0] // len(lefts)
    grad = None
    for i, left in enumerate(lefts):
        term = dot_tn(left[...], right_ref[i * size : (i + 1) * size, :])
        grad = term if grad is None else grad + term
    for z in range(out_ref.shape[0]):
        out_ref[z] = grad[z * depth : (z + 1) * depth].astype(BF16)


def weight_grad_call(lefts, right, earlier, depth, name):
    seq, parts = lax.axis_size("seq"), lax.axis_size("rows")
    width = lefts[0].shape[1]
    block = width // seq
    tokens, cols = right.shape
    return pl.pallas_call(
        weight_grad_kernel,
        grid=(seq,),
        in_specs=[pl.BlockSpec((left.shape[0], block), lambda i: (0, i)) for left in lefts]
        + [
            pl.BlockSpec(right.shape, lambda i: (0, 0), pipeline_mode=pl.Buffered(1)),
            pl.BlockSpec(memory_space=pl.ANY),
        ],
        out_specs=pl.BlockSpec((parts, depth, cols), lambda i: (0, i, 0)),
        out_shape=jax.ShapeDtypeStruct((parts, seq * depth, cols), BF16),
        compiler_params=pltpu.CompilerParams(vmem_limit_bytes=VMEM),
        cost_estimate=pl.CostEstimate(
            flops=2 * tokens * width * cols,
            bytes_accessed=2 * tokens * (width + cols),
            transcendentals=0,
        ),
        name=name,
    )(*lefts, right, earlier)


def grad_send_kernel(
    left_ref, right_ref, to_x, to_y, out_ref, from_x, from_y, send, recv
):
    seq, rows = lax.axis_index("seq"), lax.axis_index("rows")
    to = neighbours(seq)
    lines = pl.ds(0, from_x.shape[0])
    copies = [
        remote(source.at[lines], target, (to[device], rows), send.at[i], recv.at[i])
        for i, (source, target, device) in enumerate(((to_x, from_x, "x"), (to_y, from_y, "y")))
    ]

    @pl.when(pl.program_id(0) == 0)
    def _():
        greet([(to["x"], rows), (to["y"], rows)])
        for copy in copies:
            copy.start()

    depth = out_ref.shape[1]
    grad = dot_tn(left_ref[...], right_ref[...])
    for z in range(out_ref.shape[0]):
        out_ref[z] = grad[z * depth : (z + 1) * depth].astype(BF16)

    @pl.when(pl.program_id(0) == pl.num_programs(0) - 1)
    def _():
        for copy in copies:
            copy.wait()


def grad_send_call(left, right, to_x, to_y, count, depth):
    seq, parts = lax.axis_size("seq"), lax.axis_size("rows")
    tokens, cols = right.shape
    width = left.shape[1]
    there = pl.BlockSpec(memory_space=pl.ANY)
    lines = jax.ShapeDtypeStruct((count, to_x.shape[1]), BF16)
    return pl.pallas_call(
        grad_send_kernel,
        grid=(seq,),
        in_specs=[
            pl.BlockSpec((tokens, width // seq), lambda i: (0, i)),
            pl.BlockSpec(right.shape, lambda i: (0, 0), pipeline_mode=pl.Buffered(1)),
            there,
            there,
        ],
        out_specs=[pl.BlockSpec((parts, depth, cols), lambda i: (0, i, 0)), there, there],
        out_shape=[jax.ShapeDtypeStruct((parts, seq * depth, cols), BF16), lines, lines],
        scratch_shapes=[pltpu.SemaphoreType.DMA((2,)), pltpu.SemaphoreType.DMA((2,))],
        compiler_params=pltpu.CompilerParams(
            collective_id=5, has_side_effects=True, vmem_limit_bytes=VMEM
        ),
        cost_estimate=pl.CostEstimate(
            flops=2 * tokens * width * cols,
            bytes_accessed=2 * tokens * (width + cols),
            transcendentals=0,
        ),
        name="gate_up_grad",
    )(left, right, to_x, to_y)


def branch_sum_kernel(
    act_ref, w_ref, left_ref, right_ref, spread_ref, blocks_ref,
    mine, to_x, to_y, to_diagonal, spread_out, blocks_out,
    odd, even, other, odd_send, odd_recv, store, *sems,
):
    width = spread_out.shape[2]
    half = odd.shape[1]
    outs = (mine, to_x, to_y, to_diagonal)

    def columns(i):
        return spread_ref.at[:, pl.ds(pl.multiple_of(i * width, width), width)]

    spread = PlaneExchange(columns, spread_out, *sems[:3])
    blocks = PlaneExchange(lambda i: blocks_ref.at[i], blocks_out, *sems[3:])
    core = (neighbours(spread.seq)["core"], spread.rows)
    greet(spread.peers())
    spread.start()
    blocks.start()

    def hand_over(pair):
        slot = lax.rem(pair, 2)
        return remote(odd.at[slot], other.at[pair], core, odd_send.at[slot], odd_recv.at[pair])

    def keep(pair):
        at, place = (pair // 2, pair % 2) if pair < 8 else (pair - 8, 2)
        target = outs[at].at[pl.ds(place * half, half)]
        return pltpu.make_async_copy(even.at[pair % 2], target, store.at[pair % 2])

    def body(unit, carry):
        pair, side = lax.div(unit, 2), 1 - lax.rem(unit, 2)
        begin = pl.multiple_of((pair + 8 * side) * half, half)
        value = dot_nt(act_ref[pl.ds(begin, half), :], w_ref[...])

        @pl.when(side == 1)
        def _():
            @pl.when(pair >= 2)
            def _():
                hand_over(pair - 2).wait_send()

            odd[lax.rem(pair, 2)] = value.astype(BF16)
            hand_over(pair).start()

        @pl.when(side == 0)
        def _():
            hand_over(pair).wait_recv()
            for p in range(8):

                @pl.when(pair == p)
                def _(p=p):
                    if p >= 2:
                        keep(p - 2).wait()
                    even[p % 2] = (value + other[p].astype(F32)).astype(BF16)
                    keep(p).start()

        return carry

    lax.fori_loop(0, 16, body, 0)

    def columns_grad(mask):
        at = pl.multiple_of(flipped(spread.seq, mask, spread.size) * half, half)
        return dot_tn(left_ref[:, pl.ds(at, half)], right_ref[...])

    for pair in range(8, 12):
        mask = 2 * (pair - 8)
        hand_over(pair - 2).wait_send()
        odd[pair % 2] = columns_grad(mask + 1).astype(BF16)
        hand_over(pair).start()
        value = columns_grad(mask)
        hand_over(pair).wait_recv()
        keep(pair - 2).wait()
        even[pair % 2] = (value + other[pair].astype(F32)).astype(BF16)
        keep(pair).start()
    for pair in (10, 11):
        hand_over(pair).wait_send()
        keep(pair).wait()
    spread.finish()
    blocks.finish()


def branch_sum_call(act, w, left, right, spread, blocks):
    tokens, part = act.shape
    width = w.shape[0]
    seq = lax.axis_size("seq")
    count = tokens // seq
    half = count // 2
    here, there = pl.BlockSpec(memory_space=pltpu.VMEM), pl.BlockSpec(memory_space=pl.ANY)
    return pl.pallas_call(
        branch_sum_kernel,
        in_specs=[here] * 4 + [there] * 2,
        out_specs=[there] * 6,
        out_shape=[jax.ShapeDtypeStruct((count + half, width), BF16)] * 4
        + [
            jax.ShapeDtypeStruct((seq, spread.shape[0], spread.shape[1] // seq), BF16),
            jax.ShapeDtypeStruct(blocks.shape, BF16),
        ],
        scratch_shapes=[
            pltpu.VMEM((2, half, width), BF16),
            pltpu.VMEM((2, half, width), BF16),
            pltpu.VMEM((12, half, width), BF16),
            pltpu.SemaphoreType.DMA((2,)),
            pltpu.SemaphoreType.DMA((12,)),
            pltpu.SemaphoreType.DMA((2,)),
        ]
        + PlaneExchange.scratch()
        + PlaneExchange.scratch(),
        compiler_params=pltpu.CompilerParams(
            collective_id=6, has_side_effects=True, vmem_limit_bytes=VMEM
        ),
        cost_estimate=pl.CostEstimate(
            flops=2 * tokens * width * part, bytes_accessed=2 * tokens * width, transcendentals=0
        ),
        name="branch_sum",
    )(act, w, left, right, spread, blocks)


def branch_kernel(near_ref, far_ref, w_ref, _, near_out, far_out):
    near_out[...] = dot_nt(near_ref[...], w_ref[...]).astype(BF16)
    far_out[...] = dot_nt(far_ref[...], w_ref[...]).astype(BF16)


def branch_call(act, w, earlier):
    tokens, part = act.shape
    width = w.shape[0]
    block = 256
    steps = tokens // 2 // block
    shape = jax.ShapeDtypeStruct((tokens // 2, width), BF16)
    return pl.pallas_call(
        branch_kernel,
        grid=(steps,),
        in_specs=[
            pl.BlockSpec((block, part), lambda i: (i, 0)),
            pl.BlockSpec((block, part), lambda i: (i + steps, 0)),
            pl.BlockSpec(w.shape, lambda i: (0, 0), pipeline_mode=pl.Buffered(1)),
            pl.BlockSpec(memory_space=pl.ANY),
        ],
        out_specs=[pl.BlockSpec((block, width), lambda i: (i, 0))] * 2,
        out_shape=[shape, shape],
        compiler_params=pltpu.CompilerParams(vmem_limit_bytes=VMEM),
        cost_estimate=pl.CostEstimate(
            flops=2 * tokens * width * part, bytes_accessed=2 * tokens * width, transcendentals=0
        ),
        name="branch",
    )(act, act, w, earlier)


def out_grad_kernel(me, near_ref, far_ref, right_ref, _, near_out, far_out):
    near_out[...] = dot_tn(near_ref[...], right_ref[...]).astype(BF16)
    far_out[...] = dot_tn(far_ref[...], right_ref[...]).astype(BF16)


def out_grad_call(me, left, right, earlier):
    seq = lax.axis_size("seq")
    tokens, width = left.shape
    block, cols = width // seq, right.shape[1]
    shape = jax.ShapeDtypeStruct((width // 2, cols), BF16)
    return pl.pallas_call(
        out_grad_kernel,
        grid_spec=pltpu.PrefetchScalarGridSpec(
            num_scalar_prefetch=1,
            grid=(seq // 2,),
            in_specs=[
                pl.BlockSpec((tokens, block), lambda i, me: (0, natural(i, me, seq))),
                pl.BlockSpec((tokens, block), lambda i, me: (0, natural(i + seq // 2, me, seq))),
                pl.BlockSpec(right.shape, lambda i, me: (0, 0)),
                pl.BlockSpec(memory_space=pl.ANY),
            ],
            out_specs=[pl.BlockSpec((block, cols), lambda i, me: (i, 0))] * 2,
        ),
        out_shape=[shape, shape],
        compiler_params=pltpu.CompilerParams(vmem_limit_bytes=VMEM),
        cost_estimate=pl.CostEstimate(
            flops=2 * tokens * width * cols, bytes_accessed=2 * width * cols, transcendentals=0
        ),
        name="out_grad",
    )(me, left, left, right, earlier)


def finish_kernel(blocks_ref, weight_ref, gain_ref, out_ref, sum_ref):
    @pl.when((pl.program_id(0) == 0) & (pl.program_id(1) == 0))
    def _():
        sum_ref[...] = jnp.zeros_like(sum_ref)

    part = blocks_ref.shape[2]
    for i in range(blocks_ref.shape[0]):
        lanes = slice(i * part, (i + 1) * part)
        grad = blocks_ref[i].astype(F32)
        products = weight_ref[:, lanes].astype(F32) * grad
        sum_ref[...] += jnp.broadcast_to(jnp.sum(products, axis=1, keepdims=True), sum_ref.shape)
        out_ref[:, lanes] = grad * gain_ref[...]


def finish_call(blocks, weight, gain, groups):
    seq, depth, cols = blocks.shape
    part = cols // groups
    many = 4
    steps = seq // many
    grad, sums = pl.pallas_call(
        finish_kernel,
        grid=(steps, groups),
        in_specs=[
            pl.BlockSpec((many, depth, part), lambda i, g: (i, 0, g)),
            pl.BlockSpec((depth, many * part), lambda i, g: (0, g * steps + i)),
            pl.BlockSpec((depth, 1), lambda i, g: (0, 0)),
        ],
        out_specs=[
            pl.BlockSpec((depth, many * part), lambda i, g: (0, g * steps + i)),
            pl.BlockSpec((depth, 128), lambda i, g: (0, 0)),
        ],
        out_shape=[
            jax.ShapeDtypeStruct((depth, seq * cols), F32),
            jax.ShapeDtypeStruct((depth, 128), F32),
        ],
        compiler_params=pltpu.CompilerParams(vmem_limit_bytes=VMEM),
        cost_estimate=pl.CostEstimate(
            flops=4 * depth * seq * cols, bytes_accessed=8 * depth * seq * cols, transcendentals=0
        ),
        name="finish_grad",
    )(blocks, weight, gain)
    return grad, sums[:, 0]


def scatter_shapes(count, width):
    return [
        jax.ShapeDtypeStruct((count, width), F32),
        jax.ShapeDtypeStruct((count, width), BF16),
        jax.ShapeDtypeStruct((count, width), BF16),
    ]


def ffn_back_call(near, far, gate_up, gu, down, count, earlier):
    width, part = down.shape
    half = count // 2
    there = pl.BlockSpec(memory_space=pl.ANY)
    own, from_x, from_y, d_gu = pl.pallas_call(
        ffn_back_kernel,
        in_specs=[there] * 6,
        out_specs=[there] * 4,
        out_shape=scatter_shapes(count, width) + [jax.ShapeDtypeStruct(gate_up.shape, BF16)],
        scratch_shapes=[
            pltpu.VMEM(gu.shape, BF16),
            pltpu.VMEM(down.shape, BF16),
            pltpu.VMEM((2, half, width), BF16),
            pltpu.VMEM((2, half, 2 * part), BF16),
            pltpu.VMEM((2, half, 2 * part), BF16),
            pltpu.VMEM((half, width), F32),
        ]
        + PlaneScatter.scratch(half, width)
        + [
            pltpu.SemaphoreType.DMA((2,)),
            pltpu.SemaphoreType.DMA((2, 2)),
            pltpu.SemaphoreType.DMA((2,)),
        ],
        compiler_params=pltpu.CompilerParams(
            collective_id=3, has_side_effects=True, vmem_limit_bytes=VMEM
        ),
        cost_estimate=pl.CostEstimate(
            flops=8 * gate_up.shape[0] * width * part, bytes_accessed=gate_up.shape[0] * width * 8, transcendentals=0
        ),
        name="ffn_back",
    )(near, far, gate_up, gu, down, earlier)
    return own + from_x.astype(F32) + from_y.astype(F32), d_gu


def project_back_kernel(
    d_ref, w_ref, gain_ref, blocks_ref, _, own, from_x, from_y, gain_out, blocks_out,
    gain_sum, gain_from, gain_send, gain_recv, block_send, block_recv, block_local,
    total, odd, even, held, other, diagonal, odd_send, odd_recv, send, recv, keep,
):
    scatter = PlaneScatter(
        own, from_x, from_y, odd, even, held, other, diagonal, (odd_send, odd_recv, send, recv, keep)
    )
    half = scatter.half
    blocks = PlaneExchange(
        lambda i: blocks_ref.at[i], blocks_out, block_send, block_recv, block_local
    )
    partners = [(scatter.to[device], scatter.rows) for device in ("core", "x", "y")]
    size = lax.axis_size("rows")
    mask = 1
    others = []
    while mask < size:
        others.append((scatter.seq, flipped(scatter.rows, mask, size)))
        mask *= 2
    partners = partners + others
    greet(blocks.peers() + others)
    gain_sum[0] = gain_ref[...]

    def exchange(i):
        return remote(
            gain_sum.at[i], gain_from.at[i], partners[i], gain_send.at[i], gain_recv.at[i]
        )

    def add_gains(i):
        exchange(i).wait_recv()
        gain_sum[i + 1] = gain_sum[i] + gain_from[i]

    def body(unit, carry):
        for i in range(len(partners)):
            at_unit(unit, 2 * i + 1, exchange(i).start)
            at_unit(unit, 2 * i + 2, partial(add_gains, i))
        at_unit(unit, 13, blocks.start)
        pair, side = lax.div(unit, 2), 1 - lax.rem(unit, 2)
        begin = pl.multiple_of((PlaneScatter.place(pair) + 8 * side) * half, half)
        total[...] = dot_nt(d_ref[pl.ds(begin, half), :], w_ref[...])

        @pl.when(side == 1)
        def _():
            scatter.give_odd(pair, total[...])

        @pl.when(side == 0)
        def _():
            scatter.give_even(pair, total)

        return carry

    lax.fori_loop(0, 16, body, 0)
    gain_out[...] = gain_sum[len(partners)]
    blocks.finish()
    for i in range(len(partners)):
        exchange(i).wait_send()
    scatter.finish()


def project_back_call(d, w, gains, blocks, count, earlier):
    width = w.shape[0]
    half = count // 2
    here, there = pl.BlockSpec(memory_space=pltpu.VMEM), pl.BlockSpec(memory_space=pl.ANY)
    rounds = 3 + (lax.axis_size("rows") - 1).bit_length()
    own, from_x, from_y, gains, blocks = pl.pallas_call(
        project_back_kernel,
        in_specs=[here] * 3 + [there] * 2,
        out_specs=[there] * 3 + [here, there],
        out_shape=scatter_shapes(count, width) + [
            jax.ShapeDtypeStruct(gains.shape, F32),
            jax.ShapeDtypeStruct(blocks.shape, BF16),
        ],
        scratch_shapes=[
            pltpu.VMEM((rounds + 1,) + gains.shape, F32),
            pltpu.VMEM((rounds,) + gains.shape, F32),
            pltpu.SemaphoreType.DMA((rounds,)),
            pltpu.SemaphoreType.DMA((rounds,)),
        ]
        + PlaneExchange.scratch()
        + [
            pltpu.VMEM((half, width), F32),
        ]
        + PlaneScatter.scratch(half, width),
        compiler_params=pltpu.CompilerParams(
            collective_id=4, has_side_effects=True, vmem_limit_bytes=VMEM
        ),
        cost_estimate=pl.CostEstimate(
            flops=16 * d.shape[0] * width * w.shape[1], bytes_accessed=d.shape[0] * width * 8, transcendentals=0
        ),
        name="project_back",
    )(d, w, gains, blocks, earlier)
    return own + from_x.astype(F32) + from_y.astype(F32), gains, blocks


def ffn_kernel(hidden_ref, grad_ref, gu_ref, down_ref, act_ref, dgu_ref):
    part = down_ref.shape[1]
    gate, up, act = gate_and_up(hidden_ref[...], gu_ref)
    d_gate, d_up = gate_and_up_back(gate, up, dot_nn(grad_ref[...], down_ref[...]))
    act_ref[...] = act
    dgu_ref[:, :part] = d_gate
    dgu_ref[:, part:] = d_up


def ffn_call(hidden, grad, gu, down):
    count, width = hidden.shape
    part = down.shape[1]
    block = 256
    return pl.pallas_call(
        ffn_kernel,
        grid=(count // block,),
        in_specs=[
            pl.BlockSpec((block, width), lambda i: (i, 0)),
            pl.BlockSpec((block, width), lambda i: (i, 0)),
            pl.BlockSpec(gu.shape, lambda i: (0, 0), pipeline_mode=pl.Buffered(1)),
            pl.BlockSpec(down.shape, lambda i: (0, 0), pipeline_mode=pl.Buffered(1)),
        ],
        out_specs=[
            pl.BlockSpec((block, part), lambda i: (i, 0)),
            pl.BlockSpec((block, 2 * part), lambda i: (i, 0)),
        ],
        out_shape=[
            jax.ShapeDtypeStruct((count, part), BF16),
            jax.ShapeDtypeStruct((count, 2 * part), BF16),
        ],
        compiler_params=pltpu.CompilerParams(vmem_limit_bytes=VMEM),
        name="ffn",
    )(hidden, grad, gu, down)


def all_to_all(block):
    return lax.all_to_all(block, "seq", 0, 0, tiled=True)


def gather_z(block):
    full = lax.all_gather(block, "rows", axis=1, tiled=True)
    return full.reshape(-1, full.shape[-1])


def scatter_z(grad):
    parts, lines, cols = grad.shape
    grad = lax.psum_scatter(
        grad.reshape(parts * lines, cols), "rows", scatter_dimension=0, tiled=True
    )
    return grad.reshape(lax.axis_size("seq"), -1, cols)


def shards(
    tokens,
    lengths,
    norm_gains,
    qk_gains,
    qkv_weight,
    out_weight,
    gate_up_weight,
    down_weight,
    cotangent,
):
    rows, slots, width = tokens.shape
    count = rows * slots
    seq = lax.axis_size("seq")
    group = QUERY_HEADS // seq
    query_width = group * HEAD
    sharing = seq // KEY_VALUE_HEADS
    total = seq * slots
    depth = qkv_weight.shape[0]
    kv_at = QUERY_HEADS * HEAD
    part = down_weight.shape[1] // seq
    me = lax.axis_index("seq").astype(jnp.int32)[None]
    gains = norm_gains.astype(F32)

    qkv_scaled = (qkv_weight.astype(F32) * gains[0][:, None]).astype(BF16)
    kv_scaled = qkv_scaled[:, kv_at:].reshape(depth, 2, KEY_VALUE_HEADS, HEAD)
    qkv_blocks = jnp.concatenate(
        [
            qkv_scaled[:, :kv_at].reshape(depth, seq, query_width),
            jnp.repeat(kv_scaled[:, 0], sharing, axis=1),
            jnp.repeat(kv_scaled[:, 1], sharing, axis=1),
        ],
        axis=2,
    ).transpose(1, 0, 2)
    qkv_mine = gather_z(all_to_all(qkv_blocks))
    out_block = lax.all_gather(out_weight, "rows", axis=0, tiled=True)
    gu_scaled = (gate_up_weight.astype(F32) * gains[1][:, None]).astype(BF16)
    gu_blocks = gu_scaled.reshape(depth, 2, seq, part).transpose(2, 0, 1, 3)
    gu_mine = gather_z(all_to_all(gu_blocks.reshape(seq, depth, 2 * part)))
    down_blocks = down_weight.reshape(depth, seq, part).transpose(1, 0, 2)

    lane = jnp.arange(128) % HEAD
    frequency = jnp.exp(
        -math.log(10000.0) * ((lane % (HEAD // 2)).astype(F32) * (2.0 / HEAD))
    )
    angles = jnp.arange(total).astype(F32)[:, None] * frequency[None, :]
    cos = jnp.cos(angles)
    sin = jnp.where(lane < HEAD // 2, -1.0, 1.0)[None, :] * jnp.sin(angles)
    qk = qk_gains.astype(F32)
    head_gains = jnp.concatenate([jnp.tile(qk[0], group), qk[1], jnp.ones((HEAD,), F32)])[None, :]

    inputs = tokens.reshape(count, width).astype(F32)
    r0 = lax.rsqrt(jnp.mean(inputs * inputs, axis=-1, keepdims=True) + EPSILON)
    unit0 = (inputs * r0).astype(BF16)
    if seq == 8:
        unit0, raw, q, kv = gather_qkv_call(unit0, qkv_mine, cos, sin, head_gains, rows, slots)
    else:
        unit0 = gather_plane(unit0)
        raw, q, kv = qkv_call(me, unit0, qkv_mine, cos, sin, head_gains, rows, slots)
    out_full = gather_natural(after(out_block, q))
    down_mine = gather_z(after(all_to_all(down_blocks), q))
    attended_mine, attended_low, logs = attend_call(lengths, q, kv, slots)
    attended = all_to_all(attended_low).transpose(1, 2, 0, 3).reshape(count, kv_at)
    middle = inputs + dot_nt(attended, out_full)
    r1 = lax.rsqrt(jnp.mean(middle * middle, axis=-1, keepdims=True) + EPSILON)

    grad_low = cotangent.reshape(count, width)
    unit1 = (middle * r1).astype(BF16)
    half = seq * count // 2
    if seq == 8:
        unit1, near, far, gate_up, act = gather_ffn_call(
            unit1, gather_pieces(grad_low, q), gu_mine
        )
        down_grad = weight_grad_call([near, far], act, act, depth, "down_grad")
        u, d_gu = ffn_back_call(near, far, gate_up, gu_mine, down_mine, count, down_grad)
    else:
        grad_all = gather_plane(grad_low)
        unit1 = gather_plane(unit1)
        act, d_gu = ffn_call(unit1, grad_all, gu_mine, down_mine)
        u_odd = dot_nt(d_gu[half:], gu_mine).astype(BF16)
        u = scatter_plane(u_odd, dot_nt(d_gu[:half], gu_mine))
        near, far = grad_all[:half], grad_all[half:]
        down_grad = weight_grad_call([near, far], act, act, depth, "down_grad")
    down_sum = scatter_z(down_grad)

    d_middle = (
        grad_low.astype(F32)
        + r1 * u
        - middle * (r1 * r1 * r1) * jnp.mean(u * middle, axis=-1, keepdims=True)
    )
    d_branch = d_middle.astype(BF16)
    d_attended = dot_nn(d_branch, out_full).astype(BF16)
    if seq == 8:
        *sums, d_attended, down_owned = branch_sum_call(
            act, down_mine, d_branch, attended, d_attended, down_sum
        )
        d_attended = d_attended.reshape(seq, rows, slots, query_width)
        gu_grad, from_x, from_y = grad_send_call(unit1, d_gu, sums[1], sums[2], count, depth)
    else:
        branch_near, branch_far = branch_call(act, down_mine, d_attended)
        branch_far = swap(branch_far, 1).astype(F32)
        branch_all = (branch_near.astype(F32) + branch_far).astype(BF16)
        branch_parts = [branch_all[i * count : (i + 1) * count] for i in range(seq // 2)]
        gu_grad = weight_grad_call([unit1], d_gu, branch_near, depth, "gate_up_grad")
        d_attended = d_attended.reshape(rows, slots, seq, query_width).transpose(2, 0, 1, 3)
        d_attended = all_to_all(d_attended)
        down_owned = all_to_all(down_sum)
    gu_sum = scatter_z(gu_grad)
    features = width // seq
    if seq != 8:
        out_near, out_far = out_grad_call(me, d_branch, attended, gu_grad)
        out_all = (out_near.astype(F32) + swap(out_far, 1).astype(F32)).astype(BF16)
        sums = [
            jnp.concatenate([branch_parts[i], out_all[i * features : (i + 1) * features]], axis=0)
            for i in range(seq // 2)
        ]
    dq, dkv = attend_back_call(
        lengths, q, kv, attended_mine, d_attended, logs, [gu_grad, *sums]
    )
    d_qkv, head_gain_grad = prepare_back_call(
        me, raw, dq, dkv, cos, sin, head_gains, slots, dq
    )
    if seq == 8:
        diagonal = swap(sums[3], 6)
        arrived = [from_x, from_y, diagonal[:count]]
        out_arrived = [swap(sums[i][count:], 2 * i) for i in (1, 2)] + [diagonal[count:]]
    else:
        arrived = [swap(sums[i], 2 * i) for i in range(1, seq // 2)]
        out_arrived = [part[count:] for part in arrived]
        arrived = [part[:count] for part in arrived]
    branch = after(sums[0][:count].astype(F32), d_qkv)
    for part_sum in arrived:
        branch = branch + part_sum.astype(F32)
    out_sum = after(sums[0][count:].astype(F32), d_qkv)
    for part_sum in out_arrived:
        out_sum = out_sum + part_sum.astype(F32)
    output = (middle + branch).astype(BF16).reshape(rows, slots, width)
    qkv_grad = weight_grad_call([unit0], d_qkv, output, depth, "qkv_grad")
    if seq == 8:
        gain_rows = jnp.broadcast_to(head_gain_grad, (8, head_gain_grad.shape[1]))
        u0, head_gain_grad, gu_owned = project_back_call(
            d_qkv, qkv_mine, gain_rows, gu_sum, count, qkv_grad
        )
    else:
        u0_odd = dot_nt(d_qkv[half:], qkv_mine).astype(BF16)
        u0 = scatter_plane(u0_odd, dot_nt(d_qkv[:half], qkv_mine))
        head_gain_grad = sum_everywhere(head_gain_grad)
        gu_owned = all_to_all(gu_sum)
    parts = lax.axis_size("rows")
    out_blocks = out_sum.astype(BF16).reshape(parts, depth * seq, kv_at // seq)
    attn_grad = after(jnp.concatenate([qkv_grad, out_blocks], axis=2), gu_sum)
    attn_sum = scatter_z(attn_grad)
    qkv_sum = attn_sum[:, :, : query_width + 2 * HEAD]
    out_sum = attn_sum[:, :, query_width + 2 * HEAD :].reshape(depth, kv_at)
    input_grad = (
        d_middle + r0 * u0 - inputs * (r0 * r0 * r0) * jnp.mean(u0 * inputs, axis=-1, keepdims=True)
    )
    input_grad = input_grad.astype(BF16).reshape(rows, slots, width)
    qk_grad = jnp.stack(
        [head_gain_grad[0, :query_width].reshape(group, HEAD).sum(0), head_gain_grad[0, query_width : query_width + HEAD]]
    )

    gu_out, gu_rows = finish_call(gu_owned, gate_up_weight, gains[1][:, None], 2)
    down_out, _ = finish_call(down_owned, down_weight, jnp.ones((depth, 1), F32), 1)
    qkv_sum = all_to_all(qkv_sum).transpose(1, 0, 2).astype(F32)
    kv_sum = qkv_sum[:, :, query_width:].reshape(depth, KEY_VALUE_HEADS, sharing, 2 * HEAD).sum(2)
    qkv_sum = jnp.concatenate(
        [
            qkv_sum[:, :, :query_width].reshape(depth, -1),
            kv_sum[:, :, :HEAD].reshape(depth, -1),
            kv_sum[:, :, HEAD:].reshape(depth, -1),
        ],
        axis=1,
    )
    norm_gain_grad = jnp.stack(
        [
            jnp.sum(qkv_weight.astype(F32) * qkv_sum, axis=1),
            gu_rows,
        ]
    )
    return (
        output,
        input_grad,
        norm_gain_grad,
        qk_grad,
        qkv_sum * gains[0][:, None],
        out_sum.astype(F32),
        gu_out,
        down_out,
    )


def solution(mesh):
    in_specs = (
        P("rows", "seq", None),
        P("rows"),
        P(None, ("seq", "rows")),
        P(),
        P(("seq", "rows"), None),
        P(("seq", "rows"), None),
        P(("seq", "rows"), None),
        P(("seq", "rows"), None),
        P("rows", "seq", None),
    )
    out_specs = (
        P("rows", "seq", None),
        P("rows", "seq", None),
        P(None, ("seq", "rows")),
        P(),
        P(("seq", "rows"), None),
        P(("seq", "rows"), None),
        P(("seq", "rows"), None),
        P(("seq", "rows"), None),
    )
    return jax.shard_map(shards, mesh=mesh, in_specs=in_specs, out_specs=out_specs, check_vma=False)
```
